32 devices in a mesh: role: 2 (over y), dp: 16 (over z, x, core).
Axes of the slice: x: 2, y: 2, z: 4, core: 2. Of those that a mesh axis runs over, the one named last changes fastest.
Arguments:
- frames: bfloat16 [2, 2, 4096, 1024], P('role', None, 'dp'), may hold values from -6 to 6
- cotangent: bfloat16 [2, 2, 4096, 1024], P('role', None, 'dp'), may hold values from -6 to 6
- inner_weight: bfloat16 [2, 1024, 3072], P(None, 'dp'), may hold values from -0.1875 to 0.1875
- outer_weight: bfloat16 [2, 1024, 1024], P(None, 'dp'), may hold values from -0.5 to 0.5
- expand_weight: bfloat16 [2, 1024, 4096], P(None, 'dp'), may hold values from -0.1875 to 0.1875
- shrink_weight: bfloat16 [2, 4096, 1024], P(None, 'dp'), may hold values from -0.09375 to 0.09375
- causal_gain: bfloat16 [2, 1024], P(None, 'dp'), may hold values from 0.099609375 to 1.8984375
- causal_shift: bfloat16 [2, 1024], P(None, 'dp'), may hold values from -2 to 2
- section_scale: bfloat16 [7, 2, 1024], P(None, None, 'dp'), may hold values from 0.099609375 to 1.8984375
- section_shift: bfloat16 [7, 2, 1024], P(None, None, 'dp'), may hold values from -2 to 2
- prompt_lengths: int32 [2, 16, 4], P(None, 'dp'), may hold values from 1 to 128, 256 in all within a row
- target_lengths: int32 [2, 16, 4], P(None, 'dp'), may hold values from 1 to 128, 256 in all within a row
- sections: int32 [2, 16, 4], P(None, 'dp'), may hold values from 0 to 6
Outputs:
- mixed: bfloat16 [2, 2, 4096, 1024], P('role', None, 'dp')
- frames_grad: bfloat16 [2, 2, 4096, 1024], P('role', None, 'dp')
- inner_grad: float32 [2, 1024, 3072], P(None, 'dp')
- outer_grad: float32 [2, 1024, 1024], P(None, 'dp')
- expand_grad: float32 [2, 1024, 4096], P(None, 'dp')
- shrink_grad: float32 [2, 4096, 1024], P(None, 'dp')
- causal_gain_grad: float32 [2, 1024], P(None, 'dp')
- causal_shift_grad: float32 [2, 1024], P(None, 'dp')
- section_scale_grad: float32 [7, 2, 1024], P(None, None, 'dp')
- section_shift_grad: float32 [7, 2, 1024], P(None, None, 'dp')
The draws below stay inside these ranges and needn't reach their ends.
Inputs may be any that keep to these rules, and one draw needn't show every extreme that they name: `prompt_lengths`: each row of 4 lengths sums to 256. `target_lengths`: each row of 4 lengths sums to 256.
All inputs are finite; a program needn't handle non-finite values.
Results may differ from the reference program's by a relative error of at most 0.018.
Values may be sent and summed in bfloat16 or wider, within the bound.
A program may use at most 320 MiB of HBM per device.

```python
import math
import jax
import jax.numpy as jnp
import numpy as np
from jax import lax

D = 1024
HEADS = 16
HD = 64
FF = 4096
SECTIONS = 7
MB = 2
SEGS = 4
ROWS = 256
FRAMES = 4096
N_DP = 16


def plant(values, own_key, smallest, top_value):
    shape = values.shape
    index_at = [jax.random.randint(jax.random.fold_in(own_key, axis), (), 0, shape[axis]) for axis in range(len(shape))]
    values = values.at[tuple(index_at)].set(smallest)
    longest = shape.index(max(shape))
    index_at[longest] = (index_at[longest] + 1) % shape[longest]
    return values.at[tuple(index_at)].set(top_value)


def level_of(own_key, shape, split, least, largest):
    def one(dim, blocks):
        heights = jax.random.uniform(jax.random.fold_in(jax.random.fold_in(own_key, 6), dim), (blocks,), jnp.float32, least / len(split), largest / len(split))
        return jnp.repeat(jnp.exp(heights), shape[dim] // blocks).reshape((-1,) + (1,) * (len(shape) - dim - 1))

    loudness = one(*split[0])
    for cut in split[1:]:
        loudness = loudness * one(*cut)
    return loudness


def profile(number_of, total, most, lean):
    portions = [(1 << 20) // math.isqrt(grade ** lean) + 1 for grade in range(2, number_of + 1)]
    rest, counts = total - most - (number_of - 1), [1] * (number_of - 1)
    while rest > 0:
        movable = [i for i in range(number_of - 1) if counts[i] < most]
        pool, remaining = sum([portions[i] for i in movable]), rest
        for i in movable:
            addition = min(most - counts[i], max(1, remaining * portions[i] // pool), rest)
            counts[i] = counts[i] + addition
            rest = rest - addition
    return np.array([most] + counts)


def ragged_sizes(key, amount, total, reach, slope):
    if amount == 2:
        one = jax.random.randint(key, (), max(1, total - reach), min(reach, total - 1) + 1)
        return jnp.stack([one, total - one])
    sizes = jnp.asarray(profile(amount, total, reach, slope), jnp.int32)
    couples = (amount - 1) // 2
    source_of, sink = sizes[1:1 + 2 * couples:2], sizes[2:2 + 2 * couples:2]
    margin = jnp.minimum(source_of - 1, reach - sink)
    moved = jax.random.randint(jax.random.fold_in(key, 1), (couples,), 0, 1 << 20) % (margin + 1)
    sizes = sizes.at[1:1 + 2 * couples:2].set(source_of - moved).at[2:2 + 2 * couples:2].set(sink + moved)
    return sizes[jax.random.permutation(jax.random.fold_in(key, 2), amount)]


def bell_draw(stream_key, extent, width, reach, pieces=(), kind=jnp.bfloat16):
    level = level_of(stream_key, extent, pieces, -0.22, 0.18) if pieces else 1.0
    drawn = jax.random.normal(stream_key, extent, jnp.float32) * width * level
    return jnp.minimum(jnp.maximum(drawn, -reach), reach).astype(kind)


def setup_inputs(seed: int = 0) -> dict:
    key_list = jax.random.split(jax.random.key(seed), 14)
    return {
        "frames": bell_draw(key_list[0], (2, MB, FRAMES, D), 1.0, 6.0, ((0, 2), (2, 16))),
        "cotangent": bell_draw(key_list[1], (2, MB, FRAMES, D), 1.0, 6.0, ((0, 2), (2, 16))),
        "inner_weight": bell_draw(key_list[2], (2, D, 3 * D), D ** -0.5, 0.1875, ((1, 16),)),
        "outer_weight": bell_draw(key_list[3], (2, D, D), (D // 8) ** -0.5, 0.5, ((1, 16),)),
        "expand_weight": bell_draw(key_list[4], (2, D, FF), D ** -0.5, 0.1875, ((1, 16),)),
        "shrink_weight": bell_draw(key_list[5], (2, FF, D), FF ** -0.5, 0.09375, ((1, 16),)),
        "causal_gain": jnp.clip(1.0 + 0.18 * jax.random.normal(key_list[6], (2, D), jnp.float32), 0.099609375, 1.8984375).astype(jnp.bfloat16),
        "causal_shift": bell_draw(key_list[7], (2, D), 0.3, 2.0, ((1, 16),)),
        "section_scale": jnp.clip(1.0 + 0.18 * jax.random.normal(key_list[8], (SECTIONS, 2, D), jnp.float32), 0.099609375, 1.8984375).astype(jnp.bfloat16),
        "section_shift": bell_draw(key_list[9], (SECTIONS, 2, D), 0.3, 2.0, ((2, 16),)),
        "prompt_lengths": jax.vmap(lambda own: ragged_sizes(own, SEGS, ROWS, ROWS // 2, 2))(jax.random.split(key_list[10], MB * N_DP)).reshape((MB, N_DP, SEGS)).astype(jnp.int32),
        "target_lengths": jax.vmap(lambda own: ragged_sizes(own, SEGS, ROWS, ROWS // 2, 2))(jax.random.split(key_list[11], MB * N_DP)).reshape((MB, N_DP, SEGS)).astype(jnp.int32),
        "sections": plant(jax.random.randint(key_list[12], (MB, N_DP, SEGS), 0, SECTIONS), jax.random.fold_in(key_list[12], 1), 0, SECTIONS - 1).astype(jnp.int32),
    }


highest = lax.Precision.HIGHEST

@jax.custom_vjp
def low(v):
    return lax.optimization_barrier(v.astype(jnp.bfloat16)).astype(jnp.float32)

@jax.custom_vjp
def low_back(v):
    return v

def low_keep(v):
    return (low(v), None)

def low_pass(kept, grad):
    return (grad,)

def back_keep(v):
    return (v, None)

def back_low(kept, grad):
    return (low(grad),)
low.defvjp(low_keep, low_pass)
low_back.defvjp(back_keep, back_low)

def normalize(hidden):
    average = lax.optimization_barrier(jnp.mean(hidden, axis=-1, keepdims=True))
    centred = hidden - average
    spread = lax.optimization_barrier(jnp.mean(centred * centred, axis=-1, keepdims=True))
    return centred * lax.rsqrt(spread + 1e-05)

def frame_tags(lengths, offsets, total_rows):
    places = jnp.arange(total_rows, dtype=jnp.int32)
    finish = jnp.cumsum(lengths).astype(jnp.int32)
    segment = lax.optimization_barrier(jnp.sum((places[:, None] >= finish[None, :]).astype(jnp.int32), axis=1))
    member = segment[:, None] == jnp.arange(lengths.shape[0], dtype=jnp.int32)[None, :]
    shifted = offsets - (finish - lengths)
    position = places + lax.optimization_barrier(jnp.sum(jnp.where(member, shifted[None, :], 0), axis=1)).astype(jnp.int32)
    return (segment, position)

def attend(normed, project, restore, allowed):
    total_rows = normed.shape[0]
    packed = low_back(low(jnp.dot(low(normed), project, precision=highest)))
    packed = packed.reshape(total_rows, 3, HEADS, HD)
    queries = packed[:, 0]
    key_rows = packed[:, 1]
    value_rows = packed[:, 2]
    scores = low_back(jnp.einsum('qhd,khd->hqk', queries, key_rows, precision=highest) * HD ** (-0.5))
    scores = jnp.where(allowed[None], scores, -1e+30)
    highest_score = lax.optimization_barrier(jnp.max(scores, axis=-1, keepdims=True))
    exponent = jnp.exp(scores - highest_score)
    softened = exponent / lax.optimization_barrier(jnp.sum(exponent, axis=-1, keepdims=True))
    mixture = jnp.einsum('hqk,khd->qhd', low(softened), value_rows, precision=highest)
    mixture = mixture.reshape(total_rows, HEADS * HD)
    return low_back(jnp.dot(low_back(low(mixture)), restore, precision=highest))

def feed(normed, expand, shrink):
    upper = low_back(jnp.dot(low(normed), expand, precision=highest))
    lifted = low(jax.nn.gelu(upper, approximate=False))
    return low_back(jnp.dot(lifted, shrink, precision=highest))

def reference(frames, cotangent, inner_weight, outer_weight, expand_weight, shrink_weight, causal_gain, causal_shift, section_scale, section_shift, prompt_lengths, target_lengths, sections):
    groups = MB * N_DP
    prompt_flat = prompt_lengths.reshape(groups, SEGS)
    target_flat = target_lengths.reshape(groups, SEGS)
    section_flat = sections.reshape(groups, SEGS)

    def tags_of(prompt_row, target_row, section_row):
        prompt_tags = frame_tags(prompt_row, jnp.zeros_like(prompt_row), ROWS)
        target_tags = frame_tags(target_row, prompt_row, ROWS)
        segment = jnp.concatenate([prompt_tags[0], target_tags[0]])
        position = jnp.concatenate([prompt_tags[1], target_tags[1]])
        sides = jnp.concatenate([jnp.zeros((ROWS,), jnp.int32), jnp.ones((ROWS,), jnp.int32)])
        return (segment, position, sides, section_row[segment])
    segments, positions, sides, section_frames = jax.vmap(tags_of)(prompt_flat, target_flat, section_flat)

    def forward(inputs, params):
        project, restore, expand, shrink, gains, shifts, scales, moves = params
        grouped = inputs.reshape(2, MB, N_DP, ROWS, D).transpose(1, 2, 0, 3, 4).reshape(groups, 2 * ROWS, D)

        def one_group(carried):
            hidden, segment, position, side_tag, section_frame = carried
            same = segment[:, None] == segment[None, :]
            causal = same & (position[None, :] <= position[:, None])
            prefix = same & ((side_tag[None, :] == 0) | (side_tag[:, None] == 1))
            normed = gains[0] * normalize(hidden) + shifts[0]
            hidden = hidden + attend(normed, project[0], restore[0], causal)
            normed = gains[1] * normalize(hidden) + shifts[1]
            hidden = hidden + feed(normed, expand[0], shrink[0])
            scale_rows = scales[section_frame]
            move_rows = moves[section_frame]
            normed = scale_rows[:, 0] * normalize(hidden) + move_rows[:, 0]
            hidden = hidden + attend(normed, project[1], restore[1], prefix)
            normed = scale_rows[:, 1] * normalize(hidden) + move_rows[:, 1]
            hidden = hidden + feed(normed, expand[1], shrink[1])
            return hidden
        result = lax.map(jax.checkpoint(one_group), (grouped, segments, positions, sides, section_frames))
        return result.reshape(MB, N_DP, 2, ROWS, D).transpose(2, 0, 1, 3, 4).reshape(2, MB, N_DP * ROWS, D)
    params = (inner_weight.astype(jnp.float32), outer_weight.astype(jnp.float32), expand_weight.astype(jnp.float32), shrink_weight.astype(jnp.float32), causal_gain.astype(jnp.float32), causal_shift.astype(jnp.float32), section_scale.astype(jnp.float32), section_shift.astype(jnp.float32))
    output, pullback = jax.vjp(forward, frames.astype(jnp.float32), params)
    input_grad, param_grads = pullback(cotangent.astype(jnp.float32))
    return (output.astype(jnp.bfloat16), input_grad.astype(jnp.bfloat16), param_grads[0], param_grads[1], param_grads[2], param_grads[3], param_grads[4], param_grads[5], param_grads[6], param_grads[7])
```

```python
import functools

import jax
import jax.numpy as jnp
from jax import lax
from jax.experimental import pallas as pl
from jax.experimental.pallas import tpu as pltpu
from jax.sharding import PartitionSpec as P

HEADS = 16
HD = 64
MESH = pl.DeviceIdType.MESH
SLOTS = 4
F32 = jnp.float32
BF16 = jnp.bfloat16


class Place:
    def __init__(self, outer_count):
        self.outers = outer_count
        self.role = lax.axis_index("role")
        dp = lax.axis_index("dp")
        self.core = dp % 2
        self.pair = (dp // 2) % 2
        self.outer = dp // 4
        self.dp = dp

    def at(self, role, outer, pair, core):
        return (role, (outer * 2 + pair) * 2 + core)

    def sibling(self):
        return self.at(self.role, self.outer, self.pair, 1 - self.core)

    def across(self):
        return self.at(self.role, self.outer, 1 - self.pair, self.core)

    def other_role(self):
        return self.at(1 - self.role, self.outer, self.pair, self.core)

    def along(self, by):
        return self.at(self.role, (self.outer + by) % self.outers, self.pair, self.core)

    def greet(self):
        barrier = pltpu.get_barrier_semaphore()
        peers = [self.sibling(), self.across(), self.other_role()]
        peers += [self.along(by) for by in range(1, self.outers)]
        for peer in peers:
            pl.semaphore_signal(barrier, inc=1, device_id=peer, device_id_type=MESH)
        pl.semaphore_wait(barrier, len(peers))


def remote(src, dst, send, recv, peer):
    return pltpu.make_async_remote_copy(
        src_ref=src, dst_ref=dst, send_sem=send, recv_sem=recv, device_id=peer, device_id_type=MESH
    )


def gather_kernel(count, outers, split, part_ref, full_ref, own_sem, zs, zr, xs, xr, us, ur, vs, vr, cs, cr):
    me = Place(outers)
    width = part_ref.shape[-1]
    main = width - split
    main_cols = pl.ds(pl.multiple_of(me.role * split, 128), main)
    give_cols = pl.ds(pl.multiple_of(me.role * main, 128), split)
    take_cols = pl.ds(pl.multiple_of((1 - me.role) * main, 128), split)
    me.greet()

    def own(k):
        return pltpu.make_async_copy(part_ref.at[k], full_ref.at[k, me.outer, me.pair, me.core], own_sem.at[k % SLOTS])

    def z_copy(k, by):
        s = k % SLOTS
        return remote(
            part_ref.at[k, :, main_cols],
            full_ref.at[k, me.outer, me.pair, me.core, :, main_cols],
            zs.at[s, by - 1], zr.at[s, by - 1], me.along(by),
        )

    def z_wait(k, by):
        s = k % SLOTS
        dst = full_ref.at[k, (me.outer - by + outers) % outers, me.pair, me.core, :, main_cols]
        remote(dst, dst, zs.at[s, by - 1], zr.at[s, by - 1], me.along(by)).wait_recv()

    def x_copy(k, pair):
        s = k % SLOTS
        ref = full_ref.at[k, :, pair, me.core, :, main_cols]
        return remote(ref, ref, xs.at[s], xr.at[s], me.across())

    def u_copy(k, by, cols):
        s = k % (2 * SLOTS)
        ref = full_ref.at[k, (me.outer - by + outers) % outers, me.pair, me.core, :, cols]
        return remote(ref, ref, us.at[s, by - 1], ur.at[s, by - 1], me.other_role())

    def v_copy(k, cols):
        s = k % SLOTS
        ref = full_ref.at[k, :, 1 - me.pair, me.core, :, cols]
        return remote(ref, ref, vs.at[s], vr.at[s], me.other_role())

    def c_copy(k, core):
        s = k % SLOTS
        ref = full_ref.at[k, :, :, core]
        return remote(ref, ref, cs.at[s], cr.at[s], me.sibling())

    def step(t, _):
        @pl.when(t < count)
        def _():
            own(t).start()
            for by in range(1, outers):
                z_copy(t, by).start()

        @pl.when((t >= 1) & (t < count + 1))
        def _():
            k = t - 1
            own(k).wait()
            for by in range(1, outers):
                z_wait(k, by)
            x_copy(k, me.pair).start()
            for by in range(1, outers):
                u_copy(k, by, give_cols).start()

        @pl.when((t >= 2) & (t < count + 2))
        def _():
            k = t - 2
            x_copy(k, 1 - me.pair).wait_recv()
            v_copy(k, give_cols).start()

        @pl.when((t >= 3) & (t < count + 3))
        def _():
            k = t - 3
            for by in range(1, outers):
                u_copy(k, by, take_cols).wait_recv()
            v_copy(k, take_cols).wait_recv()
            c_copy(k, me.core).start()
            for by in range(1, outers):
                z_copy(k, by).wait_send()
                u_copy(k, by, give_cols).wait_send()
            x_copy(k, me.pair).wait_send()
            v_copy(k, give_cols).wait_send()

        @pl.when(t >= 4)
        def _():
            k = t - 4
            c_copy(k, 1 - me.core).wait_recv()
            c_copy(k, me.core).wait_send()

        return 0

    lax.fori_loop(0, count + 4, step, 0)


def gather_all(parts, outers, split, collective_id):
    count, rows, width = parts.shape
    dma = pltpu.SemaphoreType.DMA
    many = outers - 1
    return pl.pallas_call(
        functools.partial(gather_kernel, count, outers, split),
        out_shape=jax.ShapeDtypeStruct((count, outers, 2, 2, rows, width), parts.dtype),
        in_specs=[pl.BlockSpec(memory_space=pl.ANY)],
        out_specs=pl.BlockSpec(memory_space=pl.ANY),
        scratch_shapes=[
            dma((SLOTS,)),
            dma((SLOTS, many)), dma((SLOTS, many)),
            dma((SLOTS,)), dma((SLOTS,)),
            dma((2 * SLOTS, many)), dma((2 * SLOTS, many)),
            dma((SLOTS,)), dma((SLOTS,)),
            dma((SLOTS,)), dma((SLOTS,)),
        ],
        compiler_params=pltpu.CompilerParams(collective_id=collective_id, has_side_effects=True),
        name="gather_weights",
    )(parts)


def reduce_kernel(
    count, outers, split, grad_ref, out_ref,
    own_buf, core_buf, role_buf, pair_buf, outer_buf, last_buf, sum_buf, low_buf, end_buf, fin_buf,
    own_sem, cs, cr, ys, yr, xs, xr, zs, zr, es, er, fs,
):
    me = Place(outers)
    width = grad_ref.shape[-1]
    main = width - split
    rows = grad_ref.shape[-2]
    main_cols = pl.ds(pl.multiple_of(me.role * split, 128), main)
    keep_cols = pl.ds(pl.multiple_of(me.role * main, 128), split)
    give_cols = pl.ds(pl.multiple_of((1 - me.role) * main, 128), split)
    me.greet()

    def own(k):
        return pltpu.make_async_copy(grad_ref.at[k, :, :, me.core], own_buf.at[k % SLOTS], own_sem.at[k % SLOTS])

    def c_copy(k):
        s = k % SLOTS
        return remote(grad_ref.at[k, :, :, 1 - me.core], core_buf.at[s], cs.at[s], cr.at[s], me.sibling())

    def y_copy(k):
        s = k % SLOTS
        return remote(sum_buf.at[s, :, :, :, give_cols], role_buf.at[s], ys.at[s], yr.at[s], me.other_role())

    def x_copy(k):
        s = k % SLOTS
        return remote(sum_buf.at[s, :, 1 - me.pair, :, main_cols], pair_buf.at[s], xs.at[s], xr.at[s], me.across())

    def z_copy(k, by):
        s = k % SLOTS
        return remote(
            low_buf.at[s, (me.outer + by) % outers], outer_buf.at[s, by - 1], zs.at[s, by - 1], zr.at[s, by - 1], me.along(by)
        )

    def e_copy(k):
        s = k % SLOTS
        return remote(end_buf.at[s], last_buf.at[s], es.at[s], er.at[s], me.other_role())

    def f_copy(k):
        s = k % SLOTS
        return pltpu.make_async_copy(fin_buf.at[s], out_ref.at[k], fs.at[s])

    def step(t, _):
        @pl.when(t < count)
        def _():
            own(t).start()
            c_copy(t).start()

        @pl.when((t >= 1) & (t < count + 1))
        def _():
            k = t - 1
            s = k % SLOTS
            own(k).wait()
            c_copy(k).wait()
            for o in range(outers):
                for p in range(2):
                    sum_buf[s, o, p] = (own_buf[s, o, p].astype(F32) + core_buf[s, o, p].astype(F32)).astype(BF16)
            y_copy(k).start()

        @pl.when((t >= 2) & (t < count + 2))
        def _():
            k = t - 2
            s = k % SLOTS
            y_copy(k).wait()
            for o in range(outers):
                for p in range(2):
                    had = sum_buf[s, o, p, :, keep_cols].astype(F32)
                    sum_buf[s, o, p, :, keep_cols] = (had + role_buf[s, o, p].astype(F32)).astype(BF16)
            x_copy(k).start()

        @pl.when((t >= 3) & (t < count + 3))
        def _():
            k = t - 3
            s = k % SLOTS
            x_copy(k).wait()
            for o in range(outers):
                had = sum_buf[s, o, me.pair, :, main_cols].astype(F32)
                low_buf[s, o] = (had + pair_buf[s, o].astype(F32)).astype(BF16)
            for by in range(1, outers):
                z_copy(k, by).start()

        @pl.when((t >= 4) & (t < count + 4))
        def _():
            k = t - 4
            s = k % SLOTS
            for by in range(1, outers):
                z_copy(k, by).wait()
            total = low_buf[s, me.outer].astype(F32)
            for by in range(1, outers):
                total = total + outer_buf[s, by - 1].astype(F32)
            end_buf[s] = total.astype(BF16)
            e_copy(k).start()

        @pl.when((t >= 5) & (t < count + 5))
        def _():
            k = t - 5
            s = k % SLOTS
            e_copy(k).wait()

            @pl.when(k >= SLOTS)
            def _():
                f_copy(k - SLOTS).wait()

            mid = main - split
            mine = end_buf[s].astype(F32)
            theirs = last_buf[s].astype(F32)

            @pl.when(me.role == 0)
            def _():
                fin_buf[s, :, :split] = mine[:, :split]
                fin_buf[s, :, split:main] = mine[:, split:] + theirs[:, :mid]
                fin_buf[s, :, main:] = theirs[:, mid:]

            @pl.when(me.role == 1)
            def _():
                fin_buf[s, :, :split] = theirs[:, :split]
                fin_buf[s, :, split:main] = theirs[:, split:] + mine[:, :mid]
                fin_buf[s, :, main:] = mine[:, mid:]

            f_copy(k).start()

        return 0

    lax.fori_loop(0, count + 5, step, 0)
    for k in range(count - SLOTS, count):
        f_copy(k).wait()


def reduce_all(grads, split, collective_id):
    count, outers, _, _, rows, width = grads.shape
    dma = pltpu.SemaphoreType.DMA
    many = outers - 1
    main = width - split
    return pl.pallas_call(
        functools.partial(reduce_kernel, count, outers, split),
        out_shape=jax.ShapeDtypeStruct((count, rows, width), F32),
        in_specs=[pl.BlockSpec(memory_space=pl.ANY)],
        out_specs=pl.BlockSpec(memory_space=pl.ANY),
        scratch_shapes=[
            pltpu.VMEM((SLOTS, outers, 2, rows, width), BF16),
            pltpu.VMEM((SLOTS, outers, 2, rows, width), BF16),
            pltpu.VMEM((SLOTS, outers, 2, rows, split), BF16),
            pltpu.VMEM((SLOTS, outers, rows, main), BF16),
            pltpu.VMEM((SLOTS, many, rows, main), BF16),
            pltpu.VMEM((SLOTS, rows, main), BF16),
            pltpu.VMEM((SLOTS, outers, 2, rows, width), BF16),
            pltpu.VMEM((SLOTS, outers, rows, main), BF16),
            pltpu.VMEM((SLOTS, rows, main), BF16),
            pltpu.VMEM((SLOTS, rows, width), F32),
            dma((SLOTS,)),
            dma((SLOTS,)), dma((SLOTS,)),
            dma((SLOTS,)), dma((SLOTS,)),
            dma((SLOTS,)), dma((SLOTS,)),
            dma((SLOTS, many)), dma((SLOTS, many)),
            dma((SLOTS,)), dma((SLOTS,)),
            dma((SLOTS,)),
        ],
        compiler_params=pltpu.CompilerParams(
            collective_id=collective_id, has_side_effects=True, vmem_limit_bytes=40 * 2**20
        ),
        name="reduce_gradients",
    )(grads)


def frame_tags(lengths, offsets, total_rows):
    places = jnp.arange(total_rows, dtype=jnp.int32)
    segs = lengths.shape[0]
    upto = jnp.arange(segs)[:, None] >= jnp.arange(segs)[None, :]
    finish = jnp.sum(jnp.where(upto, lengths[None, :], 0), axis=1)
    segment = jnp.sum((places[:, None] >= finish[None, :]).astype(jnp.int32), axis=1)
    member = segment[:, None] == jnp.arange(segs, dtype=jnp.int32)[None, :]
    shifted = offsets - (finish - lengths)
    position = places + jnp.sum(jnp.where(member, shifted[None, :], 0), axis=1)
    return (segment, position, member)


def dot(a, b):
    return jnp.dot(a, b, preferred_element_type=F32)


def dot_t(a, b):
    return lax.dot_general(a, b, (((1,), (1,)), ((), ())), preferred_element_type=F32)


def t_dot(a, b):
    return lax.dot_general(a, b, (((0,), (0,)), ((), ())), preferred_element_type=F32)


def normalize(hidden):
    average = jnp.mean(hidden, axis=-1, keepdims=True)
    centred = hidden - average
    spread = jnp.mean(centred * centred, axis=-1, keepdims=True)
    inverse = lax.rsqrt(spread + 1e-05)
    return centred * inverse, inverse


def norm_backward(grad, scale, unit, inverse):
    inner = grad * scale
    return inverse * (
        inner - jnp.mean(inner, axis=-1, keepdims=True) - unit * jnp.mean(inner * unit, axis=-1, keepdims=True)
    )


def attend(queries, keys, values, allowed):
    scores = jnp.einsum("gqhd,gkhd->ghqk", queries, keys, preferred_element_type=F32) * HD**-0.5
    scores = jnp.where(allowed[:, None], scores, -1e30)
    top = jnp.max(scores, axis=-1, keepdims=True)
    exponent = jnp.exp(scores - top)
    totals = jnp.sum(exponent, axis=-1, keepdims=True)
    soft = exponent / totals
    mixture = jnp.einsum("ghqk,gkhd->gqhd", soft.astype(BF16), values, preferred_element_type=F32)
    return mixture.astype(BF16), top + jnp.log(totals)


def attend_back(grad, queries, keys, values, allowed, lse):
    scores = jnp.einsum("gqhd,gkhd->ghqk", queries, keys, preferred_element_type=F32) * HD**-0.5
    soft = jnp.exp(jnp.where(allowed[:, None], scores, -1e30) - lse)
    grad_values = jnp.einsum("ghqk,gqhd->gkhd", soft.astype(BF16), grad, preferred_element_type=F32)
    grad_soft = jnp.einsum("gqhd,gkhd->ghqk", grad, values, preferred_element_type=F32)
    inner = jnp.sum(soft * grad_soft, axis=-1, keepdims=True)
    grad_scores = (soft * (grad_soft - inner)).astype(BF16)
    grad_queries = jnp.einsum("ghqk,gkhd->gqhd", grad_scores, keys, preferred_element_type=F32) * HD**-0.5
    grad_keys = jnp.einsum("ghqk,gqhd->gkhd", grad_scores, queries, preferred_element_type=F32) * HD**-0.5
    return grad_queries, grad_keys, grad_values


def gelu_parts(upper):
    cumulative = 0.5 * (1.0 + lax.erf(upper * 0.7071067811865476))
    density = jnp.exp(-0.5 * upper * upper) * 0.3989422804014327
    return upper * cumulative, cumulative + upper * density


def layer_forward(hidden, weights, tables, allowed, micro):
    count = hidden.shape[0]
    rows = count // micro
    pieces = (weights.shape[0] - 4) // 2
    scale_a, shift_a, scale_f, shift_f = tables
    unit_a, inverse_a = normalize(hidden)
    attn_in = (scale_a * unit_a + shift_a).astype(BF16)
    queries, keys, values = (
        dot(attn_in, weights[i]).astype(BF16).reshape(micro, rows, HEADS, HD) for i in range(3)
    )
    far_keys, far_values = lax.ppermute((keys, values), "role", [(0, 1)])
    keys = jnp.concatenate([far_keys, keys], axis=1)
    values = jnp.concatenate([far_values, values], axis=1)
    mixture, lse = attend(queries, keys, values, allowed)
    mixture = mixture.reshape(count, -1)
    middle = hidden + dot(mixture, weights[3])
    unit_f, inverse_f = normalize(middle)
    ffn_in = (scale_f * unit_f + shift_f).astype(BF16)
    result = middle
    lifted, slopes = [], []
    for j in range(pieces):
        up, slope = gelu_parts(dot(ffn_in, weights[4 + j]))
        lifted.append(up.astype(BF16))
        slopes.append(slope.astype(BF16))
        result = result + dot(lifted[j], weights[4 + pieces + j])
    kept = (unit_a, inverse_a, attn_in, queries, keys, values, lse, mixture, unit_f, inverse_f, ffn_in, lifted, slopes)
    return result, kept


def layer_backward(grad, weights, tables, allowed, kept, table_sums):
    unit_a, inverse_a, attn_in, queries, keys, values, lse, mixture, unit_f, inverse_f, ffn_in, lifted, slopes = kept
    scale_a, _, scale_f, _ = tables
    pieces = (weights.shape[0] - 4) // 2
    micro, rows = queries.shape[:2]
    count = micro * rows
    low = grad.astype(BF16)
    shrink_grads, expand_grads = [], []
    grad_ffn = 0.0
    for j in range(pieces):
        shrink_grads.append(t_dot(lifted[j], low).astype(BF16))
        grad_upper = (dot_t(low, weights[4 + pieces + j]) * slopes[j].astype(F32)).astype(BF16)
        expand_grads.append(t_dot(ffn_in, grad_upper).astype(BF16))
        grad_ffn = grad_ffn + dot_t(grad_upper, weights[4 + j])
    table_f = (table_sums(grad_ffn * unit_f), table_sums(grad_ffn))
    grad_middle = grad + norm_backward(grad_ffn, scale_f, unit_f, inverse_f)
    middle_low = grad_middle.astype(BF16)
    outer_grad = t_dot(mixture, middle_low).astype(BF16)
    grad_mixture = dot_t(middle_low, weights[3]).astype(BF16).reshape(micro, rows, HEADS, HD)
    grad_queries, grad_keys, grad_values = attend_back(grad_mixture, queries, keys, values, allowed, lse)
    back_keys, back_values = lax.ppermute(
        (grad_keys[:, :rows].astype(BF16), grad_values[:, :rows].astype(BF16)), "role", [(1, 0)]
    )
    grad_keys = grad_keys[:, rows:] + back_keys.astype(F32)
    grad_values = grad_values[:, rows:] + back_values.astype(F32)
    inner_grads = []
    grad_attn = 0.0
    for i, part in enumerate((grad_queries, grad_keys, grad_values)):
        part = part.astype(BF16).reshape(count, -1)
        inner_grads.append(t_dot(attn_in, part).astype(BF16))
        grad_attn = grad_attn + dot_t(part, weights[i])
    table_a = (table_sums(grad_attn * unit_a), table_sums(grad_attn))
    grad_hidden = grad_middle + norm_backward(grad_attn, scale_a, unit_a, inverse_a)
    tables_grad = (table_a[0], table_a[1], table_f[0], table_f[1])
    return grad_hidden, jnp.stack(inner_grads + [outer_grad] + expand_grads + shrink_grads), tables_grad


def body(
    frames, cotangent, inner_weight, outer_weight, expand_weight, shrink_weight, causal_gain, causal_shift,
    section_scale, section_shift, prompt_lengths, target_lengths, sections,
):
    is_target = lax.axis_index("role") == 1
    _, micro, rows, width = frames.shape
    shard = inner_weight.shape[1]
    devices = width // shard
    outers = devices // 4
    pieces = expand_weight.shape[2] // width
    layers = inner_weight.shape[0]
    count = micro * rows
    segs = section_scale.shape[0]

    parts = jnp.concatenate(
        [
            inner_weight.reshape(layers, shard, 3, width).transpose(0, 2, 1, 3),
            outer_weight[:, None],
            expand_weight.reshape(layers, shard, devices, pieces, shard).transpose(0, 3, 1, 2, 4).reshape(layers, pieces, shard, width),
            shrink_weight.reshape(layers, pieces, shard, width),
        ],
        axis=1,
    )
    per_layer = parts.shape[1]
    full = gather_all(parts.reshape(layers * per_layer, shard, width), outers, 3 * width // 8, 0)
    full = full.reshape(layers, per_layer, width, width)

    small = jnp.concatenate(
        [causal_gain, causal_shift, section_scale.reshape(2 * segs, -1), section_shift.reshape(2 * segs, -1)], axis=0
    )
    small = lax.all_gather(small, "dp", axis=1, tiled=True).astype(F32)
    scales = small[4 : 4 + 2 * segs].reshape(segs, 2, width)
    shifts = small[4 + 2 * segs :].reshape(segs, 2, width)

    allowed_sets = [[], []]
    section_frames = []
    for m in range(micro):
        prompt_row, target_row, section_row = prompt_lengths[m, 0], target_lengths[m, 0], sections[m, 0]
        prompt_segment, prompt_position, prompt_member = frame_tags(prompt_row, jnp.zeros_like(prompt_row), rows)
        target_segment, target_position, target_member = frame_tags(target_row, prompt_row, rows)
        own_segment = jnp.where(is_target, target_segment, prompt_segment)
        own_position = jnp.where(is_target, target_position, prompt_position)
        own_member = jnp.where(is_target, target_member, prompt_member)
        same_far = (own_segment[:, None] == prompt_segment[None, :]) & is_target
        same_own = own_segment[:, None] == own_segment[None, :]
        causal_own = same_own & (own_position[None, :] <= own_position[:, None])
        allowed_sets[0].append(jnp.concatenate([same_far, causal_own], axis=1))
        allowed_sets[1].append(jnp.concatenate([same_far, same_own], axis=1))
        section_frames.append(jnp.sum(jnp.where(own_member, section_row[None, :], 0), axis=1))
    allowed_sets = [jnp.stack(a) for a in allowed_sets]
    section_frame = jnp.concatenate(section_frames)
    picker = section_frame[:, None] == jnp.arange(segs, dtype=jnp.int32)[None, :]

    def rows_of(table):
        return jnp.sum(jnp.where(picker[:, :, None], table[None], 0.0), axis=1)

    def all_sum(values):
        return jnp.sum(values, axis=0, keepdims=True)

    def section_sum(values):
        return jnp.dot(picker.T.astype(F32), values, precision=lax.Precision.HIGHEST)

    tables = [
        (small[0:1], small[2:3], small[1:2], small[3:4]),
        (rows_of(scales[:, 0]), rows_of(shifts[:, 0]), rows_of(scales[:, 1]), rows_of(shifts[:, 1])),
    ]
    hidden = frames[0].reshape(count, width).astype(F32)
    kept = [None, None]
    for layer in range(2):
        hidden, kept[layer] = layer_forward(hidden, full[layer], tables[layer], allowed_sets[layer], micro)
    mixed = hidden.astype(BF16).reshape(1, micro, rows, width)
    grad = cotangent[0].reshape(count, width).astype(F32)
    weight_grads = [None, None]
    table_grads = [None, None]
    sums = [all_sum, section_sum]
    for layer in (1, 0):
        grad, weight_grads[layer], table_grads[layer] = layer_backward(
            grad, full[layer], tables[layer], allowed_sets[layer], kept[layer], sums[layer]
        )
    frames_grad = grad.astype(BF16).reshape(1, micro, rows, width)

    small_grads = jnp.concatenate(
        [
            table_grads[0][0], table_grads[0][2], table_grads[0][1], table_grads[0][3],
            jnp.stack([table_grads[1][0], table_grads[1][2]], axis=1).reshape(2 * segs, width),
            jnp.stack([table_grads[1][1], table_grads[1][3]], axis=1).reshape(2 * segs, width),
        ],
        axis=0,
    )
    small_grads = lax.psum(lax.psum_scatter(small_grads, "dp", scatter_dimension=1, tiled=True), "role")

    stacked = jnp.concatenate(weight_grads, axis=0).reshape(layers * per_layer, outers, 2, 2, shard, width)
    owned = reduce_all(stacked, width // 4, 1).reshape(layers, per_layer, shard, width)
    inner_grad = owned[:, :3].transpose(0, 2, 1, 3).reshape(layers, shard, 3 * width)
    outer_grad = owned[:, 3]
    expand_grad = (
        owned[:, 4 : 4 + pieces].reshape(layers, pieces, shard, devices, shard).transpose(0, 2, 3, 1, 4).reshape(layers, shard, -1)
    )
    shrink_grad = owned[:, 4 + pieces :].reshape(layers, pieces * shard, width)
    return (
        mixed, frames_grad, inner_grad, outer_grad, expand_grad, shrink_grad,
        small_grads[0:2], small_grads[2:4],
        small_grads[4 : 4 + 2 * segs].reshape(segs, 2, shard),
        small_grads[4 + 2 * segs :].reshape(segs, 2, shard),
    )


def solution(mesh):
    rows = P("role", None, "dp", None)
    second = P(None, "dp", None)
    placed = (rows, rows, second, second, second, second, P(None, "dp"), P(None, "dp"), P(None, None, "dp"), P(None, None, "dp"), second, second, second)
    given = (rows, rows, second, second, second, second, P(None, "dp"), P(None, "dp"), P(None, None, "dp"), P(None, None, "dp"))
    return jax.shard_map(body, mesh=mesh, in_specs=placed, out_specs=given, check_vma=False)
```

```python
import functools

import jax
import jax.numpy as jnp
from jax import lax
from jax.experimental import pallas as pl
from jax.experimental.pallas import tpu as pltpu
from jax.sharding import PartitionSpec as P

HEADS = 16
HD = 64
MESH = pl.DeviceIdType.MESH
SLOTS = 4
F32 = jnp.float32
BF16 = jnp.bfloat16


class Place:
    def __init__(self, outer_count):
        self.outers = outer_count
        self.role = lax.axis_index("role")
        dp = lax.axis_index("dp")
        self.core = dp % 2
        self.pair = (dp // 2) % 2
        self.outer = dp // 4
        self.dp = dp

    def at(self, role, outer, pair, core):
        return (role, (outer * 2 + pair) * 2 + core)

    def sibling(self):
        return self.at(self.role, self.outer, self.pair, 1 - self.core)

    def across(self):
        return self.at(self.role, self.outer, 1 - self.pair, self.core)

    def other_role(self):
        return self.at(1 - self.role, self.outer, self.pair, self.core)

    def along(self, by):
        return self.at(self.role, (self.outer + by) % self.outers, self.pair, self.core)

    def around(self, by):
        return (self.role, (self.dp + by) % (4 * self.outers))

    def greet(self):
        barrier = pltpu.get_barrier_semaphore()
        pl.semaphore_signal(barrier, inc=1, device_id=self.other_role(), device_id_type=MESH)

        def greet_one(i, carry):
            pl.semaphore_signal(barrier, inc=1, device_id=self.around(i + 1), device_id_type=MESH)
            return carry

        lax.fori_loop(0, 4 * self.outers - 1, greet_one, 0)
        pl.semaphore_wait(barrier, 4 * self.outers)


def remote(src, dst, send, recv, peer):
    return pltpu.make_async_remote_copy(
        src_ref=src, dst_ref=dst, send_sem=send, recv_sem=recv, device_id=peer, device_id_type=MESH
    )


def frame_tags(lengths, offsets, total_rows):
    places = jnp.arange(total_rows, dtype=jnp.int32)
    segs = lengths.shape[0]
    upto = jnp.arange(segs)[:, None] >= jnp.arange(segs)[None, :]
    finish = jnp.sum(jnp.where(upto, lengths[None, :], 0), axis=1)
    segment = jnp.sum((places[:, None] >= finish[None, :]).astype(jnp.int32), axis=1)
    member = segment[:, None] == jnp.arange(segs, dtype=jnp.int32)[None, :]
    shifted = offsets - (finish - lengths)
    position = places + jnp.sum(jnp.where(member, shifted[None, :], 0), axis=1)
    return (segment, position, member)


def dot(a, b):
    return jnp.dot(a, b, preferred_element_type=F32)


def dot_t(a, b):
    return lax.dot_general(a, b, (((1,), (1,)), ((), ())), preferred_element_type=F32)


def t_dot(a, b):
    return lax.dot_general(a, b, (((0,), (0,)), ((), ())), preferred_element_type=F32)


def normalize(hidden):
    average = jnp.mean(hidden, axis=-1, keepdims=True)
    centred = hidden - average
    spread = jnp.mean(centred * centred, axis=-1, keepdims=True)
    inverse = lax.rsqrt(spread + 1e-05)
    return centred * inverse, inverse


def norm_backward(grad, scale, unit, inverse):
    inner = grad * scale
    return inverse * (
        inner - jnp.mean(inner, axis=-1, keepdims=True) - unit * jnp.mean(inner * unit, axis=-1, keepdims=True)
    )


def gelu_parts(upper):
    cumulative = 0.5 * (1.0 + lax.erf(upper * 0.7071067811865476))
    density = jnp.exp(-0.5 * upper * upper) * 0.3989422804014327
    return upper * cumulative, cumulative + upper * density


class Gather:
    lag = 4

    def __init__(self, me, part_ref, full_ref, split, sems):
        self.me, self.part, self.full, self.split = me, part_ref, full_ref, split
        self.own_sem, self.zs, self.zr, self.xs, self.xr, self.us, self.ur, self.vs, self.vr, self.cs, self.cr = sems
        self.half = part_ref.shape[-1] // 2
        self.main = self.half - split
        self.steps = 2 * part_ref.shape[0]

    @staticmethod
    def semaphores(many):
        dma = pltpu.SemaphoreType.DMA
        return [
            dma((SLOTS,)),
            dma((SLOTS, many)), dma((SLOTS, many)),
            dma((SLOTS,)), dma((SLOTS,)),
            dma((2 * SLOTS, many)), dma((2 * SLOTS, many)),
            dma((SLOTS,)), dma((SLOTS,)),
            dma((SLOTS,)), dma((SLOTS,)),
        ]

    def cols(self, h, offset, size):
        return pl.ds(pl.multiple_of((h % 2) * self.half + offset, 128), size)

    def main_cols(self, h):
        return self.cols(h, self.me.role * self.split, self.main)

    def give_cols(self, h):
        return self.cols(h, self.me.role * self.main, self.split)

    def take_cols(self, h):
        return self.cols(h, (1 - self.me.role) * self.main, self.split)

    def before(self, by):
        return (self.me.outer - by + self.me.outers) % self.me.outers

    def own(self, h):
        me, cols = self.me, self.cols(h, 0, self.half)
        return pltpu.make_async_copy(
            self.part.at[h // 2, :, cols], self.full.at[h // 2, me.outer, me.pair, me.core, :, cols], self.own_sem.at[h % SLOTS]
        )

    def z_copy(self, h, by):
        me, cols, s = self.me, self.main_cols(h), h % SLOTS
        return remote(
            self.part.at[h // 2, :, cols],
            self.full.at[h // 2, me.outer, me.pair, me.core, :, cols],
            self.zs.at[s, by - 1], self.zr.at[s, by - 1], me.along(by),
        )

    def z_wait(self, h, by):
        me, s = self.me, h % SLOTS
        dst = self.full.at[h // 2, self.before(by), me.pair, me.core, :, self.main_cols(h)]
        remote(dst, dst, self.zs.at[s, by - 1], self.zr.at[s, by - 1], me.along(by)).wait_recv()

    def x_copy(self, h, pair):
        me, s = self.me, h % SLOTS
        ref = self.full.at[h // 2, :, pair, me.core, :, self.main_cols(h)]
        return remote(ref, ref, self.xs.at[s], self.xr.at[s], me.across())

    def u_copy(self, h, by, cols):
        me, s = self.me, h % (2 * SLOTS)
        ref = self.full.at[h // 2, self.before(by), me.pair, me.core, :, cols]
        return remote(ref, ref, self.us.at[s, by - 1], self.ur.at[s, by - 1], me.other_role())

    def v_copy(self, h, cols):
        me, s = self.me, h % SLOTS
        ref = self.full.at[h // 2, :, 1 - me.pair, me.core, :, cols]
        return remote(ref, ref, self.vs.at[s], self.vr.at[s], me.other_role())

    def c_copy(self, h, core):
        s = h % SLOTS
        ref = self.full.at[h // 2, :, :, core, :, self.cols(h, 0, self.half)]
        return remote(ref, ref, self.cs.at[s], self.cr.at[s], self.me.sibling())

    def step(self, t):
        me, count = self.me, self.steps
        others = range(1, me.outers)

        @pl.when(t < count)
        def _():
            self.own(t).start()
            for by in others:
                self.z_copy(t, by).start()

        @pl.when((t >= 1) & (t < count + 1))
        def _():
            h = t - 1
            self.own(h).wait()
            for by in others:
                self.z_wait(h, by)
            self.x_copy(h, me.pair).start()
            for by in others:
                self.u_copy(h, by, self.give_cols(h)).start()

        @pl.when((t >= 2) & (t < count + 2))
        def _():
            h = t - 2
            self.x_copy(h, 1 - me.pair).wait_recv()
            self.v_copy(h, self.give_cols(h)).start()

        @pl.when((t >= 3) & (t < count + 3))
        def _():
            h = t - 3
            for by in others:
                self.u_copy(h, by, self.take_cols(h)).wait_recv()
            self.v_copy(h, self.take_cols(h)).wait_recv()
            self.c_copy(h, me.core).start()
            for by in others:
                self.z_copy(h, by).wait_send()
                self.u_copy(h, by, self.give_cols(h)).wait_send()
            self.x_copy(h, me.pair).wait_send()
            self.v_copy(h, self.give_cols(h)).wait_send()

        @pl.when((t >= 4) & (t < count + 4))
        def _():
            h = t - 4
            self.c_copy(h, 1 - me.core).wait_recv()
            self.c_copy(h, me.core).wait_send()


def loop(count, action):
    def one(i, carry):
        action(i)
        return carry

    lax.fori_loop(0, count, one, 0)


def tile(i, size):
    return pl.ds(pl.multiple_of(i * size, size), size)


WIDE = 256


def forward_kernel(
    layers, outers, split,
    part_ref, frames_ref, piece_ref, pick_ref, bias_ref,
    full_ref, saved_ref, hidden_ref, probs_ref, mixed_ref, table_ref,
    tab_in, h_buf, a_buf, qkv_buf, far_buf, mix_buf, f_buf, lift_buf, slope_buf, w_buf, p_buf,
    ts, tr, w_sem, save_sem, h_sem, p_sem, out_sem, ks, kr, *gather_sems,
):
    me = Place(outers)
    devices = 4 * outers
    rows_all, width = frames_ref.shape
    per_layer = part_ref.shape[0] // layers
    pieces = (per_layer - 4) // 2
    micro = bias_ref.shape[1]
    rows = rows_all // micro
    pairs = width // 128
    gather = Gather(me, part_ref, full_ref, split, gather_sems)
    me.greet()

    def piece_copy(by):
        return remote(piece_ref, tab_in.at[me.dp], ts.at[by - 1], tr.at[by - 1], me.around(by))

    def piece_wait(by):
        here = tab_in.at[(me.dp - by + devices) % devices]
        remote(here, here, ts.at[by - 1], tr.at[by - 1], me.around(by)).wait_recv()

    loop(devices - 1, lambda i: piece_copy(i + 1).start())
    tab_in[me.dp] = piece_ref[...]

    @pl.when(me.role == 0)
    def _():
        far_buf[...] = jnp.zeros_like(far_buf)

    loop(6, gather.step)
    loop(devices - 1, lambda i: piece_wait(i + 1))
    loop(devices - 1, lambda i: piece_copy(i + 1).wait_send())
    per = 128 * devices // width
    for group in range(width // 128):
        total = tab_in[group * per]
        for i in range(1, per):
            total = total + tab_in[group * per + i]
        table_ref[:, group * 128 : group * 128 + 128] = total

    def load_rows(i):
        r = tile(i, 64)
        h_buf[0, r, :] = frames_ref[r, :].astype(F32)

    loop(rows_all // 64, load_rows)

    def load(k):
        return pltpu.make_async_copy(full_ref.at[k], w_buf.at[k % 2], w_sem.at[k % 2])

    def matmul(in_ref, k, finish):
        load(k).wait()

        def columns(n):
            cols = tile(n, WIDE)
            w = w_buf[k % 2, :, :, :, :, cols].reshape(width, WIDE)
            finish(cols, dot(in_ref[...], w))

        loop(width // WIDE, columns)

    def norm(index, src, dst_ref, l):
        def some(i):
            r = tile(i, 64)
            unit, _ = normalize(h_buf[src, r, :])
            scale = dot(pick_ref[l * 4 + 2 * index, r, :], table_ref[...])
            shift = dot(pick_ref[l * 4 + 2 * index + 1, r, :], table_ref[...])
            dst_ref[r, :] = (scale * unit + shift).astype(BF16)

        loop(rows_all // 64, some)

    def layer(l):
        base = l * per_layer

        def save(ref, slot):
            return pltpu.make_async_copy(ref, saved_ref.at[l, slot], save_sem.at[slot])

        def save_hidden(which):
            return pltpu.make_async_copy(h_buf.at[which], hidden_ref.at[l, which], h_sem.at[which])

        load(base).start()
        save_hidden(0).start()
        norm(0, 0, a_buf, l)
        save(a_buf, 0).start()

        def project(i):
            def keep(cols, value):
                qkv_buf[i, :, cols] = value.astype(BF16)

            matmul(a_buf, base + i, keep)
            gather.step(2 * (base + i) + 6)
            gather.step(2 * (base + i) + 7)
            load(base + i + 1).start()
            save(qkv_buf.at[i], 1 + i).start()

        loop(3, project)

        def far_copy():
            return remote(qkv_buf.at[pl.ds(1, 2)], far_buf.at[l], ks.at[l], kr.at[l], me.other_role())

        @pl.when(me.role == 0)
        def _():
            far_copy().start()

        @pl.when(me.role == 1)
        def _():
            far_copy().wait_recv()

        save(far_buf.at[l, 0], 4).start()
        save(far_buf.at[l, 1], 5).start()

        def save_probs(it):
            return pltpu.make_async_copy(p_buf.at[it % 2], probs_ref.at[l, it], p_sem.at[it % 2])

        def attend(it):
            m, p = it // pairs, it % pairs
            r, cols = tile(m, rows), tile(p, 128)
            first = lax.broadcasted_iota(jnp.int32, (rows, 128), 1) < HD
            q = qkv_buf[0, r, cols].astype(F32) * HD**-0.5
            both = jnp.concatenate([jnp.where(first, q, 0.0).astype(BF16), jnp.where(first, 0.0, q).astype(BF16)], axis=0)
            keys = jnp.concatenate([far_buf[l, 0, r, cols], qkv_buf[1, r, cols]], axis=0)
            values = jnp.concatenate([far_buf[l, 1, r, cols], qkv_buf[2, r, cols]], axis=0)
            bias = bias_ref[l, m].astype(F32)
            scores = dot_t(keys, both) + jnp.concatenate([bias, bias], axis=1)
            exponent = jnp.exp(scores - jnp.max(scores, axis=0, keepdims=True))
            soft = (exponent * (1.0 / jnp.sum(exponent, axis=0, keepdims=True))).astype(BF16)

            @pl.when(it >= 2)
            def _():
                save_probs(it - 2).wait()

            p_buf[it % 2] = soft
            save_probs(it).start()
            out = t_dot(values, soft)
            out = jnp.concatenate([out[:HD, :rows], out[HD:, rows:]], axis=0)
            mix_buf[r, cols] = out.T.astype(BF16)

        segment = micro * pairs // 4

        def attend_some(s):
            loop(segment, lambda i: attend(s * segment + i))
            gather.step(2 * base + 12 + s)

        loop(4, attend_some)
        save_probs(micro * pairs - 2).wait()
        save_probs(micro * pairs - 1).wait()
        save(mix_buf, 6).start()
        load(base + 4).start()

        def keep_middle(cols, value):
            h_buf[1, :, cols] = h_buf[0, :, cols] + value

        matmul(mix_buf, base + 3, keep_middle)
        save_hidden(1).start()
        save_hidden(0).wait()
        norm(1, 1, f_buf, l)
        save(f_buf, 7).start()
        h_buf[0] = h_buf[1]

        def feed(j):
            load(base + 5 + 2 * j).start()

            def raise_columns(cols, value):
                up, slope = gelu_parts(value)
                lift_buf[:, cols] = up.astype(BF16)
                slope_buf[:, cols] = slope.astype(BF16)

            matmul(f_buf, base + 4 + 2 * j, raise_columns)
            lift_save = pltpu.make_async_copy(lift_buf, saved_ref.at[l, 8 + j], save_sem.at[8])
            slope_save = pltpu.make_async_copy(slope_buf, saved_ref.at[l, 8 + pieces + j], save_sem.at[9])
            lift_save.start()
            slope_save.start()
            gather.step(2 * base + 16 + 4 * j)
            gather.step(2 * base + 17 + 4 * j)

            @pl.when(j < pieces - 1)
            def _():
                load(base + 6 + 2 * j).start()

            def add(cols, value):
                h_buf[0, :, cols] += value

            matmul(lift_buf, base + 5 + 2 * j, add)

            @pl.when(j < pieces - 1)
            def _():
                gather.step(2 * base + 18 + 4 * j)
                gather.step(2 * base + 19 + 4 * j)

            lift_save.wait()
            slope_save.wait()

        loop(pieces, feed)
        save_hidden(1).wait()
        save(a_buf, 0).wait()
        for i in range(3):
            save(qkv_buf.at[i], 1 + i).wait()
        save(far_buf.at[l, 0], 4).wait()
        save(far_buf.at[l, 1], 5).wait()
        save(mix_buf, 6).wait()
        save(f_buf, 7).wait()

        @pl.when(me.role == 0)
        def _():
            far_copy().wait_send()

    loop(layers, layer)

    def store_rows(i):
        r = tile(i, 64)
        a_buf[r, :] = h_buf[0, r, :].astype(BF16)

    loop(rows_all // 64, store_rows)
    done = pltpu.make_async_copy(a_buf, mixed_ref, out_sem)
    done.start()
    done.wait()


def forward(parts, frames, piece, pick, bias, outers, layers, collective_id):
    count, shard, width = parts.shape
    rows_all = frames.shape[0]
    pieces = (count // layers - 4) // 2
    many = outers - 1
    dma = pltpu.SemaphoreType.DMA
    devices = 4 * outers
    split = width // 8
    micro = bias.shape[1]
    keys, rows = bias.shape[2:]
    pairs = width // 128
    any_space = pl.BlockSpec(memory_space=pl.ANY)
    vmem = pl.BlockSpec(memory_space=pltpu.VMEM)
    grid_rows = (rows_all, width)
    return pl.pallas_call(
        functools.partial(forward_kernel, layers, outers, split),
        out_shape=(
            jax.ShapeDtypeStruct((count, outers, 2, 2, shard, width), BF16),
            jax.ShapeDtypeStruct((layers, 8 + 2 * pieces) + grid_rows, BF16),
            jax.ShapeDtypeStruct((layers, 2) + grid_rows, F32),
            jax.ShapeDtypeStruct((layers, micro * pairs, keys, 2 * rows), BF16),
            jax.ShapeDtypeStruct(grid_rows, BF16),
            jax.ShapeDtypeStruct((piece.shape[0], width), BF16),
        ),
        in_specs=[any_space, vmem, vmem, vmem, vmem],
        out_specs=(any_space, any_space, any_space, any_space, any_space, vmem),
        scratch_shapes=[
            pltpu.VMEM((devices,) + piece.shape, BF16),
            pltpu.VMEM((2,) + grid_rows, F32),
            pltpu.VMEM(grid_rows, BF16),
            pltpu.VMEM((3,) + grid_rows, BF16),
            pltpu.VMEM((layers, 2) + grid_rows, BF16),
            pltpu.VMEM(grid_rows, BF16),
            pltpu.VMEM(grid_rows, BF16),
            pltpu.VMEM(grid_rows, BF16),
            pltpu.VMEM(grid_rows, BF16),
            pltpu.VMEM((2, outers, 2, 2, shard, width), BF16),
            pltpu.VMEM((2, keys, 2 * rows), BF16),
            dma((devices - 1,)), dma((devices - 1,)),
            dma((2,)), dma((10,)), dma((2,)), dma((2,)), dma(()), dma((layers,)), dma((layers,)),
        ]
        + Gather.semaphores(many),
        compiler_params=pltpu.CompilerParams(
            collective_id=collective_id, has_side_effects=True, vmem_limit_bytes=58 * 2**20
        ),
        name="gather_and_forward",
    )(parts, frames, piece, pick, bias)


class Reduce:
    lag = 5

    def __init__(self, me, grad_ref, out_ref, split, refs):
        self.me, self.grad, self.out, self.split = me, grad_ref, out_ref, split
        (
            self.own_buf, self.core_buf, self.role_buf, self.pair_buf, self.outer_buf, self.last_buf, self.sum_buf, self.low_buf,
            self.end_buf, self.fin_buf,
            self.own_sem, self.cs, self.cr, self.ys, self.yr, self.xs, self.xr, self.zs, self.zr, self.es, self.er, self.fs,
        ) = refs
        self.width = grad_ref.shape[-1]
        self.main = self.width - split
        self.steps = grad_ref.shape[0]

    @staticmethod
    def scratch(outers, rows, width, split):
        dma = pltpu.SemaphoreType.DMA
        many = outers - 1
        main = width - split
        return [
            pltpu.VMEM((2, outers, 2, rows, width), BF16),
            pltpu.VMEM((SLOTS, outers, 2, rows, width), BF16),
            pltpu.VMEM((SLOTS, outers, 2, rows, split), BF16),
            pltpu.VMEM((SLOTS, outers, rows, main), BF16),
            pltpu.VMEM((SLOTS, many, rows, main), BF16),
            pltpu.VMEM((SLOTS, rows, main), BF16),
            pltpu.VMEM((SLOTS, outers, 2, rows, width), BF16),
            pltpu.VMEM((SLOTS, outers, rows, main), BF16),
            pltpu.VMEM((SLOTS, rows, main), BF16),
            pltpu.VMEM((SLOTS, rows, width), F32),
            dma((2,)),
            dma((SLOTS,)), dma((SLOTS,)),
            dma((SLOTS,)), dma((SLOTS,)),
            dma((SLOTS,)), dma((SLOTS,)),
            dma((SLOTS, many)), dma((SLOTS, many)),
            dma((SLOTS,)), dma((SLOTS,)),
            dma((SLOTS,)),
        ]

    def cols(self, offset, size):
        return pl.ds(pl.multiple_of(offset, 128), size)

    def main_cols(self):
        return self.cols(self.me.role * self.split, self.main)

    def keep_cols(self):
        return self.cols(self.me.role * self.main, self.split)

    def give_cols(self):
        return self.cols((1 - self.me.role) * self.main, self.split)

    def own(self, k):
        s = lax.rem(k, 2)
        return pltpu.make_async_copy(self.grad.at[k, :, :, self.me.core], self.own_buf.at[s], self.own_sem.at[s])

    def c_copy(self, k):
        s = lax.rem(k, SLOTS)
        return remote(self.grad.at[k, :, :, 1 - self.me.core], self.core_buf.at[s], self.cs.at[s], self.cr.at[s], self.me.sibling())

    def y_copy(self, k):
        s = lax.rem(k, SLOTS)
        return remote(
            self.sum_buf.at[s, :, :, :, self.give_cols()], self.role_buf.at[s], self.ys.at[s], self.yr.at[s], self.me.other_role()
        )

    def x_copy(self, k):
        s = lax.rem(k, SLOTS)
        return remote(
            self.sum_buf.at[s, :, 1 - self.me.pair, :, self.main_cols()],
            self.pair_buf.at[s], self.xs.at[s], self.xr.at[s], self.me.across(),
        )

    def z_copy(self, k, by):
        s = lax.rem(k, SLOTS)
        me = self.me
        return remote(
            self.low_buf.at[s, lax.rem(me.outer + by, me.outers)], self.outer_buf.at[s, by - 1],
            self.zs.at[s, by - 1], self.zr.at[s, by - 1], me.along(by),
        )

    def e_copy(self, k):
        s = lax.rem(k, SLOTS)
        return remote(self.end_buf.at[s], self.last_buf.at[s], self.es.at[s], self.er.at[s], self.me.other_role())

    def f_copy(self, k):
        s = lax.rem(k, SLOTS)
        return pltpu.make_async_copy(self.fin_buf.at[s], self.out.at[k], self.fs.at[s])

    def step(self, t):
        me, count, split, main = self.me, self.steps, self.split, self.main
        others = range(1, me.outers)

        @pl.when((t >= 0) & (t < count))
        def _():
            self.own(t).start()
            self.c_copy(t).start()

        @pl.when((t >= 1) & (t < count + 1))
        def _():
            k = t - 1
            s = lax.rem(k, SLOTS)
            self.own(k).wait()
            self.c_copy(k).wait()

            def add(i):
                o, p = lax.div(i, 2), lax.rem(i, 2)
                self.sum_buf[s, o, p] = self.own_buf[lax.rem(k, 2), o, p] + self.core_buf[s, o, p]

            loop(2 * me.outers, add)
            self.y_copy(k).start()

        @pl.when((t >= 2) & (t < count + 2))
        def _():
            k = t - 2
            s = lax.rem(k, SLOTS)
            self.y_copy(k).wait()
            keep = self.keep_cols()

            def add(i):
                o, p = lax.div(i, 2), lax.rem(i, 2)
                self.sum_buf[s, o, p, :, keep] = self.sum_buf[s, o, p, :, keep] + self.role_buf[s, o, p]

            loop(2 * me.outers, add)
            self.x_copy(k).start()

        @pl.when((t >= 3) & (t < count + 3))
        def _():
            k = t - 3
            s = lax.rem(k, SLOTS)
            self.x_copy(k).wait()
            cols = self.main_cols()

            def add(o):
                self.low_buf[s, o] = self.sum_buf[s, o, me.pair, :, cols] + self.pair_buf[s, o]

            loop(me.outers, add)
            for by in others:
                self.z_copy(k, by).start()

        @pl.when((t >= 4) & (t < count + 4))
        def _():
            k = t - 4
            s = lax.rem(k, SLOTS)
            for by in others:
                self.z_copy(k, by).wait()
            total = self.low_buf[s, me.outer].astype(F32)
            for by in others:
                total = total + self.outer_buf[s, by - 1].astype(F32)
            self.end_buf[s] = total.astype(BF16)
            self.e_copy(k).start()

        @pl.when((t >= 5) & (t < count + 5))
        def _():
            k = t - 5
            s = lax.rem(k, SLOTS)
            self.e_copy(k).wait()

            @pl.when(k >= SLOTS)
            def _():
                self.f_copy(k - SLOTS).wait()

            mid = main - split
            mine = self.end_buf[s].astype(F32)
            theirs = self.last_buf[s].astype(F32)

            @pl.when(me.role == 0)
            def _():
                self.fin_buf[s, :, :split] = mine[:, :split]
                self.fin_buf[s, :, split:main] = mine[:, split:] + theirs[:, :mid]
                self.fin_buf[s, :, main:] = theirs[:, mid:]

            @pl.when(me.role == 1)
            def _():
                self.fin_buf[s, :, :split] = theirs[:, :split]
                self.fin_buf[s, :, split:main] = theirs[:, split:] + mine[:, :mid]
                self.fin_buf[s, :, main:] = mine[:, mid:]

            self.f_copy(k).start()

    def finish(self):
        for k in range(self.steps - SLOTS, self.steps):
            self.f_copy(k).wait()


def backward_kernel(
    layers, outers, split,
    full_ref, saved_ref, hidden_ref, probs_ref, cot_ref, table_ref, pick_ref, used_ref,
    grad_ref, out_ref, frames_grad_ref, table_out_ref,
    g_buf, acc_buf, h_buf, w_buf, low_buf, act_buf, give_buf, back_buf, p_buf, stage_buf, tab_sum, tab_in, tab_role, tab_back,
    act_sem, h_sem, w_sem, p_sem, stage_sem, ks, kr, ts, tr, rs_sem, rr_sem, out_sem, *reduce_refs,
):
    me = Place(outers)
    devices = 4 * outers
    rows_all, width = cot_ref.shape
    per_layer = full_ref.shape[0] // layers
    pieces = (per_layer - 4) // 2
    pairs = width // 128
    micro = probs_ref.shape[1] // pairs
    rows = rows_all // micro
    shard = grad_ref.shape[-2]
    tile_outers = WIDE // (4 * shard)
    block = 128
    reduce = Reduce(me, grad_ref, out_ref, split, reduce_refs)
    me.greet()

    def load_rows(i):
        r = tile(i, block)
        g_buf[r, :] = cot_ref[r, :].astype(F32)

    loop(rows_all // block, load_rows)
    tab_sum[...] = jnp.zeros_like(tab_sum)

    def get(l, item, slot):
        return pltpu.make_async_copy(saved_ref.at[l, item], act_buf.at[slot], act_sem.at[slot])

    def get_hidden(l, which):
        return pltpu.make_async_copy(hidden_ref.at[l, which], h_buf, h_sem)

    def get_w(k, slot):
        return pltpu.make_async_copy(full_ref.at[k], w_buf.at[slot], w_sem.at[slot])

    def send_stage(n):
        s = lax.rem(n, 2)
        return pltpu.make_async_copy(stage_buf.at[s], grad_ref.at[n], stage_sem.at[s])

    def produce(n, left, right):
        s = lax.rem(n, 2)

        def some(i):
            value = t_dot(left[:, tile(i, WIDE)], right[...]).astype(BF16)
            stage_buf[s, pl.ds(i * tile_outers, tile_outers)] = value.reshape(tile_outers, 2, 2, shard, width)

        loop(width // WIDE, some)
        send_stage(n).start()

        @pl.when(n >= 1)
        def _():
            send_stage(n - 1).wait()

    def through(left, slot, finish):
        def some(i):
            cols = tile(i, WIDE)
            finish(cols, dot_t(left[...], w_buf[slot, cols, :]))

        loop(width // WIDE, some)

    def lower(dst, src):
        def some(i):
            r = tile(i, block)
            dst[r, :] = src[r, :].astype(BF16)

        loop(rows_all // block, some)

    def norm_back(index, l):
        def some(i):
            r = tile(i, block)
            unit, inverse = normalize(h_buf[r, :])
            scale = dot(pick_ref[l * 4 + 2 * index, r, :], table_ref[...])
            grad = acc_buf[r, :]
            g_buf[r, :] = g_buf[r, :] + norm_backward(grad, scale, unit, inverse)
            for which, values in ((0, grad * unit), (1, grad)):
                picked = used_ref[l * 4 + 2 * index + which, :, r]
                high = values.astype(BF16)
                rest = (values - high.astype(F32)).astype(BF16)
                tab_sum[...] += dot(picked, high) + dot(picked, rest)

        loop(rows_all // block, some)

    def layer(turn):
        l = layers - 1 - turn
        base = l * per_layer
        n0 = turn * per_layer

        def service(index):
            reduce.step(n0 + index - 1)

        get(l, 7, 0).start()
        get(l, 8, 1).start()
        get(l, 8 + pieces, 3).start()
        get_w(base + 5, 0).start()
        get_hidden(l, 1).start()
        lower(low_buf, g_buf)
        acc_buf[...] = jnp.zeros_like(acc_buf)
        get(l, 7, 0).wait()

        def feed(j):
            s = lax.rem(j, 2)
            get_w(base + 4 + 2 * j, 1).start()
            get(l, 8 + j, 1 + s).wait()
            get(l, 8 + pieces + j, 3 + s).wait()

            @pl.when(j < pieces - 1)
            def _():
                get(l, 9 + j, 2 - s).start()
                get(l, 9 + pieces + j, 4 - s).start()

            produce(n0 + 2 * j, act_buf.at[1 + s], low_buf)
            get_w(base + 5 + 2 * j, 0).wait()

            def lift(cols, value):
                act_buf[5, :, cols] = (value * act_buf[3 + s, :, cols].astype(F32)).astype(BF16)

            through(low_buf, 0, lift)

            @pl.when(j < pieces - 1)
            def _():
                get_w(base + 7 + 2 * j, 0).start()

            service(j)
            produce(n0 + 2 * j + 1, act_buf.at[0], act_buf.at[5])
            get_w(base + 4 + 2 * j, 1).wait()

            def add(cols, value):
                acc_buf[:, cols] += value

            through(act_buf.at[5], 1, add)

        loop(pieces, feed)
        get_w(base + 3, 0).start()
        get(l, 6, 0).start()
        for i in range(5):
            get(l, 1 + i, 1 + i).start()

        def get_probs(it):
            s = lax.rem(it, 2)
            return pltpu.make_async_copy(probs_ref.at[l, it], p_buf.at[s], p_sem.at[s])

        get_probs(0).start()
        get_hidden(l, 1).wait()
        norm_back(1, l)
        lower(low_buf, g_buf)
        service(pieces)
        get(l, 6, 0).wait()
        produce(n0 + 2 * pieces, act_buf.at[0], low_buf)
        get_w(base + 3, 0).wait()

        def keep_mixture(cols, value):
            act_buf[6, :, cols] = value.astype(BF16)

        through(low_buf, 0, keep_mixture)
        get_w(base, 0).start()
        get(l, 0, 8).start()
        for i in range(5):
            get(l, 1 + i, 1 + i).wait()

        def attend(it):
            m, p = lax.div(it, pairs), lax.rem(it, pairs)
            r, cols = tile(m, rows), tile(p, 128)
            first = lax.broadcasted_iota(jnp.int32, (rows, 128), 1) < HD

            def both_of(x):
                return jnp.concatenate([jnp.where(first, x, 0.0).astype(BF16), jnp.where(first, 0.0, x).astype(BF16)], axis=0)

            queries = both_of(act_buf[1, r, cols].astype(F32) * HD**-0.5)
            out_grad = both_of(act_buf[6, r, cols].astype(F32))
            keys = jnp.concatenate([act_buf[4, r, cols], act_buf[2, r, cols]], axis=0)
            values = jnp.concatenate([act_buf[5, r, cols], act_buf[3, r, cols]], axis=0)
            get_probs(it).wait()

            @pl.when(it + 1 < micro * pairs)
            def _():
                get_probs(it + 1).start()

            soft_low = p_buf[lax.rem(it, 2)]
            soft = soft_low.astype(F32)
            grad_soft = dot_t(values, out_grad)
            inner = jnp.sum(soft * grad_soft, axis=0, keepdims=True)
            grad_scores = (soft * (grad_soft - inner)).astype(BF16)
            grad_values = dot(soft_low, out_grad)
            grad_keys = dot(grad_scores, queries)
            give_buf[0, r, cols] = grad_keys[:rows].astype(BF16)
            give_buf[1, r, cols] = grad_values[:rows].astype(BF16)
            h_buf[r, cols] = grad_keys[rows:]
            acc_buf[r, cols] = grad_values[rows:]
            out = t_dot(keys, grad_scores) * HD**-0.5
            out = jnp.concatenate([out[:HD, :rows], out[HD:, rows:]], axis=0)
            act_buf[7, r, cols] = out.T.astype(BF16)

        segment = micro * pairs // 4

        def attend_some(s):
            loop(segment, lambda i: attend(s * segment + i))
            service(pieces + 1 + s)

        loop(4, attend_some)

        def back_copy():
            return remote(give_buf, back_buf.at[l], ks.at[l], kr.at[l], me.other_role())

        @pl.when(me.role == 1)
        def _():
            back_copy().start()

        @pl.when(me.role == 0)
        def _():
            back_copy().wait_recv()

            def some(i):
                r = tile(i, block)
                act_buf[1, r, :] = (h_buf[r, :] + back_buf[l, 0, r, :].astype(F32)).astype(BF16)
                act_buf[2, r, :] = (acc_buf[r, :] + back_buf[l, 1, r, :].astype(F32)).astype(BF16)

            loop(rows_all // block, some)

        @pl.when(me.role == 1)
        def _():
            def some(i):
                r = tile(i, block)
                act_buf[1, r, :] = h_buf[r, :].astype(BF16)
                act_buf[2, r, :] = acc_buf[r, :].astype(BF16)

            loop(rows_all // block, some)

        get_hidden(l, 0).start()
        acc_buf[...] = jnp.zeros_like(acc_buf)
        get(l, 0, 8).wait()

        def project(i):
            s = lax.rem(i, 2)

            @pl.when(i < 2)
            def _():
                get_w(base + 1 + i, 1 - s).start()

            part = act_buf.at[jnp.where(i == 0, 7, i)]
            produce(n0 + 2 * pieces + 1 + i, act_buf.at[8], part)
            get_w(base + i, s).wait()

            def add(cols, value):
                acc_buf[:, cols] += value

            through(part, s, add)
            service(pieces + 5 + i)

        loop(3, project)
        get_hidden(l, 0).wait()
        norm_back(0, l)

        @pl.when(me.role == 1)
        def _():
            back_copy().wait_send()

    loop(layers, layer)
    lower(low_buf, g_buf)
    done = pltpu.make_async_copy(low_buf, frames_grad_ref, out_sem)
    done.start()

    per = 128 * devices // width
    for group in range(width // 128):
        tab_role[group] = tab_sum[:, group * 128 : group * 128 + 128]

    def tab_copy(by):
        to = lax.rem(me.dp + by, devices)
        return remote(tab_role.at[lax.div(to, per)], tab_in.at[me.dp], ts.at[by - 1], tr.at[by - 1], me.around(by))

    def tab_wait(by):
        here = tab_in.at[lax.rem(me.dp - by + devices, devices)]
        remote(here, here, ts.at[by - 1], tr.at[by - 1], me.around(by)).wait_recv()

    loop(devices - 1, lambda i: tab_copy(i + 1).start())
    tab_in[me.dp] = tab_role[lax.div(me.dp, per)]
    last = layers * per_layer - 1
    send_stage(last).wait()
    loop(2, lambda i: reduce.step(last + i))
    loop(devices - 1, lambda i: tab_wait(i + 1))
    loop(devices - 1, lambda i: tab_copy(i + 1).wait_send())
    total = tab_in[0]
    for i in range(1, devices):
        total = total + tab_in[i]
    tab_back[0] = total
    swap = remote(tab_back.at[0], tab_back.at[1], rs_sem, rr_sem, me.other_role())
    swap.start()
    loop(reduce.lag - 1, lambda i: reduce.step(last + 2 + i))
    swap.wait()
    table_out_ref[...] = tab_back[0] + tab_back[1]
    reduce.finish()
    done.wait()


def backward(full, saved, hidden, probs, cotangent, table, pick, used, outers, layers, shard, collective_id):
    count = full.shape[0]
    rows_all, width = cotangent.shape
    keys = probs.shape[2]
    small = table.shape[0]
    dma = pltpu.SemaphoreType.DMA
    devices = 4 * outers
    split = width // 4
    any_space = pl.BlockSpec(memory_space=pl.ANY)
    vmem = pl.BlockSpec(memory_space=pltpu.VMEM)
    grid_rows = (rows_all, width)
    return pl.pallas_call(
        functools.partial(backward_kernel, layers, outers, split),
        out_shape=(
            jax.ShapeDtypeStruct((count, outers, 2, 2, shard, width), BF16),
            jax.ShapeDtypeStruct((count, shard, width), F32),
            jax.ShapeDtypeStruct(grid_rows, BF16),
            jax.ShapeDtypeStruct((small, 128), F32),
        ),
        in_specs=[any_space, any_space, any_space, any_space, vmem, vmem, vmem, vmem],
        out_specs=(any_space, any_space, any_space, vmem),
        scratch_shapes=[
            pltpu.VMEM(grid_rows, F32),
            pltpu.VMEM(grid_rows, F32),
            pltpu.VMEM(grid_rows, F32),
            pltpu.VMEM((2, width, width), BF16),
            pltpu.VMEM(grid_rows, BF16),
            pltpu.VMEM((9,) + grid_rows, BF16),
            pltpu.VMEM((2,) + grid_rows, BF16),
            pltpu.VMEM((layers, 2) + grid_rows, BF16),
            pltpu.VMEM((2, keys, keys), BF16),
            pltpu.VMEM((2, outers, 2, 2, shard, width), BF16),
            pltpu.VMEM((small, width), F32),
            pltpu.VMEM((devices, small, 128), F32),
            pltpu.VMEM((width // 128, small, 128), F32),
            pltpu.VMEM((2, small, 128), F32),
            dma((9,)), dma(()), dma((2,)), dma((2,)), dma((2,)), dma((layers,)), dma((layers,)),
            dma((devices - 1,)), dma((devices - 1,)), dma(()), dma(()), dma(()),
        ]
        + Reduce.scratch(outers, shard, width, split),
        compiler_params=pltpu.CompilerParams(
            collective_id=collective_id, has_side_effects=True, vmem_limit_bytes=60 * 2**20
        ),
        name="backward_and_reduce",
    )(full, saved, hidden, probs, cotangent, table, pick, used)


def prepare(
    inner_weight, outer_weight, expand_weight, shrink_weight, causal_gain, causal_shift,
    section_scale, section_shift, prompt_lengths, target_lengths, sections, rows,
):
    is_target = lax.axis_index("role") == 1
    layers, shard, _ = inner_weight.shape
    width = outer_weight.shape[2]
    devices = width // shard
    pieces = expand_weight.shape[2] // width
    segs = section_scale.shape[0]
    micro = prompt_lengths.shape[0]
    outer = outer_weight[:, None]
    inner = inner_weight.reshape(layers, shard, 3, width).transpose(0, 2, 1, 3)
    expand = expand_weight.reshape(layers, shard, devices, pieces, shard).transpose(0, 3, 1, 2, 4)
    expand = expand.reshape(layers, pieces, 1, shard, width)
    shrink = shrink_weight.reshape(layers, pieces, 1, shard, width)
    feed = jnp.concatenate([expand, shrink], axis=2).reshape(layers, 2 * pieces, shard, width)
    parts = jnp.concatenate([inner, outer, feed], axis=1).reshape(-1, shard, width)

    small = jnp.concatenate(
        [causal_gain, causal_shift, section_scale.reshape(2 * segs, -1), section_shift.reshape(2 * segs, -1)], axis=0
    )
    per = 128 // shard
    spot = (lax.axis_index("dp") % per) * shard
    piece = lax.dynamic_update_slice(jnp.zeros((small.shape[0], 128), BF16), small, (0, spot))

    masks = [[], []]
    section_frames = []
    for m in range(micro):
        prompt_row, target_row, section_row = prompt_lengths[m, 0], target_lengths[m, 0], sections[m, 0]
        prompt_segment, prompt_position, prompt_member = frame_tags(prompt_row, jnp.zeros_like(prompt_row), rows)
        target_segment, target_position, target_member = frame_tags(target_row, prompt_row, rows)
        own_segment = jnp.where(is_target, target_segment, prompt_segment)
        own_position = jnp.where(is_target, target_position, prompt_position)
        own_member = jnp.where(is_target, target_member, prompt_member)
        same_far = (own_segment[None, :] == prompt_segment[:, None]) & is_target
        same_own = own_segment[None, :] == own_segment[:, None]
        causal_own = same_own & (own_position[:, None] <= own_position[None, :])
        masks[0].append(jnp.concatenate([same_far, causal_own], axis=0))
        masks[1].append(jnp.concatenate([same_far, same_own], axis=0))
        section_frames.append(jnp.sum(jnp.where(own_member, section_row[None, :], 0), axis=1))
    bias = jnp.where(jnp.stack([jnp.stack(one) for one in masks]), 0.0, -1e30).astype(BF16)
    section = jnp.concatenate(section_frames)
    none = jnp.zeros_like(section)
    first, second = 4 + 2 * section, 4 + 2 * segs + 2 * section
    used = jnp.stack([none, none + 2, none + 1, none + 3, first, second, first + 1, second + 1])
    return parts, piece, used, bias


def body(
    frames, cotangent, inner_weight, outer_weight, expand_weight, shrink_weight, causal_gain, causal_shift,
    section_scale, section_shift, prompt_lengths, target_lengths, sections,
):
    _, micro, rows, width = frames.shape
    layers, shard, _ = inner_weight.shape
    devices = width // shard
    outers = devices // 4
    pieces = expand_weight.shape[2] // width
    segs = section_scale.shape[0]
    parts, piece, used, bias = prepare(
        inner_weight, outer_weight, expand_weight, shrink_weight, causal_gain, causal_shift,
        section_scale, section_shift, prompt_lengths, target_lengths, sections, rows,
    )
    entries = jnp.arange(piece.shape[0], dtype=jnp.int32)
    pick = (used[:, :, None] == entries[None, None, :]).astype(BF16)
    pick_t = (used[:, None, :] == entries[None, :, None]).astype(BF16)
    full, saved, hidden, probs, mixed, table = forward(
        parts, frames.reshape(micro * rows, width), piece, pick, bias, outers, layers, 0
    )
    _, owned, frames_grad, small = backward(
        full.reshape(-1, width, width), saved, hidden, probs, cotangent.reshape(micro * rows, width),
        table, pick, pick_t, outers, layers, shard, 1,
    )
    owned = owned.reshape(layers, -1, shard, width)[::-1]
    feed = owned[:, : 2 * pieces].reshape(layers, pieces, 2, shard, width)
    inner_grad = owned[:, 2 * pieces + 1 :].transpose(0, 2, 1, 3).reshape(layers, shard, 3 * width)
    outer_grad = owned[:, 2 * pieces]
    expand_grad = feed[:, :, 1].reshape(layers, pieces, shard, devices, shard).transpose(0, 2, 3, 1, 4).reshape(layers, shard, -1)
    shrink_grad = feed[:, :, 0].reshape(layers, pieces * shard, width)
    per = 128 // shard
    spot = (lax.axis_index("dp") % per) * shard
    small = lax.dynamic_slice(small, (0, spot), (small.shape[0], shard))
    return (
        mixed.reshape(1, micro, rows, width), frames_grad.reshape(1, micro, rows, width),
        inner_grad, outer_grad, expand_grad, shrink_grad,
        small[0:2], small[2:4],
        small[4 : 4 + 2 * segs].reshape(segs, 2, shard),
        small[4 + 2 * segs :].reshape(segs, 2, shard),
    )


def solution(mesh):
    rows = P("role", None, "dp", None)
    second = P(None, "dp", None)
    placed = (rows, rows, second, second, second, second, P(None, "dp"), P(None, "dp"), P(None, None, "dp"), P(None, None, "dp"), second, second, second)
    given = (rows, rows, second, second, second, second, P(None, "dp"), P(None, "dp"), P(None, None, "dp"), P(None, None, "dp"))
    return jax.shard_map(body, mesh=mesh, in_specs=placed, out_specs=given, check_vma=False)
```

```python
import functools

import jax
import jax.numpy as jnp
from jax import lax
from jax.experimental import pallas as pl
from jax.experimental.pallas import tpu as pltpu
from jax.sharding import PartitionSpec as P

HEADS = 16
HD = 64
MESH = pl.DeviceIdType.MESH
SLOTS = 4
F32 = jnp.float32
BF16 = jnp.bfloat16


class Place:
    def __init__(self, outer_count):
        self.outers = outer_count
        self.role = lax.axis_index("role")
        dp = lax.axis_index("dp")
        self.core = lax.rem(dp, 2)
        self.pair = lax.rem(lax.div(dp, 2), 2)
        self.outer = lax.div(dp, 4)
        self.dp = dp

    def at(self, role, outer, pair, core):
        return (role, (outer * 2 + pair) * 2 + core)

    def sibling(self):
        return self.at(self.role, self.outer, self.pair, 1 - self.core)

    def across(self):
        return self.at(self.role, self.outer, 1 - self.pair, self.core)

    def other_role(self):
        return self.at(1 - self.role, self.outer, self.pair, self.core)

    def along(self, by):
        return self.at(self.role, lax.rem(self.outer + by, self.outers), self.pair, self.core)

    def around(self, by):
        return (self.role, lax.rem(self.dp + by, 4 * self.outers))

    def greet(self):
        barrier = pltpu.get_barrier_semaphore()
        pl.semaphore_signal(barrier, inc=1, device_id=self.other_role(), device_id_type=MESH)

        def greet_one(i, carry):
            pl.semaphore_signal(barrier, inc=1, device_id=self.around(i + 1), device_id_type=MESH)
            return carry

        lax.fori_loop(0, 4 * self.outers - 1, greet_one, 0)
        pl.semaphore_wait(barrier, 4 * self.outers)


def remote(src, dst, send, recv, peer):
    return pltpu.make_async_remote_copy(
        src_ref=src, dst_ref=dst, send_sem=send, recv_sem=recv, device_id=peer, device_id_type=MESH
    )


def frame_tags(lengths, offsets, total_rows):
    places = jnp.arange(total_rows, dtype=jnp.int32)
    segs = lengths.shape[0]
    upto = jnp.arange(segs)[:, None] >= jnp.arange(segs)[None, :]
    finish = jnp.sum(jnp.where(upto, lengths[None, :], 0), axis=1)
    segment = jnp.sum((places[:, None] >= finish[None, :]).astype(jnp.int32), axis=1)
    member = segment[:, None] == jnp.arange(segs, dtype=jnp.int32)[None, :]
    shifted = offsets - (finish - lengths)
    position = places + jnp.sum(jnp.where(member, shifted[None, :], 0), axis=1)
    return (segment, position, member)


def dot(a, b):
    return jnp.dot(a, b, preferred_element_type=F32)


def dot_t(a, b):
    return lax.dot_general(a, b, (((1,), (1,)), ((), ())), preferred_element_type=F32)


def t_dot(a, b):
    return lax.dot_general(a, b, (((0,), (0,)), ((), ())), preferred_element_type=F32)


def normalize(hidden):
    average = jnp.mean(hidden, axis=-1, keepdims=True)
    centred = hidden - average
    spread = jnp.mean(centred * centred, axis=-1, keepdims=True)
    inverse = lax.rsqrt(spread + 1e-05)
    return centred * inverse, inverse


def norm_backward(grad, scale, unit, inverse):
    inner = grad * scale
    return inverse * (
        inner - jnp.mean(inner, axis=-1, keepdims=True) - unit * jnp.mean(inner * unit, axis=-1, keepdims=True)
    )


def gelu_parts(upper):
    cumulative = 0.5 * (1.0 + lax.erf(upper * 0.7071067811865476))
    density = jnp.exp(-0.5 * upper * upper) * 0.3989422804014327
    return upper * cumulative, cumulative + upper * density


class Gather:
    lag = 7

    def __init__(self, me, part_ref, full_ref, split, sems):
        self.me, self.part, self.full, self.split = me, part_ref, full_ref, split
        self.own_sem, self.zs, self.zr, self.xs, self.xr, self.us, self.ur, self.vs, self.vr, self.cs, self.cr = sems
        self.half = part_ref.shape[-1] // 2
        self.main = self.half - split
        self.steps = 2 * part_ref.shape[0]

    @staticmethod
    def semaphores(many):
        dma = pltpu.SemaphoreType.DMA
        return [
            dma((8,)),
            dma((8, many)), dma((8, many)),
            dma((8,)), dma((8,)),
            dma((12, many)), dma((12, many)),
            dma((8,)), dma((8,)),
            dma((8,)), dma((8,)),
        ]

    def cols(self, h, offset, size):
        return pl.ds(pl.multiple_of(lax.rem(h, 2) * self.half + offset, 128), size)

    def main_cols(self, h):
        return self.cols(h, self.me.role * self.split, self.main)

    def give_cols(self, h):
        return self.cols(h, self.me.role * self.main, self.split)

    def take_cols(self, h):
        return self.cols(h, (1 - self.me.role) * self.main, self.split)

    def before(self, by):
        return lax.rem(self.me.outer - by + self.me.outers, self.me.outers)

    def own(self, h):
        me, cols = self.me, self.cols(h, 0, self.half)
        return pltpu.make_async_copy(
            self.part.at[lax.div(h, 2), :, cols], self.full.at[lax.div(h, 2), me.outer, me.pair, me.core, :, cols], self.own_sem.at[lax.rem(h, 8)]
        )

    def z_copy(self, h, by):
        me, cols, s = self.me, self.main_cols(h), lax.rem(h, 8)
        return remote(
            self.part.at[lax.div(h, 2), :, cols],
            self.full.at[lax.div(h, 2), me.outer, me.pair, me.core, :, cols],
            self.zs.at[s, by - 1], self.zr.at[s, by - 1], me.along(by),
        )

    def z_wait(self, h, by):
        me, s = self.me, lax.rem(h, 8)
        dst = self.full.at[lax.div(h, 2), self.before(by), me.pair, me.core, :, self.main_cols(h)]
        remote(dst, dst, self.zs.at[s, by - 1], self.zr.at[s, by - 1], me.along(by)).wait_recv()

    def x_copy(self, h, pair):
        me, s = self.me, lax.rem(h, 8)
        ref = self.full.at[lax.div(h, 2), :, pair, me.core, :, self.main_cols(h)]
        return remote(ref, ref, self.xs.at[s], self.xr.at[s], me.across())

    def u_copy(self, h, by, cols):
        me, s = self.me, lax.rem(h, 12)
        ref = self.full.at[lax.div(h, 2), self.before(by), me.pair, me.core, :, cols]
        return remote(ref, ref, self.us.at[s, by - 1], self.ur.at[s, by - 1], me.other_role())

    def v_copy(self, h, cols):
        me, s = self.me, lax.rem(h, 8)
        ref = self.full.at[lax.div(h, 2), :, 1 - me.pair, me.core, :, cols]
        return remote(ref, ref, self.vs.at[s], self.vr.at[s], me.other_role())

    def c_copy(self, h, core):
        s = lax.rem(h, 8)
        ref = self.full.at[lax.div(h, 2), :, :, core, :, self.cols(h, 0, self.half)]
        return remote(ref, ref, self.cs.at[s], self.cr.at[s], self.me.sibling())

    def step(self, t):
        me, count = self.me, self.steps
        others = range(1, me.outers)

        @pl.when(t < count)
        def _():
            self.own(t).start()
            for by in others:
                self.z_copy(t, by).start()

        @pl.when((t >= 2) & (t < count + 2))
        def _():
            h = t - 2
            self.own(h).wait()
            for by in others:
                self.z_wait(h, by)
            self.x_copy(h, me.pair).start()
            for by in others:
                self.u_copy(h, by, self.give_cols(h)).start()

        @pl.when((t >= 4) & (t < count + 4))
        def _():
            h = t - 4
            self.x_copy(h, 1 - me.pair).wait_recv()
            self.v_copy(h, self.give_cols(h)).start()
            for by in others:
                self.z_copy(h, by).wait_send()

        @pl.when((t >= 6) & (t < count + 6))
        def _():
            h = t - 6
            for by in others:
                self.u_copy(h, by, self.take_cols(h)).wait_recv()
            self.v_copy(h, self.take_cols(h)).wait_recv()
            self.c_copy(h, me.core).start()
            for by in others:
                self.u_copy(h, by, self.give_cols(h)).wait_send()
            self.x_copy(h, me.pair).wait_send()
            self.v_copy(h, self.give_cols(h)).wait_send()

        @pl.when((t >= 7) & (t < count + 7))
        def _():
            h = t - 7
            self.c_copy(h, 1 - me.core).wait_recv()
            self.c_copy(h, me.core).wait_send()


def loop(count, action):
    def one(i, carry):
        action(i)
        return carry

    lax.fori_loop(0, count, one, 0)


def tile(i, size):
    return pl.ds(pl.multiple_of(i * size, size), size)


WIDE = 256


def forward_kernel(
    layers, outers, split,
    part_ref, frames_ref, piece_ref, pick_ref, bias_ref,
    full_ref, saved_ref, hidden_ref, probs_ref, mixed_ref, table_ref,
    tab_in, h_buf, a_buf, qkv_buf, far_in, far_buf, mix_buf, f_buf, lift_buf, slope_buf, w_buf, p_buf,
    ts, tr, w_sem, save_sem, h_sem, p_sem, out_sem, ks, kr, *gather_sems,
):
    me = Place(outers)
    devices = 4 * outers
    rows_all, width = frames_ref.shape
    per_layer = part_ref.shape[0] // layers
    pieces = (per_layer - 4) // 2
    micro = bias_ref.shape[1]
    rows = rows_all // micro
    pairs = width // 128
    gather = Gather(me, part_ref, full_ref, split, gather_sems)
    me.greet()

    def piece_copy(by):
        return remote(piece_ref, tab_in.at[me.dp], ts.at[by - 1], tr.at[by - 1], me.around(by))

    def piece_wait(by):
        here = tab_in.at[(me.dp - by + devices) % devices]
        remote(here, here, ts.at[by - 1], tr.at[by - 1], me.around(by)).wait_recv()

    loop(devices - 1, lambda i: piece_copy(i + 1).start())
    tab_in[me.dp] = piece_ref[...]

    @pl.when(me.role == 0)
    def _():
        far_buf[...] = jnp.zeros_like(far_buf)
        far_in[...] = jnp.zeros_like(far_in)

    ahead = gather.lag - 4
    loop(2, gather.step)
    loop(devices - 1, lambda i: piece_wait(i + 1))
    loop(devices - 1, lambda i: piece_copy(i + 1).wait_send())
    per = 128 * devices // width
    for group in range(width // 128):
        total = tab_in[group * per]
        for i in range(1, per):
            total = total + tab_in[group * per + i]
        table_ref[:, group * 128 : group * 128 + 128] = total

    def load_rows(i):
        r = tile(i, 64)
        h_buf[0, r, :] = frames_ref[r, :].astype(F32)

    loop(rows_all // 64, load_rows)

    def load(k):
        return pltpu.make_async_copy(full_ref.at[k], w_buf.at[lax.rem(k, 2)], w_sem.at[lax.rem(k, 2)])

    def matmul(in_ref, k, finish):
        load(k).wait()

        def columns(n):
            cols = tile(n, WIDE)
            w = w_buf[lax.rem(k, 2), :, :, :, :, cols].reshape(width, WIDE)
            finish(cols, dot(in_ref[...], w))

        loop(width // WIDE, columns)

    def norm(index, src, dst_ref, l):
        def some(i):
            r = tile(i, 64)
            unit, _ = normalize(h_buf[src, r, :])
            scale = dot(pick_ref[l * 4 + 2 * index, r, :], table_ref[...])
            shift = dot(pick_ref[l * 4 + 2 * index + 1, r, :], table_ref[...])
            dst_ref[r, :] = (scale * unit + shift).astype(BF16)

        loop(rows_all // 64, some)

    def save_at(l, ref, slot):
        return pltpu.make_async_copy(ref, saved_ref.at[l, slot], save_sem.at[slot])

    def save_hidden_at(l, which):
        return pltpu.make_async_copy(h_buf.at[which], hidden_ref.at[l, which], h_sem.at[which])

    def far_copy(l):
        return remote(a_buf, far_in.at[l], ks.at[l], kr.at[l], me.other_role())

    def begin(l):
        save_hidden_at(l, 0).start()
        norm(0, 0, a_buf, l)
        save_at(l, a_buf, 0).start()

        @pl.when(me.role == 0)
        def _():
            far_copy(l).start()

    begin(0)
    loop(gather.lag, lambda i: gather.step(i + 2))

    def layer(l):
        base = l * per_layer

        def save(ref, slot):
            return save_at(l, ref, slot)

        def save_hidden(which):
            return save_hidden_at(l, which)

        load(base).start()

        def project(i):
            def keep(cols, value):
                qkv_buf[i, :, cols] = value.astype(BF16)

            matmul(a_buf, base + i, keep)
            gather.step(2 * (base + i) + 6 + ahead)
            gather.step(2 * (base + i) + 7 + ahead)

            @pl.when(i < 2)
            def _():
                load(base + i + 1).start()

            save(qkv_buf.at[i], 1 + i).start()

        loop(3, project)

        @pl.when(me.role == 1)
        def _():
            load(base + 1).start()
            load(base + 2).start()
            far_copy(l).wait_recv()

            def project_far(i):
                def keep(cols, value):
                    far_buf[i, :, cols] = value.astype(BF16)

                matmul(far_in.at[l], base + 1 + i, keep)

            loop(2, project_far)

        load(base + 3).start()
        save(far_in.at[l], 8 + 2 * pieces).start()
        save(far_buf.at[0], 4).start()
        save(far_buf.at[1], 5).start()

        def save_probs(it):
            return pltpu.make_async_copy(p_buf.at[lax.rem(it, 2)], probs_ref.at[l, it], p_sem.at[lax.rem(it, 2)])

        def attend(it):
            m, p = lax.div(it, pairs), lax.rem(it, pairs)
            r, cols = tile(m, rows), tile(p, 128)
            first = lax.broadcasted_iota(jnp.int32, (rows, 128), 1) < HD
            q = qkv_buf[0, r, cols].astype(F32) * HD**-0.5
            both = jnp.concatenate([jnp.where(first, q, 0.0).astype(BF16), jnp.where(first, 0.0, q).astype(BF16)], axis=0)
            keys = jnp.concatenate([far_buf[0, r, cols], qkv_buf[1, r, cols]], axis=0)
            values = jnp.concatenate([far_buf[1, r, cols], qkv_buf[2, r, cols]], axis=0)
            bias = bias_ref[l, m].astype(F32)
            scores = dot_t(keys, both) + jnp.concatenate([bias, bias], axis=1)
            exponent = jnp.exp(scores - jnp.max(scores, axis=0, keepdims=True))
            soft = (exponent * (1.0 / jnp.sum(exponent, axis=0, keepdims=True))).astype(BF16)

            @pl.when(it >= 2)
            def _():
                save_probs(it - 2).wait()

            p_buf[lax.rem(it, 2)] = soft
            save_probs(it).start()
            out = t_dot(values, soft)
            out = jnp.concatenate([out[:HD, :rows], out[HD:, rows:]], axis=0)
            mix_buf[r, cols] = out.T.astype(BF16)

        segment = micro * pairs // 4

        def attend_some(s):
            loop(segment, lambda i: attend(s * segment + i))
            gather.step(2 * base + 12 + s + ahead)

        loop(4, attend_some)
        save_probs(micro * pairs - 2).wait()
        save_probs(micro * pairs - 1).wait()
        save(mix_buf, 6).start()
        load(base + 4).start()

        def keep_middle(cols, value):
            h_buf[1, :, cols] = h_buf[0, :, cols] + value

        matmul(mix_buf, base + 3, keep_middle)
        save_hidden(1).start()
        save_hidden(0).wait()
        norm(1, 1, f_buf, l)
        save(f_buf, 7).start()
        h_buf[0] = h_buf[1]

        def feed(j):
            load(base + 5 + 2 * j).start()

            def raise_columns(cols, value):
                up, slope = gelu_parts(value)
                lift_buf[:, cols] = up.astype(BF16)
                slope_buf[:, cols] = slope.astype(BF16)

            matmul(f_buf, base + 4 + 2 * j, raise_columns)
            lift_save = pltpu.make_async_copy(lift_buf, saved_ref.at[l, 8 + j], save_sem.at[9 + 2 * pieces])
            slope_save = pltpu.make_async_copy(slope_buf, saved_ref.at[l, 8 + pieces + j], save_sem.at[8])
            lift_save.start()
            slope_save.start()
            gather.step(2 * base + 16 + 4 * j + ahead)
            gather.step(2 * base + 17 + 4 * j + ahead)

            @pl.when(j < pieces - 1)
            def _():
                load(base + 6 + 2 * j).start()

            def add(cols, value):
                h_buf[0, :, cols] += value

            matmul(lift_buf, base + 5 + 2 * j, add)

            @pl.when(j < pieces - 1)
            def _():
                gather.step(2 * base + 18 + 4 * j + ahead)
                gather.step(2 * base + 19 + 4 * j + ahead)

            lift_save.wait()
            slope_save.wait()

        loop(pieces, feed)
        save_hidden(1).wait()
        save(a_buf, 0).wait()
        for i in range(3):
            save(qkv_buf.at[i], 1 + i).wait()
        save(far_buf.at[0], 4).wait()
        save(far_buf.at[1], 5).wait()
        save(mix_buf, 6).wait()
        save(f_buf, 7).wait()
        save(far_in.at[l], 8 + 2 * pieces).wait()

        @pl.when(me.role == 0)
        def _():
            far_copy(l).wait_send()

        @pl.when(l < layers - 1)
        def _():
            begin(l + 1)

    loop(layers, layer)

    def store_rows(i):
        r = tile(i, 64)
        a_buf[r, :] = h_buf[0, r, :].astype(BF16)

    loop(rows_all // 64, store_rows)
    done = pltpu.make_async_copy(a_buf, mixed_ref, out_sem)
    done.start()
    done.wait()


def forward(parts, frames, piece, pick, bias, outers, layers, collective_id):
    count, shard, width = parts.shape
    rows_all = frames.shape[0]
    pieces = (count // layers - 4) // 2
    many = outers - 1
    dma = pltpu.SemaphoreType.DMA
    devices = 4 * outers
    split = width // 8
    micro = bias.shape[1]
    keys, rows = bias.shape[2:]
    pairs = width // 128
    any_space = pl.BlockSpec(memory_space=pl.ANY)
    vmem = pl.BlockSpec(memory_space=pltpu.VMEM)
    grid_rows = (rows_all, width)
    return pl.pallas_call(
        functools.partial(forward_kernel, layers, outers, split),
        out_shape=(
            jax.ShapeDtypeStruct((count, outers, 2, 2, shard, width), BF16),
            jax.ShapeDtypeStruct((layers, 9 + 2 * pieces) + grid_rows, BF16),
            jax.ShapeDtypeStruct((layers, 2) + grid_rows, F32),
            jax.ShapeDtypeStruct((layers, micro * pairs, keys, 2 * rows), BF16),
            jax.ShapeDtypeStruct(grid_rows, BF16),
            jax.ShapeDtypeStruct((piece.shape[0], width), BF16),
        ),
        in_specs=[any_space, vmem, vmem, vmem, vmem],
        out_specs=(any_space, any_space, any_space, any_space, any_space, vmem),
        scratch_shapes=[
            pltpu.VMEM((devices,) + piece.shape, BF16),
            pltpu.VMEM((2,) + grid_rows, F32),
            pltpu.VMEM(grid_rows, BF16),
            pltpu.VMEM((3,) + grid_rows, BF16),
            pltpu.VMEM((layers,) + grid_rows, BF16),
            pltpu.VMEM((2,) + grid_rows, BF16),
            pltpu.VMEM(grid_rows, BF16),
            pltpu.VMEM(grid_rows, BF16),
            pltpu.VMEM(grid_rows, BF16),
            pltpu.VMEM(grid_rows, BF16),
            pltpu.VMEM((2, outers, 2, 2, shard, width), BF16),
            pltpu.VMEM((2, keys, 2 * rows), BF16),
            dma((devices - 1,)), dma((devices - 1,)),
            dma((2,)), dma((10 + 2 * pieces,)), dma((2,)), dma((2,)), dma(()), dma((layers,)), dma((layers,)),
        ]
        + Gather.semaphores(many),
        compiler_params=pltpu.CompilerParams(
            collective_id=collective_id, has_side_effects=True, vmem_limit_bytes=58 * 2**20
        ),
        name="gather_and_forward",
    )(parts, frames, piece, pick, bias)


class Reduce:
    lag = 8

    def __init__(self, me, grad_ref, out_ref, split, refs):
        self.me, self.grad, self.out, self.split = me, grad_ref, out_ref, split
        (
            self.own_buf, self.core_buf, self.role_buf, self.pair_buf, self.outer_buf, self.last_buf, self.sum_buf, self.low_buf,
            self.end_buf, self.fin_buf,
            self.own_sem, self.cs, self.cr, self.ys, self.yr, self.xs, self.xr, self.zs, self.zr, self.es, self.er, self.fs,
        ) = refs
        self.half = grad_ref.shape[-1] // 2
        self.main = self.half - split
        self.steps = 2 * grad_ref.shape[0]

    @staticmethod
    def scratch(outers, rows, width, split):
        dma = pltpu.SemaphoreType.DMA
        many = outers - 1
        half = width // 2
        main = half - split
        return [
            pltpu.VMEM((2, outers, 2, rows, half), BF16),
            pltpu.VMEM((4, outers, 2, rows, half), BF16),
            pltpu.VMEM((6, outers, 2, rows, split), BF16),
            pltpu.VMEM((6, outers, rows, main), BF16),
            pltpu.VMEM((6, many, rows, main), BF16),
            pltpu.VMEM((4, rows, main), BF16),
            pltpu.VMEM((6, outers, 2, rows, half), BF16),
            pltpu.VMEM((4, outers, rows, main), BF16),
            pltpu.VMEM((4, rows, main), BF16),
            pltpu.VMEM((4, rows, half), F32),
            dma((2,)),
            dma((4,)), dma((4,)),
            dma((6,)), dma((6,)),
            dma((6,)), dma((6,)),
            dma((6, many)), dma((6, many)),
            dma((4,)), dma((4,)),
            dma((4,)),
        ]

    def cols(self, offset, size):
        return pl.ds(pl.multiple_of(offset, 128), size)

    def main_cols(self):
        return self.cols(self.me.role * self.split, self.main)

    def keep_cols(self):
        return self.cols(self.me.role * self.main, self.split)

    def give_cols(self):
        return self.cols((1 - self.me.role) * self.main, self.split)

    def part(self, k, core):
        return self.grad.at[lax.div(k, 2), :, :, core, :, self.cols(lax.rem(k, 2) * self.half, self.half)]

    def own(self, k):
        s = lax.rem(k, 2)
        return pltpu.make_async_copy(self.part(k, self.me.core), self.own_buf.at[s], self.own_sem.at[s])

    def c_copy(self, k):
        s = lax.rem(k, 4)
        return remote(self.part(k, 1 - self.me.core), self.core_buf.at[s], self.cs.at[s], self.cr.at[s], self.me.sibling())

    def y_copy(self, k):
        s = lax.rem(k, 6)
        return remote(
            self.sum_buf.at[s, :, :, :, self.give_cols()], self.role_buf.at[s], self.ys.at[s], self.yr.at[s], self.me.other_role()
        )

    def x_copy(self, k):
        s = lax.rem(k, 6)
        return remote(
            self.sum_buf.at[s, :, 1 - self.me.pair, :, self.main_cols()],
            self.pair_buf.at[s], self.xs.at[s], self.xr.at[s], self.me.across(),
        )

    def z_copy(self, k, by):
        s = lax.rem(k, 6)
        me = self.me
        return remote(
            self.low_buf.at[lax.rem(k, 4), lax.rem(me.outer + by, me.outers)], self.outer_buf.at[s, by - 1],
            self.zs.at[s, by - 1], self.zr.at[s, by - 1], me.along(by),
        )

    def e_copy(self, k):
        s = lax.rem(k, 4)
        return remote(self.end_buf.at[s], self.last_buf.at[s], self.es.at[s], self.er.at[s], self.me.other_role())

    def f_copy(self, k):
        s = lax.rem(k, 4)
        cols = self.cols(lax.rem(k, 2) * self.half, self.half)
        return pltpu.make_async_copy(self.fin_buf.at[s], self.out.at[lax.div(k, 2), :, cols], self.fs.at[s])

    def step(self, t):
        me, count, split, main = self.me, self.steps, self.split, self.main
        others = range(1, me.outers)

        @pl.when((t >= 0) & (t < count))
        def _():
            self.own(t).start()
            self.c_copy(t).start()

        @pl.when((t >= 1) & (t < count + 1))
        def _():
            k = t - 1
            self.own(k).wait()
            self.c_copy(k).wait()

            def add(i):
                o, p = lax.div(i, 2), lax.rem(i, 2)
                self.sum_buf[lax.rem(k, 6), o, p] = self.own_buf[lax.rem(k, 2), o, p] + self.core_buf[lax.rem(k, 4), o, p]

            loop(2 * me.outers, add)
            self.y_copy(k).start()

        @pl.when((t >= 3) & (t < count + 3))
        def _():
            k = t - 3
            s = lax.rem(k, 6)
            self.y_copy(k).wait()
            keep = self.keep_cols()

            def add(i):
                o, p = lax.div(i, 2), lax.rem(i, 2)
                self.sum_buf[s, o, p, :, keep] = self.sum_buf[s, o, p, :, keep] + self.role_buf[s, o, p]

            loop(2 * me.outers, add)
            self.x_copy(k).start()

        @pl.when((t >= 5) & (t < count + 5))
        def _():
            k = t - 5
            s = lax.rem(k, 6)
            self.x_copy(k).wait()
            cols = self.main_cols()

            def add(o):
                self.low_buf[lax.rem(k, 4), o] = self.sum_buf[s, o, me.pair, :, cols] + self.pair_buf[s, o]

            loop(me.outers, add)
            for by in others:
                self.z_copy(k, by).start()

        @pl.when((t >= 7) & (t < count + 7))
        def _():
            k = t - 7
            for by in others:
                self.z_copy(k, by).wait()
            total = self.low_buf[lax.rem(k, 4), me.outer].astype(F32)
            for by in others:
                total = total + self.outer_buf[lax.rem(k, 6), by - 1].astype(F32)
            self.end_buf[lax.rem(k, 4)] = total.astype(BF16)
            self.e_copy(k).start()

        @pl.when((t >= 8) & (t < count + 8))
        def _():
            k = t - 8
            s = lax.rem(k, 4)
            self.e_copy(k).wait()

            @pl.when(k >= 4)
            def _():
                self.f_copy(k - 4).wait()

            mid = main - split
            mine = self.end_buf[s].astype(F32)
            theirs = self.last_buf[s].astype(F32)

            @pl.when(me.role == 0)
            def _():
                self.fin_buf[s, :, :split] = mine[:, :split]
                self.fin_buf[s, :, split:main] = mine[:, split:] + theirs[:, :mid]
                self.fin_buf[s, :, main:] = theirs[:, mid:]

            @pl.when(me.role == 1)
            def _():
                self.fin_buf[s, :, :split] = theirs[:, :split]
                self.fin_buf[s, :, split:main] = theirs[:, split:] + mine[:, :mid]
                self.fin_buf[s, :, main:] = mine[:, mid:]

            self.f_copy(k).start()

    def finish(self):
        for k in range(self.steps - 4, self.steps):
            self.f_copy(k).wait()


def backward_kernel(
    layers, outers, split,
    full_ref, saved_ref, hidden_ref, probs_ref, cot_ref, table_ref, pick_ref, used_ref,
    grad_ref, out_ref, frames_grad_ref, table_out_ref,
    g_buf, acc_buf, h_buf, w_buf, low_buf, act_buf, give_buf, back_buf, p_buf, stage_buf, tab_sum, tab_in, tab_role, tab_back,
    act_sem, h_sem, w_sem, p_sem, stage_sem, ks, kr, ts, tr, rs_sem, rr_sem, out_sem, *reduce_refs,
):
    me = Place(outers)
    devices = 4 * outers
    rows_all, width = cot_ref.shape
    per_layer = full_ref.shape[0] // layers
    pieces = (per_layer - 4) // 2
    pairs = width // 128
    micro = probs_ref.shape[1] // pairs
    rows = rows_all // micro
    shard = grad_ref.shape[-2]
    tile_outers = WIDE // (4 * shard)
    block = 128
    reduce = Reduce(me, grad_ref, out_ref, split, reduce_refs)
    me.greet()

    def load_rows(i):
        r = tile(i, block)
        g_buf[r, :] = cot_ref[r, :].astype(F32)

    loop(rows_all // block, load_rows)
    tab_sum[...] = jnp.zeros_like(tab_sum)

    def get(l, item, slot):
        return pltpu.make_async_copy(saved_ref.at[l, item], act_buf.at[slot], act_sem.at[slot])

    def get_hidden(l, which):
        return pltpu.make_async_copy(hidden_ref.at[l, which], h_buf, h_sem)

    def get_w(k, slot):
        return pltpu.make_async_copy(full_ref.at[k], w_buf.at[slot], w_sem.at[slot])

    def send_stage(n):
        s = lax.rem(n, 2)
        return pltpu.make_async_copy(stage_buf.at[s], grad_ref.at[n], stage_sem.at[s])

    def produce(n, left, right, far=None):
        s = lax.rem(n, 2)

        def some(i):
            cols = tile(i, WIDE)
            value = t_dot(left[:, cols], right[...])
            if far is not None:
                value = value + t_dot(far[0][:, cols], far[1][...])
            stage_buf[s, pl.ds(i * tile_outers, tile_outers)] = value.astype(BF16).reshape(tile_outers, 2, 2, shard, width)

        loop(width // WIDE, some)
        send_stage(n).start()

        @pl.when(n >= 1)
        def _():
            send_stage(n - 1).wait()

    def through(left, slot, finish):
        def some(i):
            cols = tile(i, WIDE)
            finish(cols, dot_t(left[...], w_buf[slot, cols, :]))

        loop(width // WIDE, some)

    def lower(dst, src):
        def some(i):
            r = tile(i, block)
            dst[r, :] = src[r, :].astype(BF16)

        loop(rows_all // block, some)

    def norm_back(index, l):
        def some(i):
            r = tile(i, block)
            unit, inverse = normalize(h_buf[r, :])
            scale = dot(pick_ref[l * 4 + 2 * index, r, :], table_ref[...])
            grad = acc_buf[r, :]
            g_buf[r, :] = g_buf[r, :] + norm_backward(grad, scale, unit, inverse)
            for which, values in ((0, grad * unit), (1, grad)):
                picked = used_ref[l * 4 + 2 * index + which, :, r]
                high = values.astype(BF16)
                rest = (values - high.astype(F32)).astype(BF16)
                tab_sum[...] += dot(picked, high) + dot(picked, rest)

        loop(rows_all // block, some)

    def layer(turn):
        l = layers - 1 - turn
        base = l * per_layer
        n0 = turn * per_layer

        def service(index):
            reduce.step(2 * (n0 - 1) + index)

        get(l, 7, 0).start()
        get(l, 8, 1).start()
        get(l, 8 + pieces, 3).start()
        get_w(base + 5, 0).start()
        get_hidden(l, 1).start()
        lower(low_buf, g_buf)
        acc_buf[...] = jnp.zeros_like(acc_buf)
        get(l, 7, 0).wait()

        def feed(j):
            s = lax.rem(j, 2)
            get_w(base + 4 + 2 * j, 1).start()
            get(l, 8 + j, 1 + s).wait()
            get(l, 8 + pieces + j, 3 + s).wait()

            @pl.when(j < pieces - 1)
            def _():
                get(l, 9 + j, 2 - s).start()
                get(l, 9 + pieces + j, 4 - s).start()

            produce(n0 + 2 * j, act_buf.at[1 + s], low_buf)
            service(2 * j)
            get_w(base + 5 + 2 * j, 0).wait()

            def lift(cols, value):
                act_buf[5, :, cols] = (value * act_buf[3 + s, :, cols].astype(F32)).astype(BF16)

            through(low_buf, 0, lift)

            @pl.when(j < pieces - 1)
            def _():
                get_w(base + 7 + 2 * j, 0).start()

            service(2 * j + 1)
            produce(n0 + 2 * j + 1, act_buf.at[0], act_buf.at[5])
            get_w(base + 4 + 2 * j, 1).wait()

            def add(cols, value):
                acc_buf[:, cols] += value

            through(act_buf.at[5], 1, add)

        loop(pieces, feed)
        get_w(base + 3, 0).start()
        get(l, 6, 0).start()
        for i in range(5):
            get(l, 1 + i, 1 + i).start()
        get(l, 8 + 2 * pieces, 9).start()

        def get_probs(it):
            s = lax.rem(it, 2)
            return pltpu.make_async_copy(probs_ref.at[l, it], p_buf.at[s], p_sem.at[s])

        get_probs(0).start()
        get_hidden(l, 1).wait()
        service(2 * pieces)
        norm_back(1, l)
        lower(low_buf, g_buf)
        get(l, 6, 0).wait()
        service(2 * pieces + 1)
        produce(n0 + 2 * pieces, act_buf.at[0], low_buf)
        get_w(base + 3, 0).wait()

        def keep_mixture(cols, value):
            act_buf[6, :, cols] = value.astype(BF16)

        through(low_buf, 0, keep_mixture)
        get_w(base + 1, 0).start()
        get(l, 0, 8).start()
        for i in range(5):
            get(l, 1 + i, 1 + i).wait()

        def attend(it):
            m, p = lax.div(it, pairs), lax.rem(it, pairs)
            r, cols = tile(m, rows), tile(p, 128)
            first = lax.broadcasted_iota(jnp.int32, (rows, 128), 1) < HD

            def both_of(x):
                return jnp.concatenate([jnp.where(first, x, 0.0).astype(BF16), jnp.where(first, 0.0, x).astype(BF16)], axis=0)

            queries = both_of(act_buf[1, r, cols].astype(F32) * HD**-0.5)
            out_grad = both_of(act_buf[6, r, cols].astype(F32))
            keys = jnp.concatenate([act_buf[4, r, cols], act_buf[2, r, cols]], axis=0)
            values = jnp.concatenate([act_buf[5, r, cols], act_buf[3, r, cols]], axis=0)
            get_probs(it).wait()

            @pl.when(it + 1 < micro * pairs)
            def _():
                get_probs(it + 1).start()

            soft_low = p_buf[lax.rem(it, 2)]
            soft = soft_low.astype(F32)
            grad_soft = dot_t(values, out_grad)
            inner = jnp.sum(soft * grad_soft, axis=0, keepdims=True)
            grad_scores = (soft * (grad_soft - inner)).astype(BF16)
            grad_values = dot(soft_low, out_grad)
            grad_keys = dot(grad_scores, queries)
            give_buf[0, r, cols] = grad_keys[:rows].astype(BF16)
            give_buf[1, r, cols] = grad_values[:rows].astype(BF16)
            h_buf[r, cols] = grad_keys[rows:]
            acc_buf[r, cols] = grad_values[rows:]
            out = t_dot(keys, grad_scores) * HD**-0.5
            out = jnp.concatenate([out[:HD, :rows], out[HD:, rows:]], axis=0)
            act_buf[7, r, cols] = out.T.astype(BF16)

        segment = micro * pairs // 8

        def attend_some(s):
            loop(segment, lambda i: attend(s * segment + i))
            service(2 * pieces + 2 + s)

        loop(8, attend_some)

        def some_rows(i):
            r = tile(i, block)
            act_buf[1, r, :] = h_buf[r, :].astype(BF16)
            act_buf[2, r, :] = acc_buf[r, :].astype(BF16)

        loop(rows_all // block, some_rows)
        acc_buf[...] = jnp.zeros_like(acc_buf)
        get(l, 0, 8).wait()
        get(l, 8 + 2 * pieces, 9).wait()

        def back_copy():
            return remote(low_buf, back_buf.at[l], ks.at[l], kr.at[l], me.other_role())

        def add(cols, value):
            acc_buf[:, cols] += value

        def project(i):
            get_w(base + lax.rem(2 + i, 3), 1 - i).start()
            part = act_buf.at[1 + i]
            n = n0 + 2 * pieces + 1 + i

            @pl.when(me.role == 0)
            def _():
                produce(n, act_buf.at[8], part)

            @pl.when(me.role == 1)
            def _():
                produce(n, act_buf.at[8], part, (act_buf.at[9], give_buf.at[i]))

            service(2 * pieces + 10 + 2 * i)
            get_w(base + 1 + i, i).wait()
            through(part, i, add)

            @pl.when(me.role == 1)
            def _():
                def first(cols, value):
                    h_buf[:, cols] = value

                def second(cols, value):
                    low_buf[:, cols] = (h_buf[:, cols] + value).astype(BF16)

                @pl.when(i == 0)
                def _():
                    through(give_buf.at[0], 0, first)

                @pl.when(i == 1)
                def _():
                    through(give_buf.at[1], 1, second)
                    back_copy().start()

            service(2 * pieces + 11 + 2 * i)

        loop(2, project)
        get_hidden(l, 0).start()
        produce(n0 + 2 * pieces + 3, act_buf.at[8], act_buf.at[7])
        service(2 * pieces + 14)
        get_w(base, 0).wait()
        through(act_buf.at[7], 0, add)
        service(2 * pieces + 15)

        @pl.when(me.role == 0)
        def _():
            back_copy().wait_recv()

            def some(i):
                r = tile(i, block)
                acc_buf[r, :] += back_buf[l, r, :].astype(F32)

            loop(rows_all // block, some)

        get_hidden(l, 0).wait()
        norm_back(0, l)

        @pl.when(me.role == 1)
        def _():
            back_copy().wait_send()

    loop(layers, layer)
    lower(low_buf, g_buf)
    done = pltpu.make_async_copy(low_buf, frames_grad_ref, out_sem)
    done.start()

    per = 128 * devices // width
    for group in range(width // 128):
        tab_role[group] = tab_sum[:, group * 128 : group * 128 + 128]

    def tab_copy(by):
        to = lax.rem(me.dp + by, devices)
        return remote(tab_role.at[lax.div(to, per)], tab_in.at[me.dp], ts.at[by - 1], tr.at[by - 1], me.around(by))

    def tab_wait(by):
        here = tab_in.at[lax.rem(me.dp - by + devices, devices)]
        remote(here, here, ts.at[by - 1], tr.at[by - 1], me.around(by)).wait_recv()

    loop(devices - 1, lambda i: tab_copy(i + 1).start())
    tab_in[me.dp] = tab_role[lax.div(me.dp, per)]
    last = layers * per_layer - 1
    send_stage(last).wait()
    loop(4, lambda i: reduce.step(2 * last + i))
    loop(devices - 1, lambda i: tab_wait(i + 1))
    loop(devices - 1, lambda i: tab_copy(i + 1).wait_send())
    total = tab_in[0]
    for i in range(1, devices):
        total = total + tab_in[i]
    tab_back[0] = total
    swap = remote(tab_back.at[0], tab_back.at[1], rs_sem, rr_sem, me.other_role())
    swap.start()
    loop(reduce.lag - 2, lambda i: reduce.step(2 * last + 4 + i))
    swap.wait()
    table_out_ref[...] = tab_back[0] + tab_back[1]
    reduce.finish()
    done.wait()


def backward(full, saved, hidden, probs, cotangent, table, pick, used, outers, layers, shard, collective_id):
    count = full.shape[0]
    rows_all, width = cotangent.shape
    keys = probs.shape[2]
    small = table.shape[0]
    dma = pltpu.SemaphoreType.DMA
    devices = 4 * outers
    split = width // 8
    any_space = pl.BlockSpec(memory_space=pl.ANY)
    vmem = pl.BlockSpec(memory_space=pltpu.VMEM)
    grid_rows = (rows_all, width)
    return pl.pallas_call(
        functools.partial(backward_kernel, layers, outers, split),
        out_shape=(
            jax.ShapeDtypeStruct((count, outers, 2, 2, shard, width), BF16),
            jax.ShapeDtypeStruct((count, shard, width), F32),
            jax.ShapeDtypeStruct(grid_rows, BF16),
            jax.ShapeDtypeStruct((small, 128), F32),
        ),
        in_specs=[any_space, any_space, any_space, any_space, vmem, vmem, vmem, vmem],
        out_specs=(any_space, any_space, any_space, vmem),
        scratch_shapes=[
            pltpu.VMEM(grid_rows, F32),
            pltpu.VMEM(grid_rows, F32),
            pltpu.VMEM(grid_rows, F32),
            pltpu.VMEM((2, width, width), BF16),
            pltpu.VMEM(grid_rows, BF16),
            pltpu.VMEM((10,) + grid_rows, BF16),
            pltpu.VMEM((2,) + grid_rows, BF16),
            pltpu.VMEM((layers,) + grid_rows, BF16),
            pltpu.VMEM((2, keys, keys), BF16),
            pltpu.VMEM((2, outers, 2, 2, shard, width), BF16),
            pltpu.VMEM((small, width), F32),
            pltpu.VMEM((devices, small, 128), F32),
            pltpu.VMEM((width // 128, small, 128), F32),
            pltpu.VMEM((2, small, 128), F32),
            dma((10,)), dma(()), dma((2,)), dma((2,)), dma((2,)), dma((layers,)), dma((layers,)),
            dma((devices - 1,)), dma((devices - 1,)), dma(()), dma(()), dma(()),
        ]
        + Reduce.scratch(outers, shard, width, split),
        compiler_params=pltpu.CompilerParams(
            collective_id=collective_id, has_side_effects=True, vmem_limit_bytes=60 * 2**20
        ),
        name="backward_and_reduce",
    )(full, saved, hidden, probs, cotangent, table, pick, used)


def prepare(
    inner_weight, outer_weight, expand_weight, shrink_weight, causal_gain, causal_shift,
    section_scale, section_shift, prompt_lengths, target_lengths, sections, rows,
):
    is_target = lax.axis_index("role") == 1
    layers, shard, _ = inner_weight.shape
    width = outer_weight.shape[2]
    devices = width // shard
    pieces = expand_weight.shape[2] // width
    segs = section_scale.shape[0]
    micro = prompt_lengths.shape[0]
    outer = outer_weight[:, None]
    inner = inner_weight.reshape(layers, shard, 3, width).transpose(0, 2, 1, 3)
    expand = expand_weight.reshape(layers, shard, devices, pieces, shard).transpose(0, 3, 1, 2, 4)
    expand = expand.reshape(layers, pieces, 1, shard, width)
    shrink = shrink_weight.reshape(layers, pieces, 1, shard, width)
    feed = jnp.concatenate([expand, shrink], axis=2).reshape(layers, 2 * pieces, shard, width)
    parts = jnp.concatenate([inner, outer, feed], axis=1).reshape(-1, shard, width)

    small = jnp.concatenate(
        [causal_gain, causal_shift, section_scale.reshape(2 * segs, -1), section_shift.reshape(2 * segs, -1)], axis=0
    )
    per = 128 // shard
    spot = (lax.axis_index("dp") % per) * shard
    piece = lax.dynamic_update_slice(jnp.zeros((small.shape[0], 128), BF16), small, (0, spot))

    masks = [[], []]
    section_frames = []
    for m in range(micro):
        prompt_row, target_row, section_row = prompt_lengths[m, 0], target_lengths[m, 0], sections[m, 0]
        prompt_segment, prompt_position, prompt_member = frame_tags(prompt_row, jnp.zeros_like(prompt_row), rows)
        target_segment, target_position, target_member = frame_tags(target_row, prompt_row, rows)
        own_segment = jnp.where(is_target, target_segment, prompt_segment)
        own_position = jnp.where(is_target, target_position, prompt_position)
        own_member = jnp.where(is_target, target_member, prompt_member)
        same_far = (own_segment[None, :] == prompt_segment[:, None]) & is_target
        same_own = own_segment[None, :] == own_segment[:, None]
        causal_own = same_own & (own_position[:, None] <= own_position[None, :])
        masks[0].append(jnp.concatenate([same_far, causal_own], axis=0))
        masks[1].append(jnp.concatenate([same_far, same_own], axis=0))
        section_frames.append(jnp.sum(jnp.where(own_member, section_row[None, :], 0), axis=1))
    bias = jnp.where(jnp.stack([jnp.stack(one) for one in masks]), 0.0, -1e30).astype(BF16)
    section = jnp.concatenate(section_frames)
    none = jnp.zeros_like(section)
    first, second = 4 + 2 * section, 4 + 2 * segs + 2 * section
    used = jnp.stack([none, none + 2, none + 1, none + 3, first, second, first + 1, second + 1])
    return parts, piece, used, bias


def body(
    frames, cotangent, inner_weight, outer_weight, expand_weight, shrink_weight, causal_gain, causal_shift,
    section_scale, section_shift, prompt_lengths, target_lengths, sections,
):
    _, micro, rows, width = frames.shape
    layers, shard, _ = inner_weight.shape
    devices = width // shard
    outers = devices // 4
    pieces = expand_weight.shape[2] // width
    segs = section_scale.shape[0]
    parts, piece, used, bias = prepare(
        inner_weight, outer_weight, expand_weight, shrink_weight, causal_gain, causal_shift,
        section_scale, section_shift, prompt_lengths, target_lengths, sections, rows,
    )
    entries = jnp.arange(piece.shape[0], dtype=jnp.int32)
    pick = (used[:, :, None] == entries[None, None, :]).astype(BF16)
    pick_t = (used[:, None, :] == entries[None, :, None]).astype(BF16)
    full, saved, hidden, probs, mixed, table = forward(
        parts, frames.reshape(micro * rows, width), piece, pick, bias, outers, layers, 0
    )
    _, owned, frames_grad, small = backward(
        full.reshape(-1, width, width), saved, hidden, probs, cotangent.reshape(micro * rows, width),
        table, pick, pick_t, outers, layers, shard, 1,
    )
    owned = owned.reshape(layers, -1, shard, width)[::-1]
    feed = owned[:, : 2 * pieces].reshape(layers, pieces, 2, shard, width)
    inner_grad = jnp.concatenate([owned[:, 2 * pieces + i] for i in (3, 1, 2)], axis=2)
    outer_grad = owned[:, 2 * pieces]
    expand_grad = feed[:, :, 1].reshape(layers, pieces, shard, devices, shard).transpose(0, 2, 3, 1, 4).reshape(layers, shard, -1)
    shrink_grad = feed[:, :, 0].reshape(layers, pieces * shard, width)
    per = 128 // shard
    spot = (lax.axis_index("dp") % per) * shard
    small = lax.dynamic_slice(small, (0, spot), (small.shape[0], shard))
    return (
        mixed.reshape(1, micro, rows, width), frames_grad.reshape(1, micro, rows, width),
        inner_grad, outer_grad, expand_grad, shrink_grad,
        small[0:2], small[2:4],
        small[4 : 4 + 2 * segs].reshape(segs, 2, shard),
        small[4 + 2 * segs :].reshape(segs, 2, shard),
    )


def solution(mesh):
    rows = P("role", None, "dp", None)
    second = P(None, "dp", None)
    placed = (rows, rows, second, second, second, second, P(None, "dp"), P(None, "dp"), P(None, None, "dp"), P(None, None, "dp"), second, second, second)
    given = (rows, rows, second, second, second, second, P(None, "dp"), P(None, "dp"), P(None, None, "dp"), P(None, None, "dp"))
    return jax.shard_map(body, mesh=mesh, in_specs=placed, out_specs=given, check_vma=False)
```

```python
import functools

import jax
import jax.numpy as jnp
from jax import lax
from jax.experimental import pallas as pl
from jax.experimental.pallas import tpu as pltpu
from jax.sharding import PartitionSpec as P

HEADS = 16
HD = 64
MESH = pl.DeviceIdType.MESH
SLOTS = 4
F32 = jnp.float32
BF16 = jnp.bfloat16


class Place:
    def __init__(self, outer_count):
        self.outers = outer_count
        self.role = lax.axis_index("role")
        dp = lax.axis_index("dp")
        self.core = lax.rem(dp, 2)
        self.pair = lax.rem(lax.div(dp, 2), 2)
        self.outer = lax.div(dp, 4)
        self.dp = dp

    def at(self, role, outer, pair, core):
        return (role, (outer * 2 + pair) * 2 + core)

    def sibling(self):
        return self.at(self.role, self.outer, self.pair, 1 - self.core)

    def across(self):
        return self.at(self.role, self.outer, 1 - self.pair, self.core)

    def other_role(self):
        return self.at(1 - self.role, self.outer, self.pair, self.core)

    def along(self, by):
        return self.at(self.role, lax.rem(self.outer + by, self.outers), self.pair, self.core)

    def around(self, by):
        return (self.role, lax.rem(self.dp + by, 4 * self.outers))

    def greet(self):
        barrier = pltpu.get_barrier_semaphore()
        pl.semaphore_signal(barrier, inc=1, device_id=self.other_role(), device_id_type=MESH)

        def greet_one(i, carry):
            pl.semaphore_signal(barrier, inc=1, device_id=self.around(i + 1), device_id_type=MESH)
            return carry

        lax.fori_loop(0, 4 * self.outers - 1, greet_one, 0)
        pl.semaphore_wait(barrier, 4 * self.outers)


def remote(src, dst, send, recv, peer):
    return pltpu.make_async_remote_copy(
        src_ref=src, dst_ref=dst, send_sem=send, recv_sem=recv, device_id=peer, device_id_type=MESH
    )


def frame_tags(lengths, offsets, total_rows):
    places = jnp.arange(total_rows, dtype=jnp.int32)
    segs = lengths.shape[0]
    upto = jnp.arange(segs)[:, None] >= jnp.arange(segs)[None, :]
    finish = jnp.sum(jnp.where(upto, lengths[None, :], 0), axis=1)
    segment = jnp.sum((places[:, None] >= finish[None, :]).astype(jnp.int32), axis=1)
    member = segment[:, None] == jnp.arange(segs, dtype=jnp.int32)[None, :]
    shifted = offsets - (finish - lengths)
    position = places + jnp.sum(jnp.where(member, shifted[None, :], 0), axis=1)
    return (segment, position, member)


def dot(a, b):
    return jnp.dot(a, b, preferred_element_type=F32)


def dot_t(a, b):
    return lax.dot_general(a, b, (((1,), (1,)), ((), ())), preferred_element_type=F32)


def t_dot(a, b):
    return lax.dot_general(a, b, (((0,), (0,)), ((), ())), preferred_element_type=F32)


def normalize(hidden):
    average = jnp.mean(hidden, axis=-1, keepdims=True)
    centred = hidden - average
    spread = jnp.mean(centred * centred, axis=-1, keepdims=True)
    inverse = lax.rsqrt(spread + 1e-05)
    return centred * inverse, inverse


def norm_backward(grad, scale, unit, inverse):
    inner = grad * scale
    return inverse * (
        inner - jnp.mean(inner, axis=-1, keepdims=True) - unit * jnp.mean(inner * unit, axis=-1, keepdims=True)
    )


def gelu_parts(upper):
    cumulative = 0.5 * (1.0 + lax.erf(upper * 0.7071067811865476))
    density = jnp.exp(-0.5 * upper * upper) * 0.3989422804014327
    return upper * cumulative, cumulative + upper * density


class Gather:
    lag = 7

    def __init__(self, me, part_ref, full_ref, split, sems):
        self.me, self.part, self.full, self.split = me, part_ref, full_ref, split
        self.own_sem, self.zs, self.zr, self.xs, self.xr, self.us, self.ur, self.vs, self.vr, self.cs, self.cr = sems
        self.half = part_ref.shape[-1] // 2
        self.main = self.half - split
        self.steps = 2 * part_ref.shape[0]

    @staticmethod
    def semaphores(many):
        dma = pltpu.SemaphoreType.DMA
        return [
            dma((8,)),
            dma((8, many)), dma((8, many)),
            dma((8,)), dma((8,)),
            dma((12, many)), dma((12, many)),
            dma((8,)), dma((8,)),
            dma((8,)), dma((8,)),
        ]

    def cols(self, h, offset, size):
        return pl.ds(pl.multiple_of(lax.rem(h, 2) * self.half + offset, 128), size)

    def main_cols(self, h):
        return self.cols(h, self.me.role * self.split, self.main)

    def give_cols(self, h):
        return self.cols(h, self.me.role * self.main, self.split)

    def take_cols(self, h):
        return self.cols(h, (1 - self.me.role) * self.main, self.split)

    def before(self, by):
        return lax.rem(self.me.outer - by + self.me.outers, self.me.outers)

    def own(self, h):
        me, cols = self.me, self.cols(h, 0, self.half)
        return pltpu.make_async_copy(
            self.part.at[lax.div(h, 2), :, cols], self.full.at[lax.div(h, 2), me.outer, me.pair, me.core, :, cols], self.own_sem.at[lax.rem(h, 8)]
        )

    def z_copy(self, h, by):
        me, cols, s = self.me, self.main_cols(h), lax.rem(h, 8)
        return remote(
            self.part.at[lax.div(h, 2), :, cols],
            self.full.at[lax.div(h, 2), me.outer, me.pair, me.core, :, cols],
            self.zs.at[s, by - 1], self.zr.at[s, by - 1], me.along(by),
        )

    def z_wait(self, h, by):
        me, s = self.me, lax.rem(h, 8)
        dst = self.full.at[lax.div(h, 2), self.before(by), me.pair, me.core, :, self.main_cols(h)]
        remote(dst, dst, self.zs.at[s, by - 1], self.zr.at[s, by - 1], me.along(by)).wait_recv()

    def x_copy(self, h, pair):
        me, s = self.me, lax.rem(h, 8)
        ref = self.full.at[lax.div(h, 2), :, pair, me.core, :, self.main_cols(h)]
        return remote(ref, ref, self.xs.at[s], self.xr.at[s], me.across())

    def u_copy(self, h, by, cols):
        me, s = self.me, lax.rem(h, 12)
        ref = self.full.at[lax.div(h, 2), self.before(by), me.pair, me.core, :, cols]
        return remote(ref, ref, self.us.at[s, by - 1], self.ur.at[s, by - 1], me.other_role())

    def v_copy(self, h, cols):
        me, s = self.me, lax.rem(h, 8)
        ref = self.full.at[lax.div(h, 2), :, 1 - me.pair, me.core, :, cols]
        return remote(ref, ref, self.vs.at[s], self.vr.at[s], me.other_role())

    def c_copy(self, h, core):
        s = lax.rem(h, 8)
        ref = self.full.at[lax.div(h, 2), :, :, core, :, self.cols(h, 0, self.half)]
        return remote(ref, ref, self.cs.at[s], self.cr.at[s], self.me.sibling())

    def step(self, t):
        me, count = self.me, self.steps
        others = range(1, me.outers)

        @pl.when(t < count)
        def _():
            self.own(t).start()
            for by in others:
                self.z_copy(t, by).start()

        @pl.when((t >= 2) & (t < count + 2))
        def _():
            h = t - 2
            self.own(h).wait()
            for by in others:
                self.z_wait(h, by)
            self.x_copy(h, me.pair).start()
            for by in others:
                self.u_copy(h, by, self.give_cols(h)).start()

        @pl.when((t >= 4) & (t < count + 4))
        def _():
            h = t - 4
            self.x_copy(h, 1 - me.pair).wait_recv()
            self.v_copy(h, self.give_cols(h)).start()
            for by in others:
                self.z_copy(h, by).wait_send()

        @pl.when((t >= 6) & (t < count + 6))
        def _():
            h = t - 6
            for by in others:
                self.u_copy(h, by, self.take_cols(h)).wait_recv()
            self.v_copy(h, self.take_cols(h)).wait_recv()
            self.c_copy(h, me.core).start()
            for by in others:
                self.u_copy(h, by, self.give_cols(h)).wait_send()
            self.x_copy(h, me.pair).wait_send()
            self.v_copy(h, self.give_cols(h)).wait_send()

        @pl.when((t >= 7) & (t < count + 7))
        def _():
            h = t - 7
            self.c_copy(h, 1 - me.core).wait_recv()
            self.c_copy(h, me.core).wait_send()


def loop(count, action):
    def one(i, carry):
        action(i)
        return carry

    lax.fori_loop(0, count, one, 0)


def tile(i, size):
    return pl.ds(pl.multiple_of(i * size, size), size)


WIDE = 1024


def forward_kernel(
    layers, outers, split,
    inner_ref, outer_ref, expand_ref, shrink_ref, frames_ref, piece_ref, pick_ref, bias_ref,
    full_ref, saved_ref, hidden_ref, probs_ref, mixed_ref, table_ref,
    part_buf, e_buf, tab_in, h_buf, a_buf, qkv_buf, far_in, far_buf, mix_buf, f_buf, lift_buf, slope_buf, w_buf, p_buf,
    pack_sem, ts, tr, w_sem, save_sem, h_sem, p_sem, out_sem, ks, kr, *gather_sems,
):
    me = Place(outers)
    devices = 4 * outers
    rows_all, width = frames_ref.shape
    count, shard, _ = part_buf.shape
    per_layer = count // layers
    pieces = (per_layer - 4) // 2
    micro = bias_ref.shape[1]
    rows = rows_all // micro
    pairs = width // 128
    gather = Gather(me, part_buf, full_ref, split, gather_sems)
    early, late = [], []
    for l in range(layers):
        base = l * per_layer
        sources = [(i, inner_ref.at[l, :, pl.ds(i * width, width)]) for i in range(3)] + [(3, outer_ref.at[l])]
        sources += [(5 + 2 * j, shrink_ref.at[l, pl.ds(j * shard, shard)]) for j in range(pieces)]
        for k, source in sources:
            copy = pltpu.make_async_copy(source, part_buf.at[base + k], pack_sem.at[base + k])
            (early if base + k < 4 else late).append(copy)
        late.append(pltpu.make_async_copy(expand_ref.at[l], e_buf.at[l], pack_sem.at[count + l]))
    for copy in early + late:
        copy.start()
    me.greet()

    def piece_copy(by):
        return remote(piece_ref, tab_in.at[me.dp], ts.at[by - 1], tr.at[by - 1], me.around(by))

    def piece_wait(by):
        here = tab_in.at[(me.dp - by + devices) % devices]
        remote(here, here, ts.at[by - 1], tr.at[by - 1], me.around(by)).wait_recv()

    loop(devices - 1, lambda i: piece_copy(i + 1).start())
    tab_in[me.dp] = piece_ref[...]

    @pl.when(me.role == 0)
    def _():
        far_buf[...] = jnp.zeros_like(far_buf)
        far_in[...] = jnp.zeros_like(far_in)

    ahead = gather.lag - 4
    for copy in early:
        copy.wait()
    loop(2, gather.step)
    for copy in late:
        copy.wait()

    def spread(index):
        l, t = lax.div(index, width // 128), lax.rem(index, width // 128)
        first = lax.broadcasted_iota(jnp.int32, (shard, 128), 1) < 64
        for j in range(pieces):
            to = part_buf.at[l * per_layer + 4 + 2 * j, :, tile(t, 128)]
            if shard == 64:
                even = e_buf[l, :, tile(t * pieces + j // 2, 128)].astype(F32)
                odd = e_buf[l, :, tile(t * pieces + pieces // 2 + j // 2, 128)].astype(F32)
                if j % 2 == 0:
                    odd = pltpu.roll(odd, 64, 1)
                else:
                    even = pltpu.roll(even, 64, 1)
                to[...] = jnp.where(first, even, odd).astype(BF16)
            else:
                to[...] = e_buf[l, :, tile(j * (width // 128) + t, 128)]

    loop(layers * width // 128, spread)
    loop(devices - 1, lambda i: piece_wait(i + 1))
    loop(devices - 1, lambda i: piece_copy(i + 1).wait_send())
    per = 128 * devices // width
    for group in range(width // 128):
        total = tab_in[group * per]
        for i in range(1, per):
            total = total + tab_in[group * per + i]
        table_ref[:, group * 128 : group * 128 + 128] = total

    def load_rows(i):
        r = tile(i, 64)
        h_buf[0, r, :] = frames_ref[r, :].astype(F32)

    loop(rows_all // 64, load_rows)

    def load(k):
        return pltpu.make_async_copy(full_ref.at[k], w_buf.at[lax.rem(k, 2)], w_sem.at[lax.rem(k, 2)])

    def matmul(in_ref, k, finish):
        load(k).wait()

        def columns(n):
            cols = tile(n, WIDE)
            w = w_buf[lax.rem(k, 2), :, :, :, :, cols].reshape(width, WIDE)
            finish(cols, dot(in_ref[...], w))

        loop(width // WIDE, columns)

    def norm(index, src, dst_ref, l):
        def some(i):
            r = tile(i, 64)
            unit, _ = normalize(h_buf[src, r, :])
            scale = dot(pick_ref[l * 4 + 2 * index, r, :], table_ref[...])
            shift = dot(pick_ref[l * 4 + 2 * index + 1, r, :], table_ref[...])
            dst_ref[r, :] = (scale * unit + shift).astype(BF16)

        loop(rows_all // 64, some)

    def save_at(l, ref, slot):
        return pltpu.make_async_copy(ref, saved_ref.at[l, slot], save_sem.at[slot])

    def save_hidden_at(l, which):
        return pltpu.make_async_copy(h_buf.at[which], hidden_ref.at[l, which], h_sem.at[which])

    def far_copy(l):
        return remote(a_buf, far_in.at[l], ks.at[l], kr.at[l], me.other_role())

    def begin(l):
        save_hidden_at(l, 0).start()
        norm(0, 0, a_buf, l)
        save_at(l, a_buf, 0).start()

        @pl.when(me.role == 0)
        def _():
            far_copy(l).start()

    begin(0)
    loop(gather.lag, lambda i: gather.step(i + 2))

    def layer(l):
        base = l * per_layer

        def save(ref, slot):
            return save_at(l, ref, slot)

        def save_hidden(which):
            return save_hidden_at(l, which)

        load(base).start()

        def project(i):
            def keep(cols, value):
                qkv_buf[i, :, cols] = value.astype(BF16)

            matmul(a_buf, base + i, keep)
            gather.step(2 * (base + i) + 6 + ahead)
            gather.step(2 * (base + i) + 7 + ahead)

            @pl.when(i < 2)
            def _():
                load(base + i + 1).start()

            save(qkv_buf.at[i], 1 + i).start()

        loop(3, project)

        @pl.when(me.role == 1)
        def _():
            load(base + 1).start()
            load(base + 2).start()
            far_copy(l).wait_recv()

            def project_far(i):
                def keep(cols, value):
                    far_buf[i, :, cols] = value.astype(BF16)

                matmul(far_in.at[l], base + 1 + i, keep)

            loop(2, project_far)

        load(base + 3).start()
        save(far_in.at[l], 8 + 2 * pieces).start()
        save(far_buf.at[0], 4).start()
        save(far_buf.at[1], 5).start()

        def save_probs(it):
            return pltpu.make_async_copy(p_buf.at[lax.rem(it, 2)], probs_ref.at[l, it], p_sem.at[lax.rem(it, 2)])

        def attend(it):
            m, p = lax.div(it, pairs), lax.rem(it, pairs)
            r, cols = tile(m, rows), tile(p, 128)
            first = lax.broadcasted_iota(jnp.int32, (rows, 128), 1) < HD
            q = qkv_buf[0, r, cols].astype(F32) * HD**-0.5
            both = jnp.concatenate([jnp.where(first, q, 0.0).astype(BF16), jnp.where(first, 0.0, q).astype(BF16)], axis=0)
            keys = jnp.concatenate([far_buf[0, r, cols], qkv_buf[1, r, cols]], axis=0)
            values = jnp.concatenate([far_buf[1, r, cols], qkv_buf[2, r, cols]], axis=0)
            bias = bias_ref[l, m].astype(F32)
            scores = dot_t(keys, both) + jnp.concatenate([bias, bias], axis=1)
            exponent = jnp.exp(scores - jnp.max(scores, axis=0, keepdims=True))
            soft = (exponent * (1.0 / jnp.sum(exponent, axis=0, keepdims=True))).astype(BF16)

            @pl.when(it >= 2)
            def _():
                save_probs(it - 2).wait()

            p_buf[lax.rem(it, 2)] = soft
            save_probs(it).start()
            out = t_dot(values, soft)
            out = jnp.concatenate([out[:HD, :rows], out[HD:, rows:]], axis=0)
            mix_buf[r, cols] = out.T.astype(BF16)

        segment = micro * pairs // 4

        def attend_some(s):
            loop(segment, lambda i: attend(s * segment + i))
            gather.step(2 * base + 12 + s + ahead)

        loop(4, attend_some)
        save_probs(micro * pairs - 2).wait()
        save_probs(micro * pairs - 1).wait()
        save(mix_buf, 6).start()
        load(base + 4).start()
        gather.step(2 * base + 16 + ahead)

        def keep_middle(cols, value):
            h_buf[1, :, cols] = h_buf[0, :, cols] + value

        matmul(mix_buf, base + 3, keep_middle)
        save_hidden(1).start()
        save_hidden(0).wait()
        gather.step(2 * base + 17 + ahead)
        norm(1, 1, f_buf, l)
        save(f_buf, 7).start()
        h_buf[0] = h_buf[1]

        def feed(j):
            gather.step(2 * base + 18 + 3 * j + ahead)
            load(base + 5 + 2 * j).start()

            def raise_columns(cols, value):
                up, slope = gelu_parts(value)
                lift_buf[:, cols] = up.astype(BF16)
                slope_buf[:, cols] = slope.astype(BF16)

            matmul(f_buf, base + 4 + 2 * j, raise_columns)
            lift_save = pltpu.make_async_copy(lift_buf, saved_ref.at[l, 8 + j], save_sem.at[9 + 2 * pieces])
            slope_save = pltpu.make_async_copy(slope_buf, saved_ref.at[l, 8 + pieces + j], save_sem.at[8])
            lift_save.start()
            slope_save.start()
            gather.step(2 * base + 19 + 3 * j + ahead)

            @pl.when(j < pieces - 1)
            def _():
                load(base + 6 + 2 * j).start()

            def add(cols, value):
                h_buf[0, :, cols] += value

            matmul(lift_buf, base + 5 + 2 * j, add)
            gather.step(2 * base + 20 + 3 * j + ahead)
            lift_save.wait()
            slope_save.wait()

        loop(pieces, feed)
        save_hidden(1).wait()
        save(a_buf, 0).wait()
        for i in range(3):
            save(qkv_buf.at[i], 1 + i).wait()
        save(far_buf.at[0], 4).wait()
        save(far_buf.at[1], 5).wait()
        save(mix_buf, 6).wait()
        save(f_buf, 7).wait()
        save(far_in.at[l], 8 + 2 * pieces).wait()

        @pl.when(me.role == 0)
        def _():
            far_copy(l).wait_send()

        @pl.when(l < layers - 1)
        def _():
            begin(l + 1)

    loop(layers, layer)

    def store_rows(i):
        r = tile(i, 64)
        a_buf[r, :] = h_buf[0, r, :].astype(BF16)

    loop(rows_all // 64, store_rows)
    done = pltpu.make_async_copy(a_buf, mixed_ref, out_sem)
    done.start()
    done.wait()


def forward(inner, outer, expand, shrink, frames, piece, pick, bias, outers, collective_id):
    layers, shard, width = outer.shape
    rows_all = frames.shape[0]
    pieces = expand.shape[2] // width
    count = layers * (4 + 2 * pieces)
    many = outers - 1
    dma = pltpu.SemaphoreType.DMA
    devices = 4 * outers
    split = width // 8
    micro = bias.shape[1]
    keys, rows = bias.shape[2:]
    pairs = width // 128
    any_space = pl.BlockSpec(memory_space=pl.ANY)
    vmem = pl.BlockSpec(memory_space=pltpu.VMEM)
    grid_rows = (rows_all, width)
    return pl.pallas_call(
        functools.partial(forward_kernel, layers, outers, split),
        out_shape=(
            jax.ShapeDtypeStruct((count, outers, 2, 2, shard, width), BF16),
            jax.ShapeDtypeStruct((layers, 9 + 2 * pieces) + grid_rows, BF16),
            jax.ShapeDtypeStruct((layers, 2) + grid_rows, F32),
            jax.ShapeDtypeStruct((layers, micro * pairs, keys, 2 * rows), BF16),
            jax.ShapeDtypeStruct(grid_rows, BF16),
            jax.ShapeDtypeStruct((piece.shape[0], width), BF16),
        ),
        in_specs=[any_space, any_space, any_space, any_space, vmem, vmem, vmem, vmem],
        out_specs=(any_space, any_space, any_space, any_space, any_space, vmem),
        scratch_shapes=[
            pltpu.VMEM((count, shard, width), BF16),
            pltpu.VMEM(expand.shape, BF16),
            pltpu.VMEM((devices,) + piece.shape, BF16),
            pltpu.VMEM((2,) + grid_rows, F32),
            pltpu.VMEM(grid_rows, BF16),
            pltpu.VMEM((3,) + grid_rows, BF16),
            pltpu.VMEM((layers,) + grid_rows, BF16),
            pltpu.VMEM((2,) + grid_rows, BF16),
            pltpu.VMEM(grid_rows, BF16),
            pltpu.VMEM(grid_rows, BF16),
            pltpu.VMEM(grid_rows, BF16),
            pltpu.VMEM(grid_rows, BF16),
            pltpu.VMEM((2, outers, 2, 2, shard, width), BF16),
            pltpu.VMEM((2, keys, 2 * rows), BF16),
            dma((count + layers,)), dma((devices - 1,)), dma((devices - 1,)),
            dma((2,)), dma((10 + 2 * pieces,)), dma((2,)), dma((2,)), dma(()), dma((layers,)), dma((layers,)),
        ]
        + Gather.semaphores(many),
        compiler_params=pltpu.CompilerParams(
            collective_id=collective_id, has_side_effects=True, vmem_limit_bytes=58 * 2**20
        ),
        name="gather_and_forward",
    )(inner, outer, expand, shrink, frames, piece, pick, bias)


class Reduce:
    lag = 8

    def __init__(self, me, layers, grad_ref, out_refs, split, refs):
        self.me, self.grad, self.split = me, grad_ref, split
        self.inner, self.outer, self.expand, self.shrink = out_refs
        (
            self.own_buf, self.core_buf, self.role_buf, self.pair_buf, self.outer_buf, self.last_buf, self.sum_buf, self.low_buf,
            self.end_buf, self.fin_buf, self.spread_buf,
            self.own_sem, self.cs, self.cr, self.ys, self.yr, self.xs, self.xr, self.zs, self.zr, self.es, self.er, self.fs,
            self.ps,
        ) = refs
        self.half = grad_ref.shape[-1] // 2
        self.main = self.half - split
        self.steps = 2 * grad_ref.shape[0]
        self.layers = layers
        self.per_layer = grad_ref.shape[0] // layers
        self.pieces = (self.per_layer - 4) // 2

    @staticmethod
    def scratch(layers, outers, rows, width, pieces, split):
        dma = pltpu.SemaphoreType.DMA
        many = outers - 1
        half = width // 2
        main = half - split
        return [
            pltpu.VMEM((2, outers, 2, rows, half), BF16),
            pltpu.VMEM((4, outers, 2, rows, half), BF16),
            pltpu.VMEM((6, outers, 2, rows, split), BF16),
            pltpu.VMEM((6, outers, rows, main), BF16),
            pltpu.VMEM((6, many, rows, main), BF16),
            pltpu.VMEM((4, rows, main), BF16),
            pltpu.VMEM((6, outers, 2, rows, half), BF16),
            pltpu.VMEM((4, outers, rows, main), BF16),
            pltpu.VMEM((4, rows, main), BF16),
            pltpu.VMEM((4, rows, half), F32),
            pltpu.VMEM((layers, rows, pieces * width), F32),
            dma((2,)),
            dma((4,)), dma((4,)),
            dma((6,)), dma((6,)),
            dma((6,)), dma((6,)),
            dma((6, many)), dma((6, many)),
            dma((4,)), dma((4,)),
            dma((4,)), dma((layers,)),
        ]

    def cols(self, offset, size):
        return pl.ds(pl.multiple_of(offset, 128), size)

    def main_cols(self):
        return self.cols(self.me.role * self.split, self.main)

    def keep_cols(self):
        return self.cols(self.me.role * self.main, self.split)

    def give_cols(self):
        return self.cols((1 - self.me.role) * self.main, self.split)

    def part(self, k, core):
        return self.grad.at[lax.div(k, 2), :, :, core, :, self.cols(lax.rem(k, 2) * self.half, self.half)]

    def own(self, k):
        s = lax.rem(k, 2)
        return pltpu.make_async_copy(self.part(k, self.me.core), self.own_buf.at[s], self.own_sem.at[s])

    def c_copy(self, k):
        s = lax.rem(k, 4)
        return remote(self.part(k, 1 - self.me.core), self.core_buf.at[s], self.cs.at[s], self.cr.at[s], self.me.sibling())

    def y_copy(self, k):
        s = lax.rem(k, 6)
        return remote(
            self.sum_buf.at[s, :, :, :, self.give_cols()], self.role_buf.at[s], self.ys.at[s], self.yr.at[s], self.me.other_role()
        )

    def x_copy(self, k):
        s = lax.rem(k, 6)
        return remote(
            self.sum_buf.at[s, :, 1 - self.me.pair, :, self.main_cols()],
            self.pair_buf.at[s], self.xs.at[s], self.xr.at[s], self.me.across(),
        )

    def z_copy(self, k, by):
        s = lax.rem(k, 6)
        me = self.me
        return remote(
            self.low_buf.at[lax.rem(k, 4), lax.rem(me.outer + by, me.outers)], self.outer_buf.at[s, by - 1],
            self.zs.at[s, by - 1], self.zr.at[s, by - 1], me.along(by),
        )

    def e_copy(self, k):
        s = lax.rem(k, 4)
        return remote(self.end_buf.at[s], self.last_buf.at[s], self.es.at[s], self.er.at[s], self.me.other_role())

    def kind(self, k):
        n = lax.div(k, 2)
        return self.layers - 1 - lax.div(n, self.per_layer), lax.rem(n, self.per_layer)

    def is_expand(self, k):
        _, q = self.kind(k)
        return (q < 2 * self.pieces) & (lax.rem(q, 2) == 1)

    def store(self, k):
        s, half = lax.rem(k, 4), lax.rem(k, 2)
        layer, q = self.kind(k)
        width, pieces = 2 * self.half, self.pieces
        rows = self.fin_buf.shape[1]
        cols = self.cols(half * self.half, self.half)
        piece = lax.div(q, 2)

        def put(dst):
            pltpu.make_async_copy(self.fin_buf.at[s], dst, self.fs.at[s]).start()

        @pl.when((q < 2 * pieces) & (lax.rem(q, 2) == 0))
        def _():
            put(self.shrink.at[layer, pl.ds(pl.multiple_of(piece * rows, rows), rows), cols])

        @pl.when(q == 2 * pieces)
        def _():
            put(self.outer.at[layer, :, cols])

        @pl.when(q > 2 * pieces)
        def _():
            put(self.inner.at[layer, :, self.cols(lax.rem(q - 2 * pieces, 3) * width + half * self.half, self.half)])

        @pl.when(self.is_expand(k))
        def _():
            self.spread(layer, piece, half, s)

            @pl.when((piece == pieces - 1) & (half == 1))
            def _():
                self.spread_copy(layer).start()

    def spread_copy(self, layer):
        return pltpu.make_async_copy(self.spread_buf.at[layer], self.expand.at[layer], self.ps.at[layer])

    def spread(self, layer, piece, half, s):
        rows, pieces = self.fin_buf.shape[1], self.pieces
        tiles = self.half // 128
        first = lax.broadcasted_iota(jnp.int32, (rows, 128), 1) < 64

        def some(i):
            value = self.fin_buf[s, :, tile(i, 128)]
            if rows != 64:
                self.spread_buf[layer, :, tile((2 * piece + half) * tiles + i, 128)] = value
                return
            moved = pltpu.roll(value, 64, 1)
            at = (half * tiles + i) * pieces + lax.div(piece, 2)
            even, odd = tile(at, 128), tile(at + pieces // 2, 128)

            @pl.when(lax.rem(piece, 2) == 0)
            def _():
                self.spread_buf[layer, :, even] = jnp.where(first, value, self.spread_buf[layer, :, even])
                self.spread_buf[layer, :, odd] = jnp.where(first, moved, self.spread_buf[layer, :, odd])

            @pl.when(lax.rem(piece, 2) == 1)
            def _():
                self.spread_buf[layer, :, even] = jnp.where(first, self.spread_buf[layer, :, even], moved)
                self.spread_buf[layer, :, odd] = jnp.where(first, self.spread_buf[layer, :, odd], value)

        loop(tiles, some)

    def stored(self, k):
        @pl.when(jnp.logical_not(self.is_expand(k)))
        def _():
            s = lax.rem(k, 4)
            pltpu.make_async_copy(self.fin_buf.at[s], self.outer.at[0, :, pl.ds(0, self.half)], self.fs.at[s]).wait()

    def step(self, t):
        me, count, split, main = self.me, self.steps, self.split, self.main
        others = range(1, me.outers)

        @pl.when((t >= 0) & (t < count))
        def _():
            self.own(t).start()
            self.c_copy(t).start()

        @pl.when((t >= 1) & (t < count + 1))
        def _():
            k = t - 1
            self.own(k).wait()
            self.c_copy(k).wait()

            def add(i):
                o, p = lax.div(i, 2), lax.rem(i, 2)
                self.sum_buf[lax.rem(k, 6), o, p] = self.own_buf[lax.rem(k, 2), o, p] + self.core_buf[lax.rem(k, 4), o, p]

            loop(2 * me.outers, add)
            self.y_copy(k).start()

        @pl.when((t >= 3) & (t < count + 3))
        def _():
            k = t - 3
            s = lax.rem(k, 6)
            self.y_copy(k).wait()
            keep = self.keep_cols()

            def add(i):
                o, p = lax.div(i, 2), lax.rem(i, 2)
                self.sum_buf[s, o, p, :, keep] = self.sum_buf[s, o, p, :, keep] + self.role_buf[s, o, p]

            loop(2 * me.outers, add)
            self.x_copy(k).start()

        @pl.when((t >= 5) & (t < count + 5))
        def _():
            k = t - 5
            s = lax.rem(k, 6)
            self.x_copy(k).wait()
            cols = self.main_cols()

            def add(o):
                self.low_buf[lax.rem(k, 4), o] = self.sum_buf[s, o, me.pair, :, cols] + self.pair_buf[s, o]

            loop(me.outers, add)
            for by in others:
                self.z_copy(k, by).start()

        @pl.when((t >= 7) & (t < count + 7))
        def _():
            k = t - 7
            for by in others:
                self.z_copy(k, by).wait()
            total = self.low_buf[lax.rem(k, 4), me.outer].astype(F32)
            for by in others:
                total = total + self.outer_buf[lax.rem(k, 6), by - 1].astype(F32)
            self.end_buf[lax.rem(k, 4)] = total.astype(BF16)
            self.e_copy(k).start()

        @pl.when((t >= 8) & (t < count + 8))
        def _():
            k = t - 8
            s = lax.rem(k, 4)
            self.e_copy(k).wait()

            @pl.when(k >= 4)
            def _():
                self.stored(k - 4)

            mid = main - split
            mine = self.end_buf[s].astype(F32)
            theirs = self.last_buf[s].astype(F32)

            @pl.when(me.role == 0)
            def _():
                self.fin_buf[s, :, :split] = mine[:, :split]
                self.fin_buf[s, :, split:main] = mine[:, split:] + theirs[:, :mid]
                self.fin_buf[s, :, main:] = theirs[:, mid:]

            @pl.when(me.role == 1)
            def _():
                self.fin_buf[s, :, :split] = theirs[:, :split]
                self.fin_buf[s, :, split:main] = theirs[:, split:] + mine[:, :mid]
                self.fin_buf[s, :, main:] = mine[:, mid:]

            self.store(k)

    def finish(self):
        loop(4, lambda i: self.stored(self.steps - 4 + i))
        for layer in range(self.layers):
            self.spread_copy(layer).wait()


def backward_kernel(
    layers, outers, split,
    full_ref, saved_ref, hidden_ref, probs_ref, cot_ref, table_ref, pick_ref, used_ref,
    grad_ref, inner_ref, outer_ref, expand_ref, shrink_ref, frames_grad_ref, table_out_ref,
    g_buf, acc_buf, h_buf, w_buf, low_buf, act_buf, give_buf, back_buf, p_buf, stage_buf, tab_sum, tab_in, tab_role, tab_back,
    act_sem, h_sem, w_sem, p_sem, stage_sem, ks, kr, ts, tr, rs_sem, rr_sem, out_sem, *reduce_refs,
):
    me = Place(outers)
    devices = 4 * outers
    rows_all, width = cot_ref.shape
    per_layer = full_ref.shape[0] // layers
    pieces = (per_layer - 4) // 2
    pairs = width // 128
    micro = probs_ref.shape[1] // pairs
    rows = rows_all // micro
    shard = grad_ref.shape[-2]
    tile_outers = WIDE // (4 * shard)
    block = 128
    reduce = Reduce(me, layers, grad_ref, (inner_ref, outer_ref, expand_ref, shrink_ref), split, reduce_refs)
    me.greet()

    def load_rows(i):
        r = tile(i, block)
        g_buf[r, :] = cot_ref[r, :].astype(F32)

    loop(rows_all // block, load_rows)
    tab_sum[...] = jnp.zeros_like(tab_sum)

    def get(l, item, slot):
        return pltpu.make_async_copy(saved_ref.at[l, item], act_buf.at[slot], act_sem.at[slot])

    def get_hidden(l, which):
        return pltpu.make_async_copy(hidden_ref.at[l, which], h_buf, h_sem)

    def get_w(k, slot):
        return pltpu.make_async_copy(full_ref.at[k], w_buf.at[slot], w_sem.at[slot])

    def send_stage(n):
        s = lax.rem(n, 2)
        return pltpu.make_async_copy(stage_buf.at[s], grad_ref.at[n], stage_sem.at[s])

    def produce(n, left, right, far=None):
        s = lax.rem(n, 2)

        def some(i):
            cols = tile(i, WIDE)
            value = t_dot(left[:, cols], right[...])
            if far is not None:
                value = value + t_dot(far[0][:, cols], far[1][...])
            stage_buf[s, pl.ds(i * tile_outers, tile_outers)] = value.astype(BF16).reshape(tile_outers, 2, 2, shard, width)

        loop(width // WIDE, some)
        send_stage(n).start()

        @pl.when(n >= 1)
        def _():
            send_stage(n - 1).wait()

    def through(left, slot, finish):
        def some(i):
            cols = tile(i, WIDE)
            finish(cols, dot_t(left[...], w_buf[slot, cols, :]))

        loop(width // WIDE, some)

    def lower(dst, src):
        def some(i):
            r = tile(i, block)
            dst[r, :] = src[r, :].astype(BF16)

        loop(rows_all // block, some)

    def norm_back(index, l):
        def some(i):
            r = tile(i, block)
            unit, inverse = normalize(h_buf[r, :])
            scale = dot(pick_ref[l * 4 + 2 * index, r, :], table_ref[...])
            grad = acc_buf[r, :]
            g_buf[r, :] = g_buf[r, :] + norm_backward(grad, scale, unit, inverse)
            for which, values in ((0, grad * unit), (1, grad)):
                picked = used_ref[l * 4 + 2 * index + which, :, r]
                high = values.astype(BF16)
                rest = (values - high.astype(F32)).astype(BF16)
                tab_sum[...] += dot(picked, high) + dot(picked, rest)

        loop(rows_all // block, some)

    def layer(turn):
        l = layers - 1 - turn
        base = l * per_layer
        n0 = turn * per_layer

        def service(index):
            reduce.step(2 * (n0 - 1) + index)

        get(l, 7, 0).start()
        get(l, 8, 1).start()
        get(l, 8 + pieces, 3).start()
        get_w(base + 5, 0).start()
        get_hidden(l, 1).start()
        lower(low_buf, g_buf)
        acc_buf[...] = jnp.zeros_like(acc_buf)
        get(l, 7, 0).wait()

        def feed(j):
            s = lax.rem(j, 2)
            get_w(base + 4 + 2 * j, 1).start()
            get(l, 8 + j, 1 + s).wait()
            get(l, 8 + pieces + j, 3 + s).wait()

            @pl.when(j < pieces - 1)
            def _():
                get(l, 9 + j, 2 - s).start()
                get(l, 9 + pieces + j, 4 - s).start()

            produce(n0 + 2 * j, act_buf.at[1 + s], low_buf)
            service(2 * j)
            get_w(base + 5 + 2 * j, 0).wait()

            def lift(cols, value):
                act_buf[5, :, cols] = (value * act_buf[3 + s, :, cols].astype(F32)).astype(BF16)

            through(low_buf, 0, lift)

            @pl.when(j < pieces - 1)
            def _():
                get_w(base + 7 + 2 * j, 0).start()

            service(2 * j + 1)
            produce(n0 + 2 * j + 1, act_buf.at[0], act_buf.at[5])
            get_w(base + 4 + 2 * j, 1).wait()

            def add(cols, value):
                acc_buf[:, cols] += value

            through(act_buf.at[5], 1, add)

        loop(pieces, feed)
        get_w(base + 3, 0).start()
        get(l, 6, 0).start()
        for i in range(5):
            get(l, 1 + i, 1 + i).start()
        get(l, 8 + 2 * pieces, 9).start()

        def get_probs(it):
            s = lax.rem(it, 2)
            return pltpu.make_async_copy(probs_ref.at[l, it], p_buf.at[s], p_sem.at[s])

        get_probs(0).start()
        get_hidden(l, 1).wait()
        service(2 * pieces)
        norm_back(1, l)
        lower(low_buf, g_buf)
        get(l, 6, 0).wait()
        service(2 * pieces + 1)
        produce(n0 + 2 * pieces, act_buf.at[0], low_buf)
        get_w(base + 3, 0).wait()

        def keep_mixture(cols, value):
            act_buf[6, :, cols] = value.astype(BF16)

        through(low_buf, 0, keep_mixture)
        get_w(base + 1, 0).start()
        get(l, 0, 8).start()
        for i in range(5):
            get(l, 1 + i, 1 + i).wait()

        def attend(it):
            m, p = lax.div(it, pairs), lax.rem(it, pairs)
            r, cols = tile(m, rows), tile(p, 128)
            first = lax.broadcasted_iota(jnp.int32, (rows, 128), 1) < HD

            def both_of(x):
                return jnp.concatenate([jnp.where(first, x, 0.0).astype(BF16), jnp.where(first, 0.0, x).astype(BF16)], axis=0)

            queries = both_of(act_buf[1, r, cols].astype(F32) * HD**-0.5)
            out_grad = both_of(act_buf[6, r, cols].astype(F32))
            keys = jnp.concatenate([act_buf[4, r, cols], act_buf[2, r, cols]], axis=0)
            values = jnp.concatenate([act_buf[5, r, cols], act_buf[3, r, cols]], axis=0)
            get_probs(it).wait()

            @pl.when(it + 1 < micro * pairs)
            def _():
                get_probs(it + 1).start()

            soft_low = p_buf[lax.rem(it, 2)]
            soft = soft_low.astype(F32)
            grad_soft = dot_t(values, out_grad)
            inner = jnp.sum(soft * grad_soft, axis=0, keepdims=True)
            grad_scores = (soft * (grad_soft - inner)).astype(BF16)
            grad_values = dot(soft_low, out_grad)
            grad_keys = dot(grad_scores, queries)
            give_buf[0, r, cols] = grad_keys[:rows].astype(BF16)
            give_buf[1, r, cols] = grad_values[:rows].astype(BF16)
            h_buf[r, cols] = grad_keys[rows:]
            acc_buf[r, cols] = grad_values[rows:]
            out = t_dot(keys, grad_scores) * HD**-0.5
            out = jnp.concatenate([out[:HD, :rows], out[HD:, rows:]], axis=0)
            act_buf[7, r, cols] = out.T.astype(BF16)

        def attend_some(s):
            loop(3, lambda i: attend(s * 3 + i))
            service(2 * pieces + 2 + s)

        loop(5, attend_some)
        loop(micro * pairs - 15, lambda i: attend(15 + i))

        def some_rows(i):
            r = tile(i, block)
            act_buf[1, r, :] = h_buf[r, :].astype(BF16)
            act_buf[2, r, :] = acc_buf[r, :].astype(BF16)

        loop(rows_all // block, some_rows)
        acc_buf[...] = jnp.zeros_like(acc_buf)
        get(l, 0, 8).wait()
        get(l, 8 + 2 * pieces, 9).wait()

        def back_copy():
            return remote(low_buf, back_buf.at[l], ks.at[l], kr.at[l], me.other_role())

        def add(cols, value):
            acc_buf[:, cols] += value

        def first(cols, value):
            h_buf[:, cols] = value

        def second(cols, value):
            low_buf[:, cols] = (h_buf[:, cols] + value).astype(BF16)

        get_w(base + 2, 1).start()
        get_w(base + 1, 0).wait()

        @pl.when(me.role == 1)
        def _():
            through(give_buf.at[0], 0, first)

        through(act_buf.at[1], 0, add)
        service(2 * pieces + 7)
        get_w(base, 0).start()
        get_w(base + 2, 1).wait()

        @pl.when(me.role == 1)
        def _():
            through(give_buf.at[1], 1, second)
            back_copy().start()

        get_hidden(l, 0).start()
        through(act_buf.at[2], 1, add)
        service(2 * pieces + 8)
        get_w(base, 0).wait()
        through(act_buf.at[7], 0, add)
        service(2 * pieces + 9)
        n = n0 + 2 * pieces + 1

        @pl.when(me.role == 0)
        def _():
            def some(i):
                produce(n + i, act_buf.at[8], act_buf.at[1 + i])
                service(2 * pieces + 10 + 2 * i)
                service(2 * pieces + 11 + 2 * i)

            loop(2, some)

        @pl.when(me.role == 1)
        def _():
            def some(i):
                produce(n + i, act_buf.at[8], act_buf.at[1 + i], (act_buf.at[9], give_buf.at[i]))
                service(2 * pieces + 10 + 2 * i)
                service(2 * pieces + 11 + 2 * i)

            loop(2, some)

        produce(n + 2, act_buf.at[8], act_buf.at[7])
        service(2 * pieces + 14)
        service(2 * pieces + 15)

        @pl.when(me.role == 0)
        def _():
            back_copy().wait_recv()

            def some(i):
                r = tile(i, block)
                acc_buf[r, :] += back_buf[l, r, :].astype(F32)

            loop(rows_all // block, some)

        get_hidden(l, 0).wait()
        norm_back(0, l)

        @pl.when(me.role == 1)
        def _():
            back_copy().wait_send()

    loop(layers, layer)
    lower(low_buf, g_buf)
    done = pltpu.make_async_copy(low_buf, frames_grad_ref, out_sem)
    done.start()

    per = 128 * devices // width
    for group in range(width // 128):
        tab_role[group] = tab_sum[:, group * 128 : group * 128 + 128]

    def tab_copy(by):
        to = lax.rem(me.dp + by, devices)
        return remote(tab_role.at[lax.div(to, per)], tab_in.at[me.dp], ts.at[by - 1], tr.at[by - 1], me.around(by))

    def tab_wait(by):
        here = tab_in.at[lax.rem(me.dp - by + devices, devices)]
        remote(here, here, ts.at[by - 1], tr.at[by - 1], me.around(by)).wait_recv()

    loop(devices - 1, lambda i: tab_copy(i + 1).start())
    tab_in[me.dp] = tab_role[lax.div(me.dp, per)]
    last = layers * per_layer - 1
    send_stage(last).wait()
    loop(4, lambda i: reduce.step(2 * last + i))
    loop(devices - 1, lambda i: tab_wait(i + 1))
    loop(devices - 1, lambda i: tab_copy(i + 1).wait_send())
    total = tab_in[0]
    for i in range(1, devices):
        total = total + tab_in[i]
    tab_back[0] = total
    swap = remote(tab_back.at[0], tab_back.at[1], rs_sem, rr_sem, me.other_role())
    swap.start()
    loop(reduce.lag - 2, lambda i: reduce.step(2 * last + 4 + i))
    swap.wait()
    table_out_ref[...] = tab_back[0] + tab_back[1]
    reduce.finish()
    done.wait()


def backward(full, saved, hidden, probs, cotangent, table, pick, used, outers, layers, shard, collective_id):
    count = full.shape[0]
    pieces = (count // layers - 4) // 2
    rows_all, width = cotangent.shape
    keys = probs.shape[2]
    small = table.shape[0]
    dma = pltpu.SemaphoreType.DMA
    devices = 4 * outers
    split = width // 8
    any_space = pl.BlockSpec(memory_space=pl.ANY)
    vmem = pl.BlockSpec(memory_space=pltpu.VMEM)
    grid_rows = (rows_all, width)
    return pl.pallas_call(
        functools.partial(backward_kernel, layers, outers, split),
        out_shape=(
            jax.ShapeDtypeStruct((count, outers, 2, 2, shard, width), BF16),
            jax.ShapeDtypeStruct((layers, shard, 3 * width), F32),
            jax.ShapeDtypeStruct((layers, shard, width), F32),
            jax.ShapeDtypeStruct((layers, shard, pieces * width), F32),
            jax.ShapeDtypeStruct((layers, pieces * shard, width), F32),
            jax.ShapeDtypeStruct(grid_rows, BF16),
            jax.ShapeDtypeStruct((small, 128), F32),
        ),
        in_specs=[any_space, any_space, any_space, any_space, vmem, vmem, vmem, vmem],
        out_specs=(any_space,) * 6 + (vmem,),
        scratch_shapes=[
            pltpu.VMEM(grid_rows, F32),
            pltpu.VMEM(grid_rows, F32),
            pltpu.VMEM(grid_rows, F32),
            pltpu.VMEM((2, width, width), BF16),
            pltpu.VMEM(grid_rows, BF16),
            pltpu.VMEM((10,) + grid_rows, BF16),
            pltpu.VMEM((2,) + grid_rows, BF16),
            pltpu.VMEM((layers,) + grid_rows, BF16),
            pltpu.VMEM((2, keys, keys), BF16),
            pltpu.VMEM((2, outers, 2, 2, shard, width), BF16),
            pltpu.VMEM((small, width), F32),
            pltpu.VMEM((devices, small, 128), F32),
            pltpu.VMEM((width // 128, small, 128), F32),
            pltpu.VMEM((2, small, 128), F32),
            dma((10,)), dma(()), dma((2,)), dma((2,)), dma((2,)), dma((layers,)), dma((layers,)),
            dma((devices - 1,)), dma((devices - 1,)), dma(()), dma(()), dma(()),
        ]
        + Reduce.scratch(layers, outers, shard, width, pieces, split),
        compiler_params=pltpu.CompilerParams(
            collective_id=collective_id, has_side_effects=True, vmem_limit_bytes=60 * 2**20
        ),
        name="backward_and_reduce",
    )(full, saved, hidden, probs, cotangent, table, pick, used)


def prepare(
    shard, causal_gain, causal_shift, section_scale, section_shift, prompt_lengths, target_lengths, sections, rows,
):
    is_target = lax.axis_index("role") == 1
    segs = section_scale.shape[0]
    micro = prompt_lengths.shape[0]
    small = jnp.concatenate(
        [causal_gain, causal_shift, section_scale.reshape(2 * segs, -1), section_shift.reshape(2 * segs, -1)], axis=0
    )
    per = 128 // shard
    spot = (lax.axis_index("dp") % per) * shard
    piece = lax.dynamic_update_slice(jnp.zeros((small.shape[0], 128), BF16), small, (0, spot))

    masks = [[], []]
    section_frames = []
    for m in range(micro):
        prompt_row, target_row, section_row = prompt_lengths[m, 0], target_lengths[m, 0], sections[m, 0]
        prompt_segment, prompt_position, prompt_member = frame_tags(prompt_row, jnp.zeros_like(prompt_row), rows)
        target_segment, target_position, target_member = frame_tags(target_row, prompt_row, rows)
        own_segment = jnp.where(is_target, target_segment, prompt_segment)
        own_position = jnp.where(is_target, target_position, prompt_position)
        own_member = jnp.where(is_target, target_member, prompt_member)
        same_far = (own_segment[None, :] == prompt_segment[:, None]) & is_target
        same_own = own_segment[None, :] == own_segment[:, None]
        causal_own = same_own & (own_position[:, None] <= own_position[None, :])
        masks[0].append(jnp.concatenate([same_far, causal_own], axis=0))
        masks[1].append(jnp.concatenate([same_far, same_own], axis=0))
        section_frames.append(jnp.sum(jnp.where(own_member, section_row[None, :], 0), axis=1))
    bias = jnp.where(jnp.stack([jnp.stack(one) for one in masks]), 0.0, -1e30).astype(BF16)
    section = jnp.concatenate(section_frames)
    none = jnp.zeros_like(section)
    first, second = 4 + 2 * section, 4 + 2 * segs + 2 * section
    used = jnp.stack([none, none + 2, none + 1, none + 3, first, second, first + 1, second + 1])
    return piece, used, bias


def body(
    frames, cotangent, inner_weight, outer_weight, expand_weight, shrink_weight, causal_gain, causal_shift,
    section_scale, section_shift, prompt_lengths, target_lengths, sections,
):
    _, micro, rows, width = frames.shape
    layers, shard, _ = inner_weight.shape
    devices = width // shard
    outers = devices // 4
    pieces = expand_weight.shape[2] // width
    segs = section_scale.shape[0]
    piece, used, bias = prepare(
        shard, causal_gain, causal_shift, section_scale, section_shift, prompt_lengths, target_lengths, sections, rows
    )
    if shard != 64:
        expand_weight = expand_weight.reshape(layers, shard, devices, pieces, shard).transpose(0, 1, 3, 2, 4).reshape(layers, shard, -1)
    entries = jnp.arange(piece.shape[0], dtype=jnp.int32)
    pick = (used[:, :, None] == entries[None, None, :]).astype(BF16)
    pick_t = (used[:, None, :] == entries[None, :, None]).astype(BF16)
    full, saved, hidden, probs, mixed, table = forward(
        inner_weight, outer_weight, expand_weight, shrink_weight, frames.reshape(micro * rows, width), piece, pick, bias, outers, 0
    )
    _, inner_grad, outer_grad, expand_grad, shrink_grad, frames_grad, small = backward(
        full.reshape(-1, width, width), saved, hidden, probs, cotangent.reshape(micro * rows, width),
        table, pick, pick_t, outers, layers, shard, 1,
    )
    if shard != 64:
        expand_grad = expand_grad.reshape(layers, shard, pieces, devices, shard).transpose(0, 1, 3, 2, 4).reshape(layers, shard, -1)
    per = 128 // shard
    spot = (lax.axis_index("dp") % per) * shard
    small = lax.dynamic_slice(small, (0, spot), (small.shape[0], shard))
    return (
        mixed.reshape(1, micro, rows, width), frames_grad.reshape(1, micro, rows, width),
        inner_grad, outer_grad, expand_grad, shrink_grad,
        small[0:2], small[2:4],
        small[4 : 4 + 2 * segs].reshape(segs, 2, shard),
        small[4 + 2 * segs :].reshape(segs, 2, shard),
    )


def solution(mesh):
    rows = P("role", None, "dp", None)
    second = P(None, "dp", None)
    placed = (rows, rows, second, second, second, second, P(None, "dp"), P(None, "dp"), P(None, None, "dp"), P(None, None, "dp"), second, second, second)
    given = (rows, rows, second, second, second, second, P(None, "dp"), P(None, "dp"), P(None, None, "dp"), P(None, None, "dp"))
    return jax.shard_map(body, mesh=mesh, in_specs=placed, out_specs=given, check_vma=False)
```

```python
import functools

import jax
import jax.numpy as jnp
from jax import lax
from jax.experimental import pallas as pl
from jax.experimental.pallas import tpu as pltpu
from jax.sharding import PartitionSpec as P

HEADS = 16
HD = 64
MESH = pl.DeviceIdType.MESH
SLOTS = 4
F32 = jnp.float32
BF16 = jnp.bfloat16


class Place:
    def __init__(self, outer_count):
        self.outers = outer_count
        self.role = lax.axis_index("role")
        dp = lax.axis_index("dp")
        self.core = lax.rem(dp, 2)
        self.pair = lax.rem(lax.div(dp, 2), 2)
        self.outer = lax.div(dp, 4)
        self.dp = dp

    def at(self, role, outer, pair, core):
        return (role, (outer * 2 + pair) * 2 + core)

    def sibling(self):
        return self.at(self.role, self.outer, self.pair, 1 - self.core)

    def across(self):
        return self.at(self.role, self.outer, 1 - self.pair, self.core)

    def other_role(self):
        return self.at(1 - self.role, self.outer, self.pair, self.core)

    def along(self, by):
        return self.at(self.role, lax.rem(self.outer + by, self.outers), self.pair, self.core)

    def around(self, by):
        return (self.role, lax.rem(self.dp + by, 4 * self.outers))

    def greet(self):
        barrier = pltpu.get_barrier_semaphore()
        pl.semaphore_signal(barrier, inc=1, device_id=self.other_role(), device_id_type=MESH)

        def greet_one(i, carry):
            pl.semaphore_signal(barrier, inc=1, device_id=self.around(i + 1), device_id_type=MESH)
            return carry

        lax.fori_loop(0, 4 * self.outers - 1, greet_one, 0)
        pl.semaphore_wait(barrier, 4 * self.outers)


def remote(src, dst, send, recv, peer):
    return pltpu.make_async_remote_copy(
        src_ref=src, dst_ref=dst, send_sem=send, recv_sem=recv, device_id=peer, device_id_type=MESH
    )


def frame_tags(lengths, offsets, total_rows):
    places = jnp.arange(total_rows, dtype=jnp.int32)
    segs = lengths.shape[0]
    upto = jnp.arange(segs)[:, None] >= jnp.arange(segs)[None, :]
    finish = jnp.sum(jnp.where(upto, lengths[None, :], 0), axis=1)
    segment = jnp.sum((places[:, None] >= finish[None, :]).astype(jnp.int32), axis=1)
    member = segment[:, None] == jnp.arange(segs, dtype=jnp.int32)[None, :]
    shifted = offsets - (finish - lengths)
    position = places + jnp.sum(jnp.where(member, shifted[None, :], 0), axis=1)
    return (segment, position, member)


def dot(a, b):
    return jnp.dot(a, b, preferred_element_type=F32)


def dot_t(a, b):
    return lax.dot_general(a, b, (((1,), (1,)), ((), ())), preferred_element_type=F32)


def t_dot(a, b):
    return lax.dot_general(a, b, (((0,), (0,)), ((), ())), preferred_element_type=F32)


def normalize(hidden):
    average = jnp.mean(hidden, axis=-1, keepdims=True)
    centred = hidden - average
    spread = jnp.mean(centred * centred, axis=-1, keepdims=True)
    inverse = lax.rsqrt(spread + 1e-05)
    return centred * inverse, inverse


def norm_backward(grad, scale, unit, inverse):
    inner = grad * scale
    return inverse * (
        inner - jnp.mean(inner, axis=-1, keepdims=True) - unit * jnp.mean(inner * unit, axis=-1, keepdims=True)
    )


def gelu_parts(upper):
    cumulative = 0.5 * (1.0 + lax.erf(upper * 0.7071067811865476))
    density = jnp.exp(-0.5 * upper * upper) * 0.3989422804014327
    return upper * cumulative, cumulative + upper * density


class Gather:
    lag = 9

    def __init__(self, me, part_ref, full_ref, split, sems):
        self.me, self.part, self.full, self.split = me, part_ref, full_ref, split
        (
            self.own_sem, self.zs, self.zr, self.fs, self.xs, self.xr, self.us, self.ur, self.vs, self.vr, self.cs, self.cr,
            self.qxs, self.qxr, self.qzs, self.qzr, self.qfs,
        ) = sems
        self.half = part_ref.shape[-1] // 2
        self.main = self.half - split
        self.steps = 2 * part_ref.shape[0]
        self.chain = me.outers == 4

    @staticmethod
    def semaphores(many):
        dma = pltpu.SemaphoreType.DMA
        return [
            dma((4,)),
            dma((6, many)), dma((6, many)), dma((6,)),
            dma((6,)), dma((6,)),
            dma((12, many)), dma((12, many)),
            dma((6,)), dma((6,)),
            dma((4,)), dma((4,)),
            dma((6,)), dma((6,)), dma((6, many)), dma((6, many)), dma((6,)),
        ]

    def cols(self, h, offset, size):
        return pl.ds(pl.multiple_of(lax.rem(h, 2) * self.half + offset, 128), size)

    def main_cols(self, h, odd):
        if odd:
            return self.cols(h, self.me.role * 2 * self.split, 2 * self.split)
        return self.cols(h, self.me.role * self.split, self.main)

    def cross_cols(self, h):
        return self.cols(h, (2 - self.me.role) * self.split, self.split)

    def give_cols(self, h):
        return self.cols(h, self.me.role * self.main, self.split)

    def take_cols(self, h):
        return self.cols(h, (1 - self.me.role) * self.main, self.split)

    def before(self, by):
        return lax.rem(self.me.outer - by + self.me.outers, self.me.outers)

    def sends(self, by, action):
        self.unless(by, {1: 3, 3: 0}, action)

    def takes(self, by, action):
        self.unless(by, {1: 0, 3: 3}, action)

    def unless(self, by, ends, action):
        if self.chain and by in ends:
            pl.when(self.me.outer != ends[by])(action)
        else:
            action()

    def passes(self, action):
        if self.chain:
            z = self.me.outer

            @pl.when((z == 1) | (z == 2))
            def _():
                action(6 - 3 * z, self.me.at(self.me.role, 3 * z - 3, self.me.pair, self.me.core), 2 * z - 2)

    def gets(self, action):
        if self.chain:
            z = self.me.outer

            @pl.when((z == 0) | (z == 3))
            def _():
                action(3 - z, jnp.where(z == 0, 0, 2))

    def own(self, h):
        me, cols = self.me, self.cols(h, 0, self.half)
        return pltpu.make_async_copy(
            self.part.at[lax.div(h, 2), :, cols],
            self.full.at[lax.div(h, 2), me.outer, me.pair, me.core, :, cols],
            self.own_sem.at[lax.rem(h, 4)],
        )

    def z_copy(self, h, by, odd):
        me, cols, s = self.me, self.main_cols(h, odd), lax.rem(h, 6)
        return remote(
            self.part.at[lax.div(h, 2), :, cols],
            self.full.at[lax.div(h, 2), me.outer, me.pair, me.core, :, cols],
            self.zs.at[s, by - 1], self.zr.at[s, by - 1], me.along(by),
        )

    def z_block(self, h, block, odd):
        return self.full.at[lax.div(h, 2), block, self.me.pair, self.me.core, :, self.main_cols(h, odd)]

    def z_wait(self, h, block, index, odd):
        dst, s = self.z_block(h, block, odd), lax.rem(h, 6)
        remote(dst, dst, self.fs.at[s], self.zr.at[s, index], self.me.across()).wait_recv()

    def f_copy(self, h, block, to, index, odd):
        ref, s = self.z_block(h, block, odd), lax.rem(h, 6)
        return remote(ref, ref, self.fs.at[s], self.zr.at[s, index], to)

    def x_copy(self, h, pair, odd):
        me, s = self.me, lax.rem(h, 6)
        ref = self.full.at[lax.div(h, 2), :, pair, me.core, :, self.main_cols(h, odd)]
        return remote(ref, ref, self.xs.at[s], self.xr.at[s], me.across())

    def qx_copy(self, h):
        me, cols, s = self.me, self.cross_cols(h), lax.rem(h, 6)
        return remote(
            self.part.at[lax.div(h, 2), :, cols],
            self.full.at[lax.div(h, 2), me.outer, me.pair, me.core, :, cols],
            self.qxs.at[s], self.qxr.at[s], me.across(),
        )

    def qx_wait(self, h):
        me, s = self.me, lax.rem(h, 6)
        dst = self.full.at[lax.div(h, 2), me.outer, 1 - me.pair, me.core, :, self.cross_cols(h)]
        remote(dst, dst, self.qxs.at[s], self.qxr.at[s], me.across()).wait_recv()

    def q_block(self, h, block):
        return self.full.at[lax.div(h, 2), block, :, self.me.core, :, self.cross_cols(h)]

    def qz_copy(self, h, by):
        ref, s = self.q_block(h, self.me.outer), lax.rem(h, 6)
        return remote(ref, ref, self.qzs.at[s, by - 1], self.qzr.at[s, by - 1], self.me.along(by))

    def qz_wait(self, h, block, index):
        dst, s = self.q_block(h, block), lax.rem(h, 6)
        remote(dst, dst, self.qfs.at[s], self.qzr.at[s, index], self.me.across()).wait_recv()

    def qf_copy(self, h, block, to, index):
        ref, s = self.q_block(h, block), lax.rem(h, 6)
        return remote(ref, ref, self.qfs.at[s], self.qzr.at[s, index], to)

    def u_copy(self, h, by, cols):
        me, s = self.me, lax.rem(h, 12)
        ref = self.full.at[lax.div(h, 2), self.before(by), me.pair, me.core, :, cols]
        return remote(ref, ref, self.us.at[s, by - 1], self.ur.at[s, by - 1], me.other_role())

    def v_copy(self, h, cols):
        me, s = self.me, lax.rem(h, 6)
        ref = self.full.at[lax.div(h, 2), :, 1 - me.pair, me.core, :, cols]
        return remote(ref, ref, self.vs.at[s], self.vr.at[s], me.other_role())

    def c_copy(self, h, core):
        s = lax.rem(h, 4)
        ref = self.full.at[lax.div(h, 2), :, :, core, :, self.cols(h, 0, self.half)]
        return remote(ref, ref, self.cs.at[s], self.cr.at[s], self.me.sibling())

    def step(self, t):
        for odd in (False, True):
            pl.when(lax.rem(t, 2) == int(odd))(functools.partial(self.stages, t, odd))

        @pl.when((t >= 9) & (t < self.steps + 9))
        def _():
            h = t - 9
            self.c_copy(h, 1 - self.me.core).wait_recv()
            self.c_copy(h, self.me.core).wait_send()

    def stages(self, t, odd):
        me, count = self.me, self.steps
        others = range(1, me.outers)

        @pl.when(t < count)
        def _():
            self.own(t).start()
            for by in others:
                self.sends(by, lambda: self.z_copy(t, by, odd).start())
            if odd:
                self.qx_copy(t).start()

        @pl.when((t >= 2) & (t < count + 2))
        def _():
            h = t - 2
            self.own(h).wait()
            for by in others:
                self.takes(by, lambda: self.z_wait(h, self.before(by), by - 1, odd))
            self.passes(lambda block, to, index: self.f_copy(h, block, to, index, odd).start())
            if odd:
                self.qx_wait(h)
                for by in others:
                    self.sends(by, lambda: self.qz_copy(h, by).start())

        @pl.when((t >= 4) & (t < count + 4))
        def _():
            h = t - 4
            self.gets(lambda block, index: self.z_wait(h, block, index, odd))
            self.x_copy(h, me.pair, odd).start()
            for by in others:
                self.u_copy(h, by, self.give_cols(h)).start()
            for by in others:
                self.sends(by, lambda: self.z_copy(h, by, odd).wait_send())
            self.passes(lambda block, to, index: self.f_copy(h, block, to, index, odd).wait_send())
            if odd:
                for by in others:
                    self.takes(by, lambda: self.qz_wait(h, self.before(by), by - 1))
                self.passes(lambda block, to, index: self.qf_copy(h, block, to, index).start())
                self.qx_copy(h).wait_send()

        @pl.when((t >= 6) & (t < count + 6))
        def _():
            h = t - 6
            self.x_copy(h, 1 - me.pair, odd).wait_recv()
            self.v_copy(h, self.give_cols(h)).start()
            if odd:
                self.gets(lambda block, index: self.qz_wait(h, block, index))
                for by in others:
                    self.sends(by, lambda: self.qz_copy(h, by).wait_send())
                self.passes(lambda block, to, index: self.qf_copy(h, block, to, index).wait_send())

        @pl.when((t >= 8) & (t < count + 8))
        def _():
            h = t - 8
            for by in others:
                self.u_copy(h, by, self.take_cols(h)).wait_recv()
            self.v_copy(h, self.take_cols(h)).wait_recv()
            self.c_copy(h, me.core).start()
            for by in others:
                self.u_copy(h, by, self.give_cols(h)).wait_send()
            self.x_copy(h, me.pair, odd).wait_send()
            self.v_copy(h, self.give_cols(h)).wait_send()


def loop(count, action):
    def one(i, carry):
        action(i)
        return carry

    lax.fori_loop(0, count, one, 0)


def tile(i, size):
    return pl.ds(pl.multiple_of(i * size, size), size)


WIDE = 1024


def forward_kernel(
    layers, outers, split,
    inner_ref, outer_ref, expand_ref, shrink_ref, frames_ref, piece_ref, pick_ref, bias_ref,
    full_ref, saved_ref, hidden_ref, probs_ref, mixed_ref, table_ref,
    part_buf, e_buf, tab_in, h_buf, a_buf, qkv_buf, far_in, far_buf, mix_buf, f_buf, lift_buf, slope_buf, w_buf, p_buf,
    pack_sem, ts, tr, w_sem, save_sem, h_sem, p_sem, out_sem, ks, kr, *gather_sems,
):
    me = Place(outers)
    devices = 4 * outers
    rows_all, width = frames_ref.shape
    count, shard, _ = part_buf.shape
    per_layer = count // layers
    pieces = (per_layer - 4) // 2
    micro = bias_ref.shape[1]
    rows = rows_all // micro
    pairs = width // 128
    gather = Gather(me, part_buf, full_ref, split, gather_sems)
    early, late = [], []
    for l in range(layers):
        base = l * per_layer
        sources = [(i, inner_ref.at[l, :, pl.ds(i * width, width)]) for i in range(3)] + [(3, outer_ref.at[l])]
        sources += [(5 + 2 * j, shrink_ref.at[l, pl.ds(j * shard, shard)]) for j in range(pieces)]
        for k, source in sources:
            copy = pltpu.make_async_copy(source, part_buf.at[base + k], pack_sem.at[base + k])
            (early if base + k < 4 else late).append(copy)
        late.append(pltpu.make_async_copy(expand_ref.at[l], e_buf.at[l], pack_sem.at[count + l]))
    for copy in early + late:
        copy.start()
    me.greet()

    def piece_copy(by):
        return remote(piece_ref, tab_in.at[me.dp], ts.at[by - 1], tr.at[by - 1], me.around(by))

    def piece_wait(by):
        here = tab_in.at[(me.dp - by + devices) % devices]
        remote(here, here, ts.at[by - 1], tr.at[by - 1], me.around(by)).wait_recv()

    loop(devices - 1, lambda i: piece_copy(i + 1).start())
    tab_in[me.dp] = piece_ref[...]

    @pl.when(me.role == 0)
    def _():
        far_buf[...] = jnp.zeros_like(far_buf)
        far_in[...] = jnp.zeros_like(far_in)

    ahead = gather.lag - 4
    for copy in early:
        copy.wait()
    loop(2, gather.step)
    for copy in late:
        copy.wait()

    def spread(index):
        l, t = lax.div(index, width // 128), lax.rem(index, width // 128)
        first = lax.broadcasted_iota(jnp.int32, (shard, 128), 1) < 64
        for j in range(pieces):
            to = part_buf.at[l * per_layer + 4 + 2 * j, :, tile(t, 128)]
            if shard == 64:
                even = e_buf[l, :, tile(t * pieces + j // 2, 128)].astype(F32)
                odd = e_buf[l, :, tile(t * pieces + pieces // 2 + j // 2, 128)].astype(F32)
                if j % 2 == 0:
                    odd = pltpu.roll(odd, 64, 1)
                else:
                    even = pltpu.roll(even, 64, 1)
                to[...] = jnp.where(first, even, odd).astype(BF16)
            else:
                to[...] = e_buf[l, :, tile(j * (width // 128) + t, 128)]

    loop(layers * width // 128, spread)
    loop(devices - 1, lambda i: piece_wait(i + 1))
    loop(devices - 1, lambda i: piece_copy(i + 1).wait_send())
    per = 128 * devices // width
    for group in range(width // 128):
        total = tab_in[group * per]
        for i in range(1, per):
            total = total + tab_in[group * per + i]
        table_ref[:, group * 128 : group * 128 + 128] = total

    def load_rows(i):
        r = tile(i, 64)
        h_buf[0, r, :] = frames_ref[r, :].astype(F32)

    loop(rows_all // 64, load_rows)

    def load(k):
        return pltpu.make_async_copy(full_ref.at[k], w_buf.at[lax.rem(k, 2)], w_sem.at[lax.rem(k, 2)])

    def matmul(in_ref, k, finish):
        load(k).wait()

        def columns(n):
            cols = tile(n, WIDE)
            w = w_buf[lax.rem(k, 2), :, :, :, :, cols].reshape(width, WIDE)
            finish(cols, dot(in_ref[...], w))

        loop(width // WIDE, columns)

    def norm(index, src, dst_ref, l):
        def some(i):
            r = tile(i, 64)
            unit, _ = normalize(h_buf[src, r, :])
            scale = dot(pick_ref[l * 4 + 2 * index, r, :], table_ref[...])
            shift = dot(pick_ref[l * 4 + 2 * index + 1, r, :], table_ref[...])
            dst_ref[r, :] = (scale * unit + shift).astype(BF16)

        loop(rows_all // 64, some)

    def save_at(l, ref, slot):
        return pltpu.make_async_copy(ref, saved_ref.at[l, slot], save_sem.at[slot])

    def save_hidden_at(l, which):
        return pltpu.make_async_copy(h_buf.at[which], hidden_ref.at[l, which], h_sem.at[which])

    def far_copy(l):
        return remote(a_buf, far_in.at[l], ks.at[l], kr.at[l], me.other_role())

    def begin(l):
        save_hidden_at(l, 0).start()
        norm(0, 0, a_buf, l)
        save_at(l, a_buf, 0).start()

        @pl.when(me.role == 0)
        def _():
            far_copy(l).start()

    begin(0)
    loop(gather.lag, lambda i: gather.step(i + 2))

    def layer(l):
        base = l * per_layer

        def save(ref, slot):
            return save_at(l, ref, slot)

        def save_hidden(which):
            return save_hidden_at(l, which)

        load(base).start()

        def project(i):
            def keep(cols, value):
                qkv_buf[i, :, cols] = value.astype(BF16)

            matmul(a_buf, base + i, keep)
            gather.step(2 * (base + i) + 6 + ahead)
            gather.step(2 * (base + i) + 7 + ahead)

            @pl.when(i < 2)
            def _():
                load(base + i + 1).start()

            save(qkv_buf.at[i], 1 + i).start()

        loop(3, project)

        @pl.when(me.role == 1)
        def _():
            load(base + 1).start()
            load(base + 2).start()
            far_copy(l).wait_recv()

            def project_far(i):
                def keep(cols, value):
                    far_buf[i, :, cols] = value.astype(BF16)

                matmul(far_in.at[l], base + 1 + i, keep)

            loop(2, project_far)

        load(base + 3).start()
        save(far_in.at[l], 8 + 2 * pieces).start()
        save(far_buf.at[0], 4).start()
        save(far_buf.at[1], 5).start()

        def save_probs(it):
            return pltpu.make_async_copy(p_buf.at[lax.rem(it, 2)], probs_ref.at[l, it], p_sem.at[lax.rem(it, 2)])

        def attend(it):
            m, p = lax.div(it, pairs), lax.rem(it, pairs)
            r, cols = tile(m, rows), tile(p, 128)
            first = lax.broadcasted_iota(jnp.int32, (rows, 128), 1) < HD
            q = qkv_buf[0, r, cols].astype(F32) * HD**-0.5
            both = jnp.concatenate([jnp.where(first, q, 0.0).astype(BF16), jnp.where(first, 0.0, q).astype(BF16)], axis=0)
            keys = jnp.concatenate([far_buf[0, r, cols], qkv_buf[1, r, cols]], axis=0)
            values = jnp.concatenate([far_buf[1, r, cols], qkv_buf[2, r, cols]], axis=0)
            bias = bias_ref[l, m].astype(F32)
            scores = dot_t(keys, both) + jnp.concatenate([bias, bias], axis=1)
            exponent = jnp.exp(scores - jnp.max(scores, axis=0, keepdims=True))
            soft = (exponent * (1.0 / jnp.sum(exponent, axis=0, keepdims=True))).astype(BF16)

            @pl.when(it >= 2)
            def _():
                save_probs(it - 2).wait()

            p_buf[lax.rem(it, 2)] = soft
            save_probs(it).start()
            out = t_dot(values, soft)
            out = jnp.concatenate([out[:HD, :rows], out[HD:, rows:]], axis=0)
            mix_buf[r, cols] = out.T.astype(BF16)

        segment = micro * pairs // 4

        def attend_some(s):
            loop(segment, lambda i: attend(s * segment + i))
            gather.step(2 * base + 12 + s + ahead)

        loop(4, attend_some)
        save_probs(micro * pairs - 2).wait()
        save_probs(micro * pairs - 1).wait()
        save(mix_buf, 6).start()
        load(base + 4).start()
        gather.step(2 * base + 16 + ahead)

        def keep_middle(cols, value):
            h_buf[1, :, cols] = h_buf[0, :, cols] + value

        matmul(mix_buf, base + 3, keep_middle)
        save_hidden(1).start()
        save_hidden(0).wait()
        gather.step(2 * base + 17 + ahead)
        norm(1, 1, f_buf, l)
        save(f_buf, 7).start()
        h_buf[0] = h_buf[1]

        def feed(j):
            gather.step(2 * base + 18 + 3 * j + ahead)
            load(base + 5 + 2 * j).start()

            def raise_columns(cols, value):
                up, slope = gelu_parts(value)
                lift_buf[:, cols] = up.astype(BF16)
                slope_buf[:, cols] = slope.astype(BF16)

            matmul(f_buf, base + 4 + 2 * j, raise_columns)
            lift_save = pltpu.make_async_copy(lift_buf, saved_ref.at[l, 8 + j], save_sem.at[9 + 2 * pieces])
            slope_save = pltpu.make_async_copy(slope_buf, saved_ref.at[l, 8 + pieces + j], save_sem.at[8])
            lift_save.start()
            slope_save.start()
            gather.step(2 * base + 19 + 3 * j + ahead)

            @pl.when(j < pieces - 1)
            def _():
                load(base + 6 + 2 * j).start()

            def add(cols, value):
                h_buf[0, :, cols] += value

            matmul(lift_buf, base + 5 + 2 * j, add)
            gather.step(2 * base + 20 + 3 * j + ahead)
            lift_save.wait()
            slope_save.wait()

        loop(pieces, feed)
        save_hidden(1).wait()
        save(a_buf, 0).wait()
        for i in range(3):
            save(qkv_buf.at[i], 1 + i).wait()
        save(far_buf.at[0], 4).wait()
        save(far_buf.at[1], 5).wait()
        save(mix_buf, 6).wait()
        save(f_buf, 7).wait()
        save(far_in.at[l], 8 + 2 * pieces).wait()

        @pl.when(me.role == 0)
        def _():
            far_copy(l).wait_send()

        @pl.when(l < layers - 1)
        def _():
            begin(l + 1)

    loop(layers, layer)

    def store_rows(i):
        r = tile(i, 64)
        a_buf[r, :] = h_buf[0, r, :].astype(BF16)

    loop(rows_all // 64, store_rows)
    done = pltpu.make_async_copy(a_buf, mixed_ref, out_sem)
    done.start()
    done.wait()


def forward(inner, outer, expand, shrink, frames, piece, pick, bias, outers, collective_id):
    layers, shard, width = outer.shape
    rows_all = frames.shape[0]
    pieces = expand.shape[2] // width
    count = layers * (4 + 2 * pieces)
    many = outers - 1
    dma = pltpu.SemaphoreType.DMA
    devices = 4 * outers
    split = width // 8
    micro = bias.shape[1]
    keys, rows = bias.shape[2:]
    pairs = width // 128
    any_space = pl.BlockSpec(memory_space=pl.ANY)
    vmem = pl.BlockSpec(memory_space=pltpu.VMEM)
    grid_rows = (rows_all, width)
    return pl.pallas_call(
        functools.partial(forward_kernel, layers, outers, split),
        out_shape=(
            jax.ShapeDtypeStruct((count, outers, 2, 2, shard, width), BF16),
            jax.ShapeDtypeStruct((layers, 9 + 2 * pieces) + grid_rows, BF16),
            jax.ShapeDtypeStruct((layers, 2) + grid_rows, F32),
            jax.ShapeDtypeStruct((layers, micro * pairs, keys, 2 * rows), BF16),
            jax.ShapeDtypeStruct(grid_rows, BF16),
            jax.ShapeDtypeStruct((piece.shape[0], width), BF16),
        ),
        in_specs=[any_space, any_space, any_space, any_space, vmem, vmem, vmem, vmem],
        out_specs=(any_space, any_space, any_space, any_space, any_space, vmem),
        scratch_shapes=[
            pltpu.VMEM((count, shard, width), BF16),
            pltpu.VMEM(expand.shape, BF16),
            pltpu.VMEM((devices,) + piece.shape, BF16),
            pltpu.VMEM((2,) + grid_rows, F32),
            pltpu.VMEM(grid_rows, BF16),
            pltpu.VMEM((3,) + grid_rows, BF16),
            pltpu.VMEM((layers,) + grid_rows, BF16),
            pltpu.VMEM((2,) + grid_rows, BF16),
            pltpu.VMEM(grid_rows, BF16),
            pltpu.VMEM(grid_rows, BF16),
            pltpu.VMEM(grid_rows, BF16),
            pltpu.VMEM(grid_rows, BF16),
            pltpu.VMEM((2, outers, 2, 2, shard, width), BF16),
            pltpu.VMEM((2, keys, 2 * rows), BF16),
            dma((count + layers,)), dma((devices - 1,)), dma((devices - 1,)),
            dma((2,)), dma((10 + 2 * pieces,)), dma((2,)), dma((2,)), dma(()), dma((layers,)), dma((layers,)),
        ]
        + Gather.semaphores(many),
        compiler_params=pltpu.CompilerParams(
            collective_id=collective_id, has_side_effects=True, vmem_limit_bytes=58 * 2**20
        ),
        name="gather_and_forward",
    )(inner, outer, expand, shrink, frames, piece, pick, bias)


class Reduce:
    lag = 10

    def __init__(self, me, layers, grad_ref, out_refs, split, refs):
        self.me, self.grad, self.split = me, grad_ref, split
        self.inner_out, self.outer_out, self.expand_out, self.shrink_out = out_refs
        (
            self.own_buf, self.core_buf, self.role_buf, self.pair_buf, self.outer_buf, self.end_in, self.last_buf, self.sum_buf,
            self.low_buf, self.cross_end, self.cross_in, self.cross_sum, self.cross_pair, self.end_buf, self.fin_buf, self.spread_buf,
            self.own_sem, self.cs, self.cr, self.ys, self.yr, self.xs, self.xr, self.zs, self.zr, self.ns, self.nr,
            self.qas, self.qar, self.qzs, self.qzr, self.qxs, self.qxr, self.es, self.er, self.fs, self.ps,
        ) = refs
        self.half = grad_ref.shape[-1] // 2
        self.main = self.half - split
        self.steps = 2 * grad_ref.shape[0]
        self.layers = layers
        self.per_layer = grad_ref.shape[0] // layers
        self.pieces = (self.per_layer - 4) // 2
        self.chain = me.outers == 4

    @staticmethod
    def scratch(layers, outers, rows, width, pieces, split):
        dma = pltpu.SemaphoreType.DMA
        many = outers - 1
        half = width // 2
        main = half - split
        return [
            pltpu.VMEM((2, outers, 2, rows, half), BF16),
            pltpu.VMEM((4, outers, 2, rows, half), BF16),
            pltpu.VMEM((8, outers, 2, rows, split), BF16),
            pltpu.VMEM((6, outers, rows, main), BF16),
            pltpu.VMEM((10, many, rows, main), BF16),
            pltpu.VMEM((8, rows, main), BF16),
            pltpu.VMEM((4, rows, half), BF16),
            pltpu.VMEM((6, outers, 2, rows, half), BF16),
            pltpu.VMEM((6, outers, rows, main), BF16),
            pltpu.VMEM((8, 2, rows, split), BF16),
            pltpu.VMEM((8, many, 2, rows, split), BF16),
            pltpu.VMEM((6, 2, rows, split), BF16),
            pltpu.VMEM((6, rows, split), BF16),
            pltpu.VMEM((4, rows, half), BF16),
            pltpu.VMEM((4, rows, half), F32),
            pltpu.VMEM((layers, rows, pieces * width), F32),
            dma((2,)),
            dma((4,)), dma((4,)),
            dma((8,)), dma((8,)),
            dma((6,)), dma((6,)),
            dma((10, many)), dma((10, many)),
            dma((8,)), dma((8,)),
            dma((8,)), dma((8,)),
            dma((8, many)), dma((8, many)),
            dma((6,)), dma((6,)),
            dma((4,)), dma((4,)),
            dma((4,)), dma((layers,)),
        ]

    def sends(self, by, action):
        self.unless(by, {1: 3, 3: 0}, action)

    def takes(self, by, action):
        self.unless(by, {1: 0, 3: 3}, action)

    def unless(self, by, ends, action):
        if self.chain and by in ends:
            pl.when(self.me.outer != ends[by])(action)
        else:
            action()

    def ends(self, action):
        if self.chain:
            z = self.me.outer

            @pl.when((z == 0) | (z == 3))
            def _():
                action(3 - z, self.me.at(self.me.role, 1 + lax.div(z, 3), self.me.pair, self.me.core))

    def inner(self, action):
        if self.chain:
            z = self.me.outer

            @pl.when((z == 1) | (z == 2))
            def _():
                action(6 - 3 * z)

    def early(self, by, action):
        if self.chain and by == 2:
            z = self.me.outer
            pl.when((z == 0) | (z == 3))(action)
        else:
            self.sends(by, action)

    def cols(self, offset, size):
        return pl.ds(pl.multiple_of(offset, 128), size)

    def main_cols(self, odd):
        return pl.ds(0, self.main) if odd else self.cols(self.me.role * self.split, self.main)

    def keep_cols(self):
        return self.cols(self.me.role * self.main, self.split)

    def give_cols(self):
        return self.cols((1 - self.me.role) * self.main, self.split)

    def part(self, k, core):
        return self.grad.at[lax.div(k, 2), :, :, core, :, self.cols(lax.rem(k, 2) * self.half, self.half)]

    def own(self, k):
        s = lax.rem(k, 2)
        return pltpu.make_async_copy(self.part(k, self.me.core), self.own_buf.at[s], self.own_sem.at[s])

    def c_copy(self, k):
        s = lax.rem(k, 4)
        return remote(self.part(k, 1 - self.me.core), self.core_buf.at[s], self.cs.at[s], self.cr.at[s], self.me.sibling())

    def y_copy(self, k):
        s = lax.rem(k, 8)
        return remote(
            self.sum_buf.at[lax.rem(k, 6), :, :, :, self.give_cols()], self.role_buf.at[s], self.ys.at[s], self.yr.at[s],
            self.me.other_role(),
        )

    def x_copy(self, k, odd):
        s = lax.rem(k, 6)
        return remote(
            self.sum_buf.at[s, :, 1 - self.me.pair, :, self.main_cols(odd)],
            self.pair_buf.at[s], self.xs.at[s], self.xr.at[s], self.me.across(),
        )

    def toward(self, by):
        return lax.rem(self.me.outer + by, self.me.outers)

    def z_copy(self, k, by):
        s = lax.rem(k, 10)
        return remote(
            self.low_buf.at[lax.rem(k, 6), self.toward(by)], self.outer_buf.at[s, by - 1],
            self.zs.at[s, by - 1], self.zr.at[s, by - 1], self.me.along(by),
        )

    def n_copy(self, k, block, to):
        s = lax.rem(k, 8)
        return remote(self.low_buf.at[lax.rem(k, 6), block], self.end_in.at[s], self.ns.at[s], self.nr.at[s], to)

    def cross(self, k, block):
        return self.sum_buf.at[lax.rem(k, 6), block, :, :, pl.ds(self.main, self.split)]

    def qa_copy(self, k, block, to):
        s = lax.rem(k, 8)
        return remote(self.cross(k, block), self.cross_end.at[s], self.qas.at[s], self.qar.at[s], to)

    def qz_copy(self, k, by):
        s = lax.rem(k, 8)
        return remote(
            self.cross(k, self.toward(by)), self.cross_in.at[s, by - 1], self.qzs.at[s, by - 1], self.qzr.at[s, by - 1], self.me.along(by)
        )

    def qx_copy(self, k):
        s = lax.rem(k, 6)
        return remote(self.cross_sum.at[s, 1 - self.me.pair], self.cross_pair.at[s], self.qxs.at[s], self.qxr.at[s], self.me.across())

    def e_copy(self, k, odd):
        s = lax.rem(k, 4)
        cols = pl.ds(0, self.half if odd else self.main)
        return remote(self.end_buf.at[s, :, cols], self.last_buf.at[s, :, cols], self.es.at[s], self.er.at[s], self.me.other_role())

    def kind(self, k):
        n = lax.div(k, 2)
        return self.layers - 1 - lax.div(n, self.per_layer), lax.rem(n, self.per_layer)

    def is_expand(self, k):
        _, q = self.kind(k)
        return (q < 2 * self.pieces) & (lax.rem(q, 2) == 1)

    def store(self, k):
        s, half = lax.rem(k, 4), lax.rem(k, 2)
        layer, q = self.kind(k)
        width, pieces = 2 * self.half, self.pieces
        rows = self.fin_buf.shape[1]
        cols = self.cols(half * self.half, self.half)
        piece = lax.div(q, 2)

        def put(dst):
            pltpu.make_async_copy(self.fin_buf.at[s], dst, self.fs.at[s]).start()

        @pl.when((q < 2 * pieces) & (lax.rem(q, 2) == 0))
        def _():
            put(self.shrink_out.at[layer, pl.ds(pl.multiple_of(piece * rows, rows), rows), cols])

        @pl.when(q == 2 * pieces)
        def _():
            put(self.outer_out.at[layer, :, cols])

        @pl.when(q > 2 * pieces)
        def _():
            put(self.inner_out.at[layer, :, self.cols(lax.rem(q - 2 * pieces, 3) * width + half * self.half, self.half)])

        @pl.when(self.is_expand(k))
        def _():
            self.spread(layer, piece, half, s)

            @pl.when((piece == pieces - 1) & (half == 1))
            def _():
                self.spread_copy(layer).start()

    def spread_copy(self, layer):
        return pltpu.make_async_copy(self.spread_buf.at[layer], self.expand_out.at[layer], self.ps.at[layer])

    def spread(self, layer, piece, half, s):
        rows, pieces = self.fin_buf.shape[1], self.pieces
        tiles = self.half // 128
        first = lax.broadcasted_iota(jnp.int32, (rows, 128), 1) < 64

        def some(i):
            value = self.fin_buf[s, :, tile(i, 128)]
            if rows != 64:
                self.spread_buf[layer, :, tile((2 * piece + half) * tiles + i, 128)] = value
                return
            moved = pltpu.roll(value, 64, 1)
            at = (half * tiles + i) * pieces + lax.div(piece, 2)
            even, odd = tile(at, 128), tile(at + pieces // 2, 128)

            @pl.when(lax.rem(piece, 2) == 0)
            def _():
                self.spread_buf[layer, :, even] = jnp.where(first, value, self.spread_buf[layer, :, even])
                self.spread_buf[layer, :, odd] = jnp.where(first, moved, self.spread_buf[layer, :, odd])

            @pl.when(lax.rem(piece, 2) == 1)
            def _():
                self.spread_buf[layer, :, even] = jnp.where(first, self.spread_buf[layer, :, even], moved)
                self.spread_buf[layer, :, odd] = jnp.where(first, self.spread_buf[layer, :, odd], value)

        loop(tiles, some)

    def stored(self, k):
        @pl.when(jnp.logical_not(self.is_expand(k)))
        def _():
            s = lax.rem(k, 4)
            pltpu.make_async_copy(self.fin_buf.at[s], self.outer_out.at[0, :, pl.ds(0, self.half)], self.fs.at[s]).wait()

    def step(self, t):
        for odd in (False, True):
            pl.when((lax.rem(t, 2) == int(odd)) & (t >= 0))(functools.partial(self.stages, t, odd))

    def stages(self, t, same):
        me, count, split, main = self.me, self.steps, self.split, self.main
        others = range(1, me.outers)
        low = self.low_buf

        @pl.when(t < count)
        def _():
            self.own(t).start()
            self.c_copy(t).start()

        @pl.when((t >= 1) & (t < count + 1))
        def _():
            k, odd = t - 1, not same
            self.own(k).wait()
            self.c_copy(k).wait()

            def add(i):
                o, p = lax.div(i, 2), lax.rem(i, 2)
                self.sum_buf[lax.rem(k, 6), o, p] = self.own_buf[lax.rem(k, 2), o, p] + self.core_buf[lax.rem(k, 4), o, p]

            loop(2 * me.outers, add)
            if odd:
                self.ends(lambda block, to: self.qa_copy(k, block, to).start())
            else:
                self.y_copy(k).start()

        @pl.when((t >= 3) & (t < count + 3))
        def _():
            k, odd = t - 3, not same
            s = lax.rem(k, 6)
            if odd:
                self.x_copy(k, odd).start()

                def take(block):
                    self.qa_copy(k, block, me.across()).wait_recv()
                    for p in range(2):
                        self.sum_buf[s, block, p, :, main:] = self.sum_buf[s, block, p, :, main:] + self.cross_end[lax.rem(k, 8), p]

                self.inner(take)
                self.ends(lambda block, to: self.qa_copy(k, block, to).wait_send())
                for by in others:
                    self.sends(by, lambda: self.qz_copy(k, by).start())
            else:
                self.y_copy(k).wait()
                keep = self.keep_cols()

                def add(i):
                    o, p = lax.div(i, 2), lax.rem(i, 2)
                    self.sum_buf[s, o, p, :, keep] = self.sum_buf[s, o, p, :, keep] + self.role_buf[lax.rem(k, 8), o, p]

                loop(2 * me.outers, add)
                self.x_copy(k, odd).start()

        @pl.when((t >= 5) & (t < count + 5))
        def _():
            k, odd = t - 5, not same
            s = lax.rem(k, 6)
            self.x_copy(k, odd).wait()
            cols = self.main_cols(odd)

            def add(o):
                low[s, o] = self.sum_buf[s, o, me.pair, :, cols] + self.pair_buf[s, o]

            loop(me.outers, add)
            self.ends(lambda block, to: self.n_copy(k, block, to).start())
            for by in others:
                self.early(by, lambda: self.z_copy(k, by).start())
            if odd:
                self.cross_sum[s] = self.sum_buf[s, me.outer, :, :, main:]
                for by in others:

                    def take():
                        self.qz_copy(k, by).wait_recv()
                        self.cross_sum[s] = self.cross_sum[s] + self.cross_in[lax.rem(k, 8), by - 1]

                    self.takes(by, take)
                    self.sends(by, lambda: self.qz_copy(k, by).wait_send())
                self.qx_copy(k).start()

        @pl.when((t >= 7) & (t < count + 7))
        def _():
            k, odd = t - 7, not same
            s = lax.rem(k, 6)

            def take(block):
                self.n_copy(k, block, me.across()).wait_recv()
                low[s, block] = low[s, block] + self.end_in[lax.rem(k, 8)]
                self.z_copy(k, 2).start()

            self.inner(take)
            self.ends(lambda block, to: self.n_copy(k, block, to).wait_send())
            if odd:
                self.qx_copy(k).wait()
                cross = self.cross_sum[s, me.pair].astype(F32) + self.cross_pair[s].astype(F32)
                self.end_buf[lax.rem(k, 4), :, main:] = cross.astype(BF16)

        @pl.when((t >= 9) & (t < count + 9))
        def _():
            k, odd = t - 9, not same
            e = lax.rem(k, 4)

            @pl.when(k >= 4)
            def _():
                self.stored(k - 4)

            self.fin_buf[e, :, :main] = low[lax.rem(k, 6), me.outer].astype(F32)
            for by in others:

                def take():
                    self.z_copy(k, by).wait_recv()
                    self.fin_buf[e, :, :main] = self.fin_buf[e, :, :main] + self.outer_buf[lax.rem(k, 10), by - 1].astype(F32)

                self.takes(by, take)
                self.sends(by, lambda: self.z_copy(k, by).wait_send())
            self.end_buf[e, :, :main] = self.fin_buf[e, :, :main].astype(BF16)
            self.e_copy(k, odd).start()

        @pl.when((t >= 10) & (t < count + 10))
        def _():
            k, odd = t - 10, same
            s = lax.rem(k, 4)
            self.e_copy(k, odd).wait()

            if odd:
                self.fin_buf[s] = self.end_buf[s].astype(F32) + self.last_buf[s].astype(F32)
            else:
                mid = main - split
                mine = self.end_buf[s, :, :main].astype(F32)
                theirs = self.last_buf[s, :, :main].astype(F32)

                @pl.when(me.role == 0)
                def _():
                    self.fin_buf[s, :, :split] = mine[:, :split]
                    self.fin_buf[s, :, split:main] = mine[:, split:] + theirs[:, :mid]
                    self.fin_buf[s, :, main:] = theirs[:, mid:]

                @pl.when(me.role == 1)
                def _():
                    self.fin_buf[s, :, :split] = theirs[:, :split]
                    self.fin_buf[s, :, split:main] = theirs[:, split:] + mine[:, :mid]
                    self.fin_buf[s, :, main:] = mine[:, mid:]

            self.store(k)

    def finish(self):
        loop(4, lambda i: self.stored(self.steps - 4 + i))
        for layer in range(self.layers):
            self.spread_copy(layer).wait()


def backward_kernel(
    layers, outers, split,
    full_ref, saved_ref, hidden_ref, probs_ref, cot_ref, table_ref, pick_ref, used_ref,
    grad_ref, inner_ref, outer_ref, expand_ref, shrink_ref, frames_grad_ref, table_out_ref,
    g_buf, acc_buf, h_buf, w_buf, low_buf, act_buf, give_buf, back_buf, p_buf, stage_buf, tab_sum, tab_in, tab_role, tab_back,
    act_sem, h_sem, w_sem, p_sem, stage_sem, ks, kr, ts, tr, rs_sem, rr_sem, out_sem, *reduce_refs,
):
    me = Place(outers)
    devices = 4 * outers
    rows_all, width = cot_ref.shape
    per_layer = full_ref.shape[0] // layers
    pieces = (per_layer - 4) // 2
    pairs = width // 128
    micro = probs_ref.shape[1] // pairs
    rows = rows_all // micro
    shard = grad_ref.shape[-2]
    tile_outers = WIDE // (4 * shard)
    block = 128
    reduce = Reduce(me, layers, grad_ref, (inner_ref, outer_ref, expand_ref, shrink_ref), split, reduce_refs)
    def load_rows(i):
        r = tile(i, block)
        g_buf[r, :] = cot_ref[r, :].astype(F32)


    def get(l, item, slot):
        return pltpu.make_async_copy(saved_ref.at[l, item], act_buf.at[slot], act_sem.at[slot])

    def get_hidden(l, which):
        return pltpu.make_async_copy(hidden_ref.at[l, which], h_buf, h_sem)

    def get_w(k, slot):
        return pltpu.make_async_copy(full_ref.at[k], w_buf.at[slot], w_sem.at[slot])

    def send_stage(n):
        s = lax.rem(n, 2)
        return pltpu.make_async_copy(stage_buf.at[s], grad_ref.at[n], stage_sem.at[s])

    def produce(n, left, right, far=None):
        s = lax.rem(n, 2)

        def some(i):
            cols = tile(i, WIDE)
            value = t_dot(left[:, cols], right[...])
            if far is not None:
                value = value + t_dot(far[0][:, cols], far[1][...])
            stage_buf[s, pl.ds(i * tile_outers, tile_outers)] = value.astype(BF16).reshape(tile_outers, 2, 2, shard, width)

        loop(width // WIDE, some)
        send_stage(n).start()

        @pl.when(n >= 1)
        def _():
            send_stage(n - 1).wait()

    def through(left, slot, finish):
        def some(i):
            cols = tile(i, WIDE)
            finish(cols, dot_t(left[...], w_buf[slot, cols, :]))

        loop(width // WIDE, some)

    def lower(dst, src):
        def some(i):
            r = tile(i, block)
            dst[r, :] = src[r, :].astype(BF16)

        loop(rows_all // block, some)

    def norm_back(index, l, between):
        def some(i):
            r = tile(i, block)
            unit, inverse = normalize(h_buf[r, :])
            scale = dot(pick_ref[l * 4 + 2 * index, r, :], table_ref[...])
            grad = acc_buf[r, :]
            g_buf[r, :] = g_buf[r, :] + norm_backward(grad, scale, unit, inverse)
            for which, values in ((0, grad * unit), (1, grad)):
                picked = used_ref[l * 4 + 2 * index + which, :, r]
                high = values.astype(BF16)
                rest = (values - high.astype(F32)).astype(BF16)
                tab_sum[...] += dot(picked, high) + dot(picked, rest)

        loop(rows_all // block // 2, some)
        between()
        loop(rows_all // block // 2, lambda i: some(i + rows_all // block // 2))

    def prefetch(l):
        get(l, 7, 0).start()
        get(l, 8, 1).start()
        get(l, 8 + pieces, 3).start()
        get_w(l * per_layer + 5, 0).start()

    prefetch(layers - 1)
    loop(rows_all // block, load_rows)
    tab_sum[...] = jnp.zeros_like(tab_sum)
    me.greet()

    def layer(turn):
        l = layers - 1 - turn
        base = l * per_layer
        n0 = turn * per_layer

        def service(index):
            reduce.step(2 * (n0 - 1) + index)

        get_hidden(l, 1).start()
        lower(low_buf, g_buf)
        acc_buf[...] = jnp.zeros_like(acc_buf)
        get(l, 7, 0).wait()

        def feed(j):
            s = lax.rem(j, 2)
            get_w(base + 4 + 2 * j, 1).start()
            get(l, 8 + j, 1 + s).wait()
            get(l, 8 + pieces + j, 3 + s).wait()

            @pl.when(j < pieces - 1)
            def _():
                get(l, 9 + j, 2 - s).start()
                get(l, 9 + pieces + j, 4 - s).start()

            produce(n0 + 2 * j, act_buf.at[1 + s], low_buf)
            service(2 * j)
            get_w(base + 5 + 2 * j, 0).wait()

            def lift(cols, value):
                act_buf[5, :, cols] = (value * act_buf[3 + s, :, cols].astype(F32)).astype(BF16)

            through(low_buf, 0, lift)

            @pl.when(j < pieces - 1)
            def _():
                get_w(base + 7 + 2 * j, 0).start()

            service(2 * j + 1)
            produce(n0 + 2 * j + 1, act_buf.at[0], act_buf.at[5])
            get_w(base + 4 + 2 * j, 1).wait()

            def add(cols, value):
                acc_buf[:, cols] += value

            through(act_buf.at[5], 1, add)

        loop(pieces, feed)
        get_w(base + 3, 0).start()
        get(l, 6, 0).start()
        for i in range(5):
            get(l, 1 + i, 1 + i).start()
        get(l, 8 + 2 * pieces, 9).start()

        def get_probs(it):
            s = lax.rem(it, 2)
            return pltpu.make_async_copy(probs_ref.at[l, it], p_buf.at[s], p_sem.at[s])

        get_probs(0).start()
        get_hidden(l, 1).wait()
        norm_back(1, l, lambda: service(2 * pieces))
        lower(low_buf, g_buf)
        get(l, 6, 0).wait()
        service(2 * pieces + 1)
        produce(n0 + 2 * pieces, act_buf.at[0], low_buf)
        get_w(base + 3, 0).wait()

        def keep_mixture(cols, value):
            act_buf[6, :, cols] = value.astype(BF16)

        through(low_buf, 0, keep_mixture)
        get_w(base + 1, 0).start()
        get(l, 0, 8).start()
        for i in range(5):
            get(l, 1 + i, 1 + i).wait()

        def attend(it):
            m, p = lax.div(it, pairs), lax.rem(it, pairs)
            r, cols = tile(m, rows), tile(p, 128)
            first = lax.broadcasted_iota(jnp.int32, (rows, 128), 1) < HD

            def both_of(x):
                return jnp.concatenate([jnp.where(first, x, 0.0).astype(BF16), jnp.where(first, 0.0, x).astype(BF16)], axis=0)

            queries = both_of(act_buf[1, r, cols].astype(F32) * HD**-0.5)
            out_grad = both_of(act_buf[6, r, cols].astype(F32))
            keys = jnp.concatenate([act_buf[4, r, cols], act_buf[2, r, cols]], axis=0)
            values = jnp.concatenate([act_buf[5, r, cols], act_buf[3, r, cols]], axis=0)
            get_probs(it).wait()

            @pl.when(it + 1 < micro * pairs)
            def _():
                get_probs(it + 1).start()

            soft_low = p_buf[lax.rem(it, 2)]
            soft = soft_low.astype(F32)
            grad_soft = dot_t(values, out_grad)
            inner = jnp.sum(soft * grad_soft, axis=0, keepdims=True)
            grad_scores = (soft * (grad_soft - inner)).astype(BF16)
            grad_values = dot(soft_low, out_grad)
            grad_keys = dot(grad_scores, queries)
            give_buf[0, r, cols] = grad_keys[:rows].astype(BF16)
            give_buf[1, r, cols] = grad_values[:rows].astype(BF16)
            h_buf[r, cols] = grad_keys[rows:]
            acc_buf[r, cols] = grad_values[rows:]
            out = t_dot(keys, grad_scores) * HD**-0.5
            out = jnp.concatenate([out[:HD, :rows], out[HD:, rows:]], axis=0)
            act_buf[7, r, cols] = out.T.astype(BF16)

        def attend_some(s):
            loop(3, lambda i: attend(s * 3 + i))
            service(2 * pieces + 2 + s)

        loop(5, attend_some)
        loop(micro * pairs - 15, lambda i: attend(15 + i))

        def some_rows(i):
            r = tile(i, block)
            act_buf[1, r, :] = h_buf[r, :].astype(BF16)
            act_buf[2, r, :] = acc_buf[r, :].astype(BF16)

        loop(rows_all // block, some_rows)
        acc_buf[...] = jnp.zeros_like(acc_buf)
        get(l, 0, 8).wait()
        get(l, 8 + 2 * pieces, 9).wait()

        def back_copy():
            return remote(low_buf, back_buf.at[l], ks.at[l], kr.at[l], me.other_role())

        def add(cols, value):
            acc_buf[:, cols] += value

        def first(cols, value):
            h_buf[:, cols] = value

        def second(cols, value):
            low_buf[:, cols] = (h_buf[:, cols] + value).astype(BF16)

        get_w(base + 2, 1).start()
        get_w(base + 1, 0).wait()

        @pl.when(me.role == 1)
        def _():
            through(give_buf.at[0], 0, first)

        through(act_buf.at[1], 0, add)
        service(2 * pieces + 7)
        get_w(base, 0).start()
        get_w(base + 2, 1).wait()

        @pl.when(me.role == 1)
        def _():
            through(give_buf.at[1], 1, second)
            back_copy().start()

        get_hidden(l, 0).start()
        through(act_buf.at[2], 1, add)
        service(2 * pieces + 8)
        get_w(base, 0).wait()
        through(act_buf.at[7], 0, add)
        service(2 * pieces + 9)
        n = n0 + 2 * pieces + 1

        @pl.when(me.role == 0)
        def _():
            def some(i):
                produce(n + i, act_buf.at[8], act_buf.at[1 + i])
                service(2 * pieces + 10 + i)

            loop(2, some)

        @pl.when(me.role == 1)
        def _():
            def some(i):
                produce(n + i, act_buf.at[8], act_buf.at[1 + i], (act_buf.at[9], give_buf.at[i]))
                service(2 * pieces + 10 + i)

            loop(2, some)

        produce(n + 2, act_buf.at[8], act_buf.at[7])
        service(2 * pieces + 12)

        @pl.when(turn < layers - 1)
        def _():
            prefetch(l - 1)

        service(2 * pieces + 13)

        @pl.when(me.role == 0)
        def _():
            back_copy().wait_recv()

            def some(i):
                r = tile(i, block)
                acc_buf[r, :] += back_buf[l, r, :].astype(F32)

            loop(rows_all // block, some)

        get_hidden(l, 0).wait()
        norm_back(0, l, lambda: service(2 * pieces + 14))
        service(2 * pieces + 15)

        @pl.when(me.role == 1)
        def _():
            back_copy().wait_send()

    loop(layers, layer)
    lower(low_buf, g_buf)
    done = pltpu.make_async_copy(low_buf, frames_grad_ref, out_sem)
    done.start()

    per = 128 * devices // width
    for group in range(width // 128):
        tab_role[group] = tab_sum[:, group * 128 : group * 128 + 128]

    def tab_copy(by):
        to = lax.rem(me.dp + by, devices)
        return remote(tab_role.at[lax.div(to, per)], tab_in.at[me.dp], ts.at[by - 1], tr.at[by - 1], me.around(by))

    def tab_wait(by):
        here = tab_in.at[lax.rem(me.dp - by + devices, devices)]
        remote(here, here, ts.at[by - 1], tr.at[by - 1], me.around(by)).wait_recv()

    loop(devices - 1, lambda i: tab_copy(i + 1).start())
    tab_in[me.dp] = tab_role[lax.div(me.dp, per)]
    last = layers * per_layer - 1
    send_stage(last).wait()
    loop(4, lambda i: reduce.step(2 * last + i))
    loop(devices - 1, lambda i: tab_wait(i + 1))
    loop(devices - 1, lambda i: tab_copy(i + 1).wait_send())
    total = tab_in[0]
    for i in range(1, devices):
        total = total + tab_in[i]
    tab_back[0] = total
    swap = remote(tab_back.at[0], tab_back.at[1], rs_sem, rr_sem, me.other_role())
    swap.start()
    loop(reduce.lag - 2, lambda i: reduce.step(2 * last + 4 + i))
    swap.wait()
    table_out_ref[...] = tab_back[0] + tab_back[1]
    reduce.finish()
    done.wait()


def backward(full, saved, hidden, probs, cotangent, table, pick, used, outers, layers, shard, collective_id):
    count = full.shape[0]
    pieces = (count // layers - 4) // 2
    rows_all, width = cotangent.shape
    keys = probs.shape[2]
    small = table.shape[0]
    dma = pltpu.SemaphoreType.DMA
    devices = 4 * outers
    split = width // 8
    any_space = pl.BlockSpec(memory_space=pl.ANY)
    vmem = pl.BlockSpec(memory_space=pltpu.VMEM)
    grid_rows = (rows_all, width)
    return pl.pallas_call(
        functools.partial(backward_kernel, layers, outers, split),
        out_shape=(
            jax.ShapeDtypeStruct((count, outers, 2, 2, shard, width), BF16),
            jax.ShapeDtypeStruct((layers, shard, 3 * width), F32),
            jax.ShapeDtypeStruct((layers, shard, width), F32),
            jax.ShapeDtypeStruct((layers, shard, pieces * width), F32),
            jax.ShapeDtypeStruct((layers, pieces * shard, width), F32),
            jax.ShapeDtypeStruct(grid_rows, BF16),
            jax.ShapeDtypeStruct((small, 128), F32),
        ),
        in_specs=[any_space, any_space, any_space, any_space, vmem, vmem, vmem, vmem],
        out_specs=(any_space,) * 6 + (vmem,),
        scratch_shapes=[
            pltpu.VMEM(grid_rows, F32),
            pltpu.VMEM(grid_rows, F32),
            pltpu.VMEM(grid_rows, F32),
            pltpu.VMEM((2, width, width), BF16),
            pltpu.VMEM(grid_rows, BF16),
            pltpu.VMEM((10,) + grid_rows, BF16),
            pltpu.VMEM((2,) + grid_rows, BF16),
            pltpu.VMEM((layers,) + grid_rows, BF16),
            pltpu.VMEM((2, keys, keys), BF16),
            pltpu.VMEM((2, outers, 2, 2, shard, width), BF16),
            pltpu.VMEM((small, width), F32),
            pltpu.VMEM((devices, small, 128), F32),
            pltpu.VMEM((width // 128, small, 128), F32),
            pltpu.VMEM((2, small, 128), F32),
            dma((10,)), dma(()), dma((2,)), dma((2,)), dma((2,)), dma((layers,)), dma((layers,)),
            dma((devices - 1,)), dma((devices - 1,)), dma(()), dma(()), dma(()),
        ]
        + Reduce.scratch(layers, outers, shard, width, pieces, split),
        compiler_params=pltpu.CompilerParams(
            collective_id=collective_id, has_side_effects=True, vmem_limit_bytes=60 * 2**20
        ),
        name="backward_and_reduce",
    )(full, saved, hidden, probs, cotangent, table, pick, used)


def prepare(
    shard, causal_gain, causal_shift, section_scale, section_shift, prompt_lengths, target_lengths, sections, rows,
):
    is_target = lax.axis_index("role") == 1
    segs = section_scale.shape[0]
    micro = prompt_lengths.shape[0]
    small = jnp.concatenate(
        [causal_gain, causal_shift, section_scale.reshape(2 * segs, -1), section_shift.reshape(2 * segs, -1)], axis=0
    )
    per = 128 // shard
    spot = (lax.axis_index("dp") % per) * shard
    piece = lax.dynamic_update_slice(jnp.zeros((small.shape[0], 128), BF16), small, (0, spot))

    masks = [[], []]
    section_frames = []
    for m in range(micro):
        prompt_row, target_row, section_row = prompt_lengths[m, 0], target_lengths[m, 0], sections[m, 0]
        prompt_segment, prompt_position, prompt_member = frame_tags(prompt_row, jnp.zeros_like(prompt_row), rows)
        target_segment, target_position, target_member = frame_tags(target_row, prompt_row, rows)
        own_segment = jnp.where(is_target, target_segment, prompt_segment)
        own_position = jnp.where(is_target, target_position, prompt_position)
        own_member = jnp.where(is_target, target_member, prompt_member)
        same_far = (own_segment[None, :] == prompt_segment[:, None]) & is_target
        same_own = own_segment[None, :] == own_segment[:, None]
        causal_own = same_own & (own_position[:, None] <= own_position[None, :])
        masks[0].append(jnp.concatenate([same_far, causal_own], axis=0))
        masks[1].append(jnp.concatenate([same_far, same_own], axis=0))
        section_frames.append(jnp.sum(jnp.where(own_member, section_row[None, :], 0), axis=1))
    bias = jnp.where(jnp.stack([jnp.stack(one) for one in masks]), 0.0, -1e30).astype(BF16)
    section = jnp.concatenate(section_frames)
    none = jnp.zeros_like(section)
    first, second = 4 + 2 * section, 4 + 2 * segs + 2 * section
    used = jnp.stack([none, none + 2, none + 1, none + 3, first, second, first + 1, second + 1])
    return piece, used, bias


def body(
    frames, cotangent, inner_weight, outer_weight, expand_weight, shrink_weight, causal_gain, causal_shift,
    section_scale, section_shift, prompt_lengths, target_lengths, sections,
):
    _, micro, rows, width = frames.shape
    layers, shard, _ = inner_weight.shape
    devices = width // shard
    outers = devices // 4
    pieces = expand_weight.shape[2] // width
    segs = section_scale.shape[0]
    piece, used, bias = prepare(
        shard, causal_gain, causal_shift, section_scale, section_shift, prompt_lengths, target_lengths, sections, rows
    )
    if shard != 64:
        expand_weight = expand_weight.reshape(layers, shard, devices, pieces, shard).transpose(0, 1, 3, 2, 4).reshape(layers, shard, -1)
    entries = jnp.arange(piece.shape[0], dtype=jnp.int32)
    pick = (used[:, :, None] == entries[None, None, :]).astype(BF16)
    pick_t = (used[:, None, :] == entries[None, :, None]).astype(BF16)
    full, saved, hidden, probs, mixed, table = forward(
        inner_weight, outer_weight, expand_weight, shrink_weight, frames.reshape(micro * rows, width), piece, pick, bias, outers, 0
    )
    _, inner_grad, outer_grad, expand_grad, shrink_grad, frames_grad, small = backward(
        full.reshape(-1, width, width), saved, hidden, probs, cotangent.reshape(micro * rows, width),
        table, pick, pick_t, outers, layers, shard, 1,
    )
    if shard != 64:
        expand_grad = expand_grad.reshape(layers, shard, pieces, devices, shard).transpose(0, 1, 3, 2, 4).reshape(layers, shard, -1)
    per = 128 // shard
    spot = (lax.axis_index("dp") % per) * shard
    small = lax.dynamic_slice(small, (0, spot), (small.shape[0], shard))
    return (
        mixed.reshape(1, micro, rows, width), frames_grad.reshape(1, micro, rows, width),
        inner_grad, outer_grad, expand_grad, shrink_grad,
        small[0:2], small[2:4],
        small[4 : 4 + 2 * segs].reshape(segs, 2, shard),
        small[4 + 2 * segs :].reshape(segs, 2, shard),
    )


def solution(mesh):
    rows = P("role", None, "dp", None)
    second = P(None, "dp", None)
    placed = (rows, rows, second, second, second, second, P(None, "dp"), P(None, "dp"), P(None, None, "dp"), P(None, None, "dp"), second, second, second)
    given = (rows, rows, second, second, second, second, P(None, "dp"), P(None, "dp"), P(None, None, "dp"), P(None, None, "dp"))
    return jax.shard_map(body, mesh=mesh, in_specs=placed, out_specs=given, check_vma=False)
```
